256 devices in a mesh: space: 32 (over z, y), group: 8 (over x, core).
Axes of the slice: x: 4, y: 4, z: 8, core: 2. Of those that a mesh axis runs over, the one named last changes fastest.
Arguments:
- feats: bfloat16 [8, 262144, 128], P('group', 'space'), may hold values from -6 to 6
- geom: bfloat16 [8, 262144, 128], P('group', 'space'), may hold values from -6 to 6
- w_value: bfloat16 [128, 128], replicated, may hold values from -0.5 to 0.5
- w_kern: bfloat16 [128, 64], replicated, may hold values from -0.5 to 0.5
- w_out: bfloat16 [128, 128], replicated, may hold values from -0.5 to 0.5
- gain: float32 [128], replicated, may hold values from 0.1 to 1.9
- t_local: int32 [8, 2048], P('group', 'space'), may hold values from 0 to 31
- t_dest: int32 [8, 2048, 1], P('group', 'space'), may hold values from 0 to 31; in each aligned block of 64 rows (0 to 63, 64 to 127, ..., all dimensions but the last counted through in order) at most 3 rows name the same one
- t_block: int32 [8, 2048], P('group', 'space'), may hold values from 0 to 31
- t_cut: int32 [8, 2048], P('group', 'space'), may hold values from 64 to 511
- x_local: int32 [8, 256], P('group', 'space'), may hold values from 0 to 31
- x_block: int32 [8, 256], P('group', 'space'), may hold values from 0 to 31
- x_cut: int32 [8, 256], P('group', 'space'), may hold values from 64 to 511
Outputs:
- mixed: bfloat16 [8, 262144, 128], P('group', 'space')
The draws below stay inside these ranges and needn't reach their ends.
Inputs may be any that keep to these rules, and one draw needn't show every extreme that they name: `t_dest`: among the 64 pairs of one device, no index is named by more than 3 pairs, a bound that some block reaches.
All inputs are finite; a program needn't handle non-finite values.
Results may differ from the reference program's by a relative error of at most 0.0054.
Values may be sent and summed in bfloat16 or wider, within the bound.
No kernel may reach another device: no remote copies, remote signals or barrier semaphores. Data moves between devices by JAX's collectives and lax.ppermute only.
A program may use at most 192 MiB of HBM per device.

```python
import math
import jax
import jax.numpy as jnp
import numpy as np
from jax import lax

C = 128
K = 64
BLK = 256
NB = 32
PT = 64
PX = 8
CAP = 3
GROUPS = 8
GROUP_PTS = 262144
GROUP_TILES = 2048
GROUP_XT = 256
N_SPACE = 32


def plant(values, stream_key, smallest, top_value):
    place = [jax.random.randint(jax.random.fold_in(stream_key, axis), (), 0, length) for axis, length in enumerate(values.shape)]
    widest = values.shape.index(max(values.shape))
    beside = place[:widest] + [(place[widest] + 1) % values.shape[widest]] + place[widest + 1:]
    return values.at[tuple(place)].set(smallest).at[tuple(beside)].set(top_value)


def level_of(stream_key, extent, pieces, low, largest):
    level, own = 1.0, jax.random.fold_in(stream_key, 6)
    for dim, blocks in pieces:
        steps = jnp.exp(jax.random.uniform(jax.random.fold_in(own, dim), (blocks,), jnp.float32, low / len(pieces), largest / len(pieces)))
        level = level * jnp.repeat(steps, extent[dim] // blocks).reshape([-1 if axis == dim else 1 for axis in range(len(extent))])
    return level


def deal_out(rng, own, number, rows, count, top, reach, skew):
    sequence = jax.random.permutation(rng, count)
    heavy_load, ordinary = portions_of(count, rows * top, reach, skew, True), portions_of(count, rows * top, reach, skew, False)
    places = jnp.arange(count)

    def named(lengths, turn):
        used = int((lengths > 0).sum())
        fixed = max(1, used // 4)
        passed = fixed + (places - fixed + turn * (used - fixed)) % max(1, count - fixed)
        return jnp.zeros((count,), jnp.int32).at[sequence[jnp.where(places < fixed, places, passed)]].set(jnp.asarray(lengths, jnp.int32))

    lengths = jnp.where(number % 4 == 0, named(heavy_load, number // 4), named(ordinary, number - number // 4 - 1))
    mixed = jax.random.permutation(jax.random.fold_in(own, 3), count)
    source_of, sink = mixed[0:count // 2 * 2:2], mixed[1:count // 2 * 2:2]
    slack = jnp.minimum(lengths[source_of] - 1, reach - lengths[sink]) // 2
    slack = jnp.where((source_of == sequence[0]) | (sink == sequence[0]) | (lengths[sink] == 0), 0, jnp.maximum(slack, 0))
    passed = jax.random.randint(jax.random.fold_in(own, 4), (count // 2,), 0, 1 << 20) % (slack + 1)
    lengths = lengths.at[source_of].add(-passed).at[sink].add(passed)
    items = jnp.searchsorted(jnp.cumsum(lengths), jnp.arange(rows * top), side="right").astype(jnp.int32)
    grid = items.reshape(top, rows).T
    grid = grid[jax.random.permutation(jax.random.fold_in(own, 1), rows)]
    turn = jax.random.randint(jax.random.fold_in(own, 2), (rows, 1), 0, top)
    return jnp.take_along_axis(grid, (jnp.arange(top)[None, :] + turn) % top, axis=1)


def portions_of(count, total, most, slope, full):
    loads = [(1 << 20) // math.isqrt(standing ** slope) + 1 for standing in range(1, count + 1)]
    largest = most if full else min(most, max(-(-total // count), total * loads[0] // sum(loads)))
    least = 1 if total - largest >= count - 1 else 0
    holding, rest = [largest] + [least] * (count - 1), total - largest - least * (count - 1)
    while rest > 0:
        movable = [i for i in range(1, count) if holding[i] < largest] or [i for i in range(1, count) if holding[i] < most]
        mass, left = sum([loads[i] for i in movable]), rest
        for i in movable:
            addition = min(most - holding[i], max(1, left * loads[i] // mass), rest)
            holding[i] = holding[i] + addition
            rest = rest - addition
    return np.array(holding)


def normal_values(key, dims, spread, most, pieces=(), held_as=jnp.bfloat16):
    array = spread * jax.random.normal(key, dims, jnp.float32)
    if pieces:
        array = array * level_of(key, dims, pieces, -0.22, 0.18)
    return jnp.clip(array, -most, most).astype(held_as)


def setup_inputs(seed: int = 0) -> dict:
    arg_keys = jax.random.split(jax.random.key(seed), 14)
    feats = normal_values(arg_keys[0], (GROUPS, GROUP_PTS, C), 1.0, 6.0, ((0, 8), (1, 32)))
    geom = normal_values(arg_keys[1], (GROUPS, GROUP_PTS, C), 1.0, 6.0, ((0, 8), (1, 32)))
    w_value = normal_values(arg_keys[2], (C, C), C ** -0.5, 0.5)
    w_kern = normal_values(arg_keys[3], (C, K), C ** -0.5, 0.5)
    w_out = normal_values(arg_keys[4], (C, C), C ** -0.5, 0.5)
    gain = jnp.clip(1.0 + 0.18 * jax.random.normal(arg_keys[5], (C,), jnp.float32), 0.1, 1.9)
    t_local = plant(jax.random.randint(arg_keys[6], (GROUPS, GROUP_TILES), 0, NB), jax.random.fold_in(arg_keys[6], 1), 0, NB - 1).astype(jnp.int32)
    t_dest_keys = jax.random.split(jax.random.fold_in(arg_keys[7], 1), GROUPS * GROUP_TILES // PT)
    t_dest_turns = jax.random.permutation(jax.random.fold_in(arg_keys[7], 3), GROUPS * GROUP_TILES // PT)
    t_dest = jax.vmap(lambda own, number: deal_out(jax.random.fold_in(arg_keys[7], 2), own, number, PT, N_SPACE, 1, CAP, 2))(t_dest_keys, t_dest_turns).reshape((GROUPS, GROUP_TILES, 1))
    t_block = plant(jax.random.randint(arg_keys[8], (GROUPS, GROUP_TILES), 0, NB), jax.random.fold_in(arg_keys[8], 1), 0, NB - 1).astype(jnp.int32)
    t_cut = plant(jax.random.randint(arg_keys[9], (GROUPS, GROUP_TILES), BLK // 4, 2 * BLK), jax.random.fold_in(arg_keys[9], 1), BLK // 4, (2 * BLK) - 1).astype(jnp.int32)
    x_local = plant(jax.random.randint(arg_keys[10], (GROUPS, GROUP_XT), 0, NB), jax.random.fold_in(arg_keys[10], 1), 0, NB - 1).astype(jnp.int32)
    x_block = plant(jax.random.randint(arg_keys[11], (GROUPS, GROUP_XT), 0, NB), jax.random.fold_in(arg_keys[11], 1), 0, NB - 1).astype(jnp.int32)
    x_cut = plant(jax.random.randint(arg_keys[12], (GROUPS, GROUP_XT), BLK // 4, 2 * BLK), jax.random.fold_in(arg_keys[12], 1), BLK // 4, (2 * BLK) - 1).astype(jnp.int32)
    return dict(feats=feats, geom=geom, w_value=w_value, w_kern=w_kern, w_out=w_out, gain=gain, t_local=t_local, t_dest=t_dest, t_block=t_block, t_cut=t_cut, x_local=x_local, x_block=x_block, x_cut=x_cut)


def pair_terms(left_block, right_block, cutoff):
    scores = jnp.dot(left_block[:, C:], right_block[:, C:].T, preferred_element_type=jnp.float32)
    places = jnp.arange(BLK, dtype=jnp.int32)
    inside = places[:, None] + places[None, :] < cutoff
    matrix = jnp.where(inside, jnp.tanh(scores * (1.0 / math.sqrt(K))), 0.0).astype(jnp.bfloat16)
    forward = jnp.dot(matrix, right_block[:, :C], preferred_element_type=jnp.float32)
    backward = jnp.dot(matrix.T, left_block[:, :C], preferred_element_type=jnp.float32)
    return (forward, backward)

def reference(feats, geom, w_value, w_kern, w_out, gain, t_local, t_dest, t_block, t_cut, x_local, x_block, x_cut):
    groups_here = feats.shape[0]
    spaces = N_SPACE
    values = jnp.dot(feats.reshape(-1, C), w_value, preferred_element_type=jnp.float32).astype(jnp.bfloat16)
    kernels = jnp.dot(geom.reshape(-1, C), w_kern, preferred_element_type=jnp.float32).astype(jnp.bfloat16)
    payload = jnp.concatenate([values, kernels], 1).reshape(groups_here, spaces, NB, BLK, C + K)
    payload = jnp.concatenate([payload, jnp.zeros((1, spaces, NB, BLK, C + K), payload.dtype)], 0)
    local_ids = t_local.reshape(groups_here, spaces, PT)
    targets = t_dest.reshape(groups_here, spaces, PT)
    partner_ids = t_block.reshape(groups_here, spaces, PT)
    cutoffs = t_cut.reshape(groups_here, spaces, PT)
    cross_local = x_local.reshape(groups_here, spaces, PX)
    cross_block = x_block.reshape(groups_here, spaces, PX)
    cross_cut = x_cut.reshape(groups_here, spaces, PX)
    start = jnp.zeros((groups_here + 1, spaces, NB, BLK, C), jnp.float32)

    def device_step(aggregate, flat_index):
        gidx = flat_index // spaces
        sidx = flat_index % spaces
        mine = local_ids[gidx, sidx]
        where_to = targets[gidx, sidx]
        theirs = partner_ids[gidx, sidx]
        own_blocks = payload[gidx, sidx][mine]
        partners = payload[gidx][where_to, theirs]
        forward, backward = jax.vmap(pair_terms)(own_blocks, partners, cutoffs[gidx, sidx])
        aggregate = aggregate.at[gidx, sidx, mine].add(forward)
        aggregate = aggregate.at[gidx, where_to, theirs].add(backward)
        xmine = cross_local[gidx, sidx]
        xtheirs = cross_block[gidx, sidx]
        forward_x, backward_x = jax.vmap(pair_terms)(payload[gidx, sidx][xmine], payload[gidx + 1, sidx][xtheirs], cross_cut[gidx, sidx])
        aggregate = aggregate.at[gidx, sidx, xmine].add(forward_x)
        aggregate = aggregate.at[gidx + 1, sidx, xtheirs].add(backward_x)
        return (aggregate, None)
    aggregate, _ = lax.scan(device_step, start, jnp.arange(groups_here * spaces, dtype=jnp.int32))
    flat = aggregate[:groups_here].reshape(-1, C)
    meansq = lax.optimization_barrier(jnp.mean(flat * flat, -1, keepdims=True))
    normed = flat * lax.rsqrt(meansq + 1e-06) * gain
    hidden = jax.nn.gelu(normed).astype(jnp.bfloat16)
    mixed = feats.reshape(-1, C).astype(jnp.float32) + jnp.dot(hidden, w_out, preferred_element_type=jnp.float32)
    return mixed.astype(jnp.bfloat16).reshape(feats.shape)
```

```python
import math

import jax
import jax.numpy as jnp
from jax import lax
from jax.experimental import pallas as pl
from jax.experimental.pallas import tpu as pltpu
from jax.sharding import PartitionSpec as P

C = 128
K = 64
BLK = 256
HALF = BLK // 2
ROWS = BLK + HALF
CAP = 3
VMEM_LIMIT = 56 * 1024 * 1024


def group_shift(value, steps):
    count = lax.axis_size("group")
    leading, last = (max(0, -steps), min(count, count - steps))
    return lax.ppermute(value, "group", [(source, source + steps) for source in range(leading, last)])


def plan_slots(t_local, t_dest, t_block, t_cut, spaces):
    pairs = t_local.shape[0]
    slots = spaces * CAP

    def kernel(local_ref, dest_ref, block_ref, cut_ref, used_ref, meta_ref, count):
        @pl.loop(0, slots)
        def _(i):
            used_ref[i] = -1
            meta_ref[2 * i] = 0
            meta_ref[2 * i + 1] = 0

        @pl.loop(0, spaces)
        def _(i):
            count[i] = 0

        @pl.loop(0, pairs)
        def _(t):
            dest = dest_ref[t]
            slot = dest * CAP + count[dest]
            count[dest] = count[dest] + 1
            used_ref[slot] = local_ref[t]
            meta_ref[2 * slot] = block_ref[t]
            meta_ref[2 * slot + 1] = cut_ref[t]

    smem = pl.BlockSpec(memory_space=pltpu.SMEM)
    return pl.pallas_call(
        kernel,
        out_shape=(
            jax.ShapeDtypeStruct((slots,), jnp.int32),
            jax.ShapeDtypeStruct((2 * slots,), jnp.int32),
        ),
        in_specs=[smem] * 4,
        out_specs=(smem, smem),
        scratch_shapes=[pltpu.SMEM((spaces,), jnp.int32)],
        name="plan_slots",
    )(t_local, t_dest, t_block, t_cut)


def project_and_pack(points, geom, w_value, w_kern, used, x_local):
    blocks = points.shape[0] // BLK
    slots = used.shape[0]
    cross = x_local.shape[0]
    step = 4

    def kernel(used_ref, cross_ref, points_ref, geom_ref, wv_ref, wk_ref, own_ref, out_ref, up_ref, held, sems):
        i = pl.program_id(0)
        values = jnp.dot(points_ref[...], wv_ref[...], preferred_element_type=jnp.float32).astype(jnp.bfloat16)
        for b in range(step):
            base = b * BLK
            wide = jnp.concatenate(
                [geom_ref[pl.ds(base, HALF), :], geom_ref[pl.ds(base + HALF, HALF), :]], axis=1
            )
            held[i * step + b, :BLK, :] = values[base : base + BLK]
            held[i * step + b, BLK:, :] = jnp.dot(
                wide, wk_ref[...], preferred_element_type=jnp.float32
            ).astype(jnp.bfloat16)

        @pl.when(i == pl.num_programs(0) - 1)
        def _():
            own = pltpu.make_async_copy(held, own_ref, sems.at[0])

            def cross_copy(t):
                return pltpu.make_async_copy(held.at[cross_ref[t]], up_ref.at[t], sems.at[1])

            def slot_copy(t):
                return pltpu.make_async_copy(held.at[jnp.maximum(used_ref[t], 0)], out_ref.at[t], sems.at[2])

            own.start()
            for t in range(cross):
                cross_copy(t).start()

            @pl.loop(0, slots)
            def _(t):
                slot_copy(t).start()

            own.wait()
            for t in range(cross):
                cross_copy(t).wait()

            @pl.loop(0, slots)
            def _(t):
                slot_copy(t).wait()

    zero = jnp.zeros_like(w_kern)
    twice = jnp.concatenate(
        [jnp.concatenate([w_kern, zero], 1), jnp.concatenate([zero, w_kern], 1)], 0
    )
    anywhere = pl.BlockSpec(memory_space=pl.ANY)
    return pl.pallas_call(
        kernel,
        grid_spec=pltpu.PrefetchScalarGridSpec(
            num_scalar_prefetch=2,
            grid=(blocks // step,),
            in_specs=[
                pl.BlockSpec((step * BLK, C), lambda i, *_: (i, 0)),
                pl.BlockSpec((step * BLK, C), lambda i, *_: (i, 0)),
                pl.BlockSpec((C, C), lambda i, *_: (0, 0)),
                pl.BlockSpec((2 * C, 2 * K), lambda i, *_: (0, 0)),
            ],
            out_specs=(anywhere, anywhere, anywhere),
            scratch_shapes=[
                pltpu.VMEM((blocks, ROWS, C), jnp.bfloat16),
                pltpu.SemaphoreType.DMA((3,)),
            ],
        ),
        out_shape=(
            jax.ShapeDtypeStruct((blocks, ROWS, C), jnp.bfloat16),
            jax.ShapeDtypeStruct((slots, ROWS, C), jnp.bfloat16),
            jax.ShapeDtypeStruct((cross, ROWS, C), jnp.bfloat16),
        ),
        compiler_params=pltpu.CompilerParams(vmem_limit_bytes=VMEM_LIMIT),
        name="project_and_pack",
    )(used, x_local, points, geom, w_value, twice)


def unpack_kernels(packed):
    return jnp.concatenate([packed[:, :K], packed[:, K:]], axis=0)


def pair_terms(theirs, own, cut):
    scores = lax.dot_general(
        unpack_kernels(theirs[BLK:]),
        unpack_kernels(own[BLK:]),
        (((1,), (1,)), ((), ())),
        preferred_element_type=jnp.float32,
    )
    rows = lax.broadcasted_iota(jnp.int32, (BLK, BLK), 0)
    columns = lax.broadcasted_iota(jnp.int32, (BLK, BLK), 1)
    tile = jnp.where(rows + columns < cut, jnp.tanh(scores * (1.0 / math.sqrt(K))), 0.0).astype(jnp.bfloat16)
    forward = jnp.dot(tile, own[:BLK], preferred_element_type=jnp.float32)
    backward = lax.dot_general(
        tile, theirs[:BLK], (((0,), (0,)), ((), ())), preferred_element_type=jnp.float32
    )
    return forward, backward


def pairs(meta, arrived, own, aggregate):
    slots = arrived.shape[0]
    blocks = own.shape[0]
    step = 4

    def kernel(meta_ref, arrived_ref, own_ref, *rest):
        if aggregate is None:
            back_ref, total_ref, total, sem = rest
        else:
            given_ref, back_ref, total_ref, total, sem = rest
        i = pl.program_id(0)

        @pl.when(i == 0)
        def _():
            if aggregate is None:
                total[...] = jnp.zeros_like(total)
            else:
                copy = pltpu.make_async_copy(given_ref, total, sem)
                copy.start()
                copy.wait()

        for b in range(step):
            slot = i * step + b
            mine = meta_ref[2 * slot]
            forward, backward = pair_terms(arrived_ref[b], own_ref[mine], meta_ref[2 * slot + 1])
            back_ref[b] = forward.astype(jnp.bfloat16)
            total[mine] = total[mine] + backward

        @pl.when(i == pl.num_programs(0) - 1)
        def _():
            copy = pltpu.make_async_copy(total, total_ref, sem)
            copy.start()
            copy.wait()

    anywhere = pl.BlockSpec(memory_space=pl.ANY)
    extra = () if aggregate is None else (aggregate,)
    return pl.pallas_call(
        kernel,
        grid_spec=pltpu.PrefetchScalarGridSpec(
            num_scalar_prefetch=1,
            grid=(slots // step,),
            in_specs=[
                pl.BlockSpec((step, ROWS, C), lambda i, *_: (i, 0, 0)),
                pl.BlockSpec((blocks, ROWS, C), lambda i, *_: (0, 0, 0)),
            ]
            + [anywhere] * len(extra),
            out_specs=(pl.BlockSpec((step, BLK, C), lambda i, *_: (i, 0, 0)), anywhere),
            scratch_shapes=[
                pltpu.VMEM((blocks, BLK, C), jnp.float32),
                pltpu.SemaphoreType.DMA,
            ],
        ),
        out_shape=(
            jax.ShapeDtypeStruct((slots, BLK, C), jnp.bfloat16),
            jax.ShapeDtypeStruct((blocks, BLK, C), jnp.float32),
        ),
        compiler_params=pltpu.CompilerParams(vmem_limit_bytes=VMEM_LIMIT),
        cost_estimate=pl.CostEstimate(
            flops=2 * slots * BLK * BLK * (K + 2 * C),
            bytes_accessed=slots * (ROWS + BLK) * C * 2 + blocks * BLK * C * 8,
            transcendentals=slots * BLK * BLK,
        ),
        name="pairs",
    )(meta, arrived, own, *extra)


def gather_and_mix(used, x_local, returned, returned_x, aggregate, points, w_out, gain):
    slots = returned.shape[0]
    cross = returned_x.shape[0]
    blocks = aggregate.shape[0]
    step = 8
    turns = slots // step
    some = 4

    def kernel(used_ref, cross_ref, back_ref, back_x_ref, total_ref, points_ref, w_ref, gain_ref, out_ref, total, sem):
        i = pl.program_id(0)

        @pl.when(i == 0)
        def _():
            copy = pltpu.make_async_copy(total_ref, total, sem)
            copy.start()
            copy.wait()
            for t in range(cross):
                mine = cross_ref[t]
                total[mine] = total[mine] + back_x_ref[t].astype(jnp.float32)

        @pl.when(i < turns)
        def _():
            for b in range(step):
                mine = used_ref[i * step + b]

                @pl.when(mine >= 0)
                def _():
                    total[mine] = total[mine] + back_ref[b].astype(jnp.float32)

        @pl.when(i >= turns)
        def _():
            for b in range(some):
                flat = total[(i - turns) * some + b]
                meansq = jnp.mean(flat * flat, -1, keepdims=True)
                normed = flat * lax.rsqrt(meansq + 1e-06) * gain_ref[...]
                hidden = jax.nn.gelu(normed).astype(jnp.bfloat16)
                mixed = points_ref[pl.ds(b * BLK, BLK), :].astype(jnp.float32) + jnp.dot(
                    hidden, w_ref[...], preferred_element_type=jnp.float32
                )
                out_ref[pl.ds(b * BLK, BLK), :] = mixed.astype(jnp.bfloat16)

    return pl.pallas_call(
        kernel,
        grid_spec=pltpu.PrefetchScalarGridSpec(
            num_scalar_prefetch=2,
            grid=(turns + blocks // some,),
            in_specs=[
                pl.BlockSpec((step, BLK, C), lambda i, *_: (jnp.minimum(i, turns - 1), 0, 0)),
                pl.BlockSpec((cross, BLK, C), lambda i, *_: (0, 0, 0)),
                pl.BlockSpec(memory_space=pl.ANY),
                pl.BlockSpec((some * BLK, C), lambda i, *_: (jnp.maximum(i - turns, 0), 0)),
                pl.BlockSpec((C, C), lambda i, *_: (0, 0)),
                pl.BlockSpec((1, C), lambda i, *_: (0, 0)),
            ],
            out_specs=pl.BlockSpec((some * BLK, C), lambda i, *_: (jnp.maximum(i - turns, 0), 0)),
            scratch_shapes=[
                pltpu.VMEM((blocks, BLK, C), jnp.float32),
                pltpu.SemaphoreType.DMA,
            ],
        ),
        out_shape=jax.ShapeDtypeStruct((blocks * BLK, C), jnp.bfloat16),
        compiler_params=pltpu.CompilerParams(vmem_limit_bytes=VMEM_LIMIT),
        name="gather_and_mix",
    )(used, x_local, returned, returned_x, aggregate, points, w_out, gain[None])


def body(feats, geom, w_value, w_kern, w_out, gain, t_local, t_dest, t_block, t_cut, x_local, x_block, x_cut):
    points = feats[0]
    spaces = lax.axis_size("space")
    used, meta = plan_slots(t_local[0], t_dest[0, :, 0], t_block[0], t_cut[0], spaces)
    meta = lax.all_to_all(meta.reshape(spaces, 2 * CAP), "space", split_axis=0, concat_axis=0, tiled=True)
    meta = meta.reshape(-1)
    cross_meta = group_shift(jnp.stack([x_block[0], x_cut[0]], 1), 1).reshape(-1)
    own, leaving, rising = project_and_pack(points, geom[0], w_value, w_kern, used, x_local[0])
    below = group_shift(rising, 1)
    arrived = lax.all_to_all(leaving, "space", split_axis=0, concat_axis=0, tiled=True)
    back_x, aggregate = pairs(cross_meta, below, own, None)
    returned_x = group_shift(back_x, -1)
    back, aggregate = pairs(meta, arrived, own, aggregate)
    returned = lax.all_to_all(back, "space", split_axis=0, concat_axis=0, tiled=True)
    mixed = gather_and_mix(used, x_local[0], returned, returned_x, aggregate, points, w_out, gain)
    return mixed[None]


def solution(mesh):
    in_specs = (
        P("group", "space", None),
        P("group", "space", None),
        P(),
        P(),
        P(),
        P(),
        P("group", "space"),
        P("group", "space", None),
        P("group", "space"),
        P("group", "space"),
        P("group", "space"),
        P("group", "space"),
        P("group", "space"),
    )
    out_specs = P("group", "space", None)
    return jax.shard_map(body, mesh=mesh, in_specs=in_specs, out_specs=out_specs, check_vma=False)
```

```python
import math

import jax
import jax.numpy as jnp
from jax import lax
from jax.experimental import pallas as pl
from jax.experimental.pallas import tpu as pltpu
from jax.sharding import PartitionSpec as P

C = 128
K = 64
BLK = 256
HALF = BLK // 2
ROWS = BLK + HALF
CAP = 3
VMEM_LIMIT = 56 * 1024 * 1024
SPAN_Z, SPAN_Y = 8, 4
SPACES = SPAN_Z * SPAN_Y
SHIFTS = tuple(
    shift for dy in range(SPAN_Y) for shift in ((3, dy), (-3, -dy), (1, dy), (-1, -dy))
)
BATCHES = ((0, 8), (8, 13), (13, 16))
PASSED = 2
MEMBERS = SPACES // 2
TEAMS = [[z * SPAN_Y + y for z in range(p, SPAN_Z, 2) for y in range(SPAN_Y)] for p in range(2)]
STAGE = 8
SMEM = pl.BlockSpec(memory_space=pltpu.SMEM)
VMEM = pl.BlockSpec(memory_space=pltpu.VMEM)
ANYWHERE = pl.BlockSpec(memory_space=pl.ANY)
CREW = 4
NOTES = CAP * ROWS
LOAD = NOTES + 16


def space_shift(value, shift):
    return lax.ppermute(
        value,
        "space",
        [
            (z * SPAN_Y + y, (z + shift[0]) % SPAN_Z * SPAN_Y + (y + shift[1]) % SPAN_Y)
            for z in range(SPAN_Z)
            for y in range(SPAN_Y)
        ],
    )


def partner_of(me, shift):
    return (me // SPAN_Y + shift[0]) % SPAN_Z * SPAN_Y + (me % SPAN_Y + shift[1]) % SPAN_Y


def team_exchange(value):
    return lax.all_to_all(
        value, "space", split_axis=0, concat_axis=0, tiled=True, axis_index_groups=TEAMS
    )


def group_shift(value, steps):
    count = lax.axis_size("group")
    leading, last = (max(0, -steps), min(count, count - steps))
    return lax.ppermute(value, "group", [(source, source + steps) for source in range(leading, last)])


def project_and_pack(points, geom, w_value, w_kern, lists, team):
    blocks = points.shape[0] // BLK
    tiles = lists[0].shape[0]
    slots = SPACES * CAP
    step = 4

    def kernel(
        local_ref, dest_ref, block_ref, cut_ref, team_ref, points_ref, geom_ref, wv_ref, wk_ref,
        used_ref, own_ref, out_ref, notes_ref, held, notes, filled, partner, cuts, sems
    ):
        i = pl.program_id(0)
        last = pl.num_programs(0) - 1

        def team_copy(t, block):
            rows = pl.ds(pl.multiple_of(t % CAP * ROWS, ROWS), ROWS)
            return pltpu.make_async_copy(held.at[block], out_ref.at[t // CAP, rows], sems.at[0])

        def own_copy(turn):
            some = pl.ds(turn * step, step)
            return pltpu.make_async_copy(held.at[some], own_ref.at[some], sems.at[1])

        def note_copy(m):
            return pltpu.make_async_copy(notes.at[team_ref[m]], out_ref.at[m, pl.ds(NOTES, 16)], sems.at[2])

        notes_out = pltpu.make_async_copy(notes, notes_ref, sems.at[3])

        @pl.when(i == 0)
        def _():
            @pl.loop(0, slots, unroll=8)
            def _(s):
                used_ref[s] = -1
                partner[s] = 0
                cuts[s] = 0

            @pl.loop(0, SPACES, unroll=8)
            def _(s):
                filled[s] = 0

            @pl.loop(0, tiles, unroll=4)
            def _(t):
                dest = dest_ref[t]
                slot = dest * CAP + filled[dest]
                filled[dest] = filled[dest] + 1
                used_ref[slot] = local_ref[t]
                partner[slot] = block_ref[t]
                cuts[slot] = cut_ref[t]

        values = jnp.dot(points_ref[...], wv_ref[...], preferred_element_type=jnp.float32).astype(jnp.bfloat16)
        for b in range(step):
            base = b * BLK
            wide = jnp.concatenate(
                [geom_ref[pl.ds(base, HALF), :], geom_ref[pl.ds(base + HALF, HALF), :]], axis=1
            )
            held[i * step + b, :BLK, :] = values[base : base + BLK]
            held[i * step + b, BLK:, :] = jnp.dot(
                wide, wk_ref[...], preferred_element_type=jnp.float32
            ).astype(jnp.bfloat16)

        own_copy(i).start()

        @pl.loop(0, MEMBERS * CAP, unroll=4)
        def _(t):
            block = jnp.maximum(used_ref[team_ref[t // CAP] * CAP + t % CAP], 0)

            @pl.when(block // step == i)
            def _():
                team_copy(t, block).start()

        @pl.when(i == 0)
        def _():
            row = lax.broadcasted_iota(jnp.int32, (16, C), 0)

            @pl.loop(0, SPACES, unroll=2)
            def _(d):
                note = jnp.zeros((16, C), jnp.int32)
                for j in range(CAP):
                    cut = cuts[d * CAP + j]
                    note = jnp.where(row == j, partner[d * CAP + j], note)
                    note = jnp.where(row == CAP + j, cut // 16, note)
                    note = jnp.where(row == 2 * CAP + j, cut % 16, note)
                notes[d] = note.astype(jnp.float32).astype(jnp.bfloat16)

            notes_out.start()
            for m in range(MEMBERS):
                note_copy(m).start()

        @pl.when(i == last)
        def _():
            notes_out.wait()
            for m in range(MEMBERS):
                note_copy(m).wait()
            for turn in range(blocks // step):
                own_copy(turn).wait()

            @pl.loop(0, MEMBERS * CAP, unroll=4)
            def _(t):
                team_copy(t, 0).wait()

    zero = jnp.zeros_like(w_kern)
    twice = jnp.concatenate(
        [jnp.concatenate([w_kern, zero], 1), jnp.concatenate([zero, w_kern], 1)], 0
    )
    return pl.pallas_call(
        kernel,
        grid_spec=pltpu.PrefetchScalarGridSpec(
            num_scalar_prefetch=5,
            grid=(blocks // step,),
            in_specs=[
                pl.BlockSpec((step * BLK, C), lambda i, *_: (i, 0)),
                pl.BlockSpec((step * BLK, C), lambda i, *_: (i, 0)),
                pl.BlockSpec((C, C), lambda i, *_: (0, 0)),
                pl.BlockSpec((2 * C, 2 * K), lambda i, *_: (0, 0)),
            ],
            out_specs=(SMEM, ANYWHERE, ANYWHERE, ANYWHERE),
            scratch_shapes=[
                pltpu.VMEM((blocks, ROWS, C), jnp.bfloat16),
                pltpu.VMEM((SPACES, 16, C), jnp.bfloat16),
                pltpu.SMEM((SPACES,), jnp.int32),
                pltpu.SMEM((slots,), jnp.int32),
                pltpu.SMEM((slots,), jnp.int32),
                pltpu.SemaphoreType.DMA((4,)),
            ],
        ),
        out_shape=(
            jax.ShapeDtypeStruct((slots,), jnp.int32),
            jax.ShapeDtypeStruct((blocks, ROWS, C), jnp.bfloat16),
            jax.ShapeDtypeStruct((MEMBERS, LOAD, C), jnp.bfloat16),
            jax.ShapeDtypeStruct((SPACES, 16, C), jnp.bfloat16),
        ),
        compiler_params=pltpu.CompilerParams(vmem_limit_bytes=VMEM_LIMIT),
        name="project_and_pack",
    )(*lists, team, points, geom, w_value, twice)


def pack_shifting(used, dests, x_local, own, notes):
    cross = x_local.shape[0]
    count = len(SHIFTS)

    def kernel(used_ref, dests_ref, cross_ref, own_ref, notes_ref, up_ref, *rest):
        out_refs, sem = rest[:count], rest[count]
        copies = []
        for k in range(count):
            for j in range(CAP):
                block = jnp.maximum(used_ref[dests_ref[k] * CAP + j], 0)
                copies.append((own_ref.at[block], out_refs[k].at[pl.ds(j * ROWS, ROWS)]))
            copies.append((notes_ref.at[dests_ref[k]], out_refs[k].at[pl.ds(NOTES, 16)]))
        for t in range(cross):
            copies.append((own_ref.at[cross_ref[t]], up_ref.at[t]))
        copies = [pltpu.make_async_copy(source, target, sem) for source, target in copies]
        for copy in copies:
            copy.start()
        for copy in copies:
            copy.wait()

    results = pl.pallas_call(
        kernel,
        in_specs=[SMEM] * 3 + [ANYWHERE] * 2,
        out_specs=(ANYWHERE,) * (1 + count),
        out_shape=(jax.ShapeDtypeStruct((cross, ROWS, C), jnp.bfloat16),)
        + (jax.ShapeDtypeStruct((LOAD, C), jnp.bfloat16),) * count,
        scratch_shapes=[pltpu.SemaphoreType.DMA],
        compiler_params=pltpu.CompilerParams(vmem_limit_bytes=VMEM_LIMIT),
        cost_estimate=pl.CostEstimate(
            flops=0, bytes_accessed=(count * LOAD + cross * ROWS) * C * 4, transcendentals=0
        ),
        name="pack_shifting",
    )(used, dests, x_local, own, notes)
    return results[0], results[1:]


def read_notes(load):
    note = load[pl.ds(NOTES, 16), :].astype(jnp.float32)
    entry = note[:CAP] * 512 + note[CAP : 2 * CAP] * 16 + note[2 * CAP : 3 * CAP]
    entries = [entry[j, 0].astype(jnp.int32) for j in range(CAP)]
    return [(value // 512, value % 512) for value in entries]


def unpack_kernels(packed):
    return jnp.concatenate([packed[:, :K], packed[:, K:]], axis=0)


def pair_terms(pairs):
    rows = lax.broadcasted_iota(jnp.int32, (BLK, BLK), 0)
    columns = lax.broadcasted_iota(jnp.int32, (BLK, BLK), 1)
    level = rows + columns
    scores = [
        lax.dot_general(
            unpack_kernels(a[BLK:, :]),
            unpack_kernels(b[BLK:, :]),
            (((1,), (1,)), ((), ())),
            preferred_element_type=jnp.float32,
        )
        for a, b, _ in pairs
    ]
    tiles = [
        jnp.where(level < cut, jnp.tanh(score * (1.0 / math.sqrt(K))), 0.0).astype(jnp.bfloat16)
        for score, (_, _, cut) in zip(scores, pairs)
    ]
    forward = [
        jnp.dot(tile, b[:BLK, :], preferred_element_type=jnp.float32) for tile, (_, b, _) in zip(tiles, pairs)
    ]
    backward = [
        lax.dot_general(tile, a[:BLK, :], (((0,), (0,)), ((), ())), preferred_element_type=jnp.float32)
        for tile, (a, _, _) in zip(tiles, pairs)
    ]
    return forward, backward


def pair_cost(number, blocks):
    return pl.CostEstimate(
        flops=2 * number * BLK * BLK * (K + 2 * C),
        bytes_accessed=number * (ROWS + BLK) * C * 2 + blocks * BLK * C * 8,
        transcendentals=number * BLK * BLK,
    )


def pairs_above(cross_meta, below, own):
    cross = below.shape[0]
    blocks = own.shape[0]

    def kernel(cross_ref, below_ref, own_ref, back_ref, total):
        total[...] = jnp.zeros_like(total)
        mine = [cross_ref[2 * t] for t in range(cross)]
        forward, backward = pair_terms(
            [(below_ref.at[t], own_ref.at[mine[t]], cross_ref[2 * t + 1]) for t in range(cross)]
        )
        for t in range(cross):
            back_ref[t] = forward[t].astype(jnp.bfloat16)
        for t in range(cross):
            total[mine[t]] = total[mine[t]] + backward[t]

    return pl.pallas_call(
        kernel,
        in_specs=[SMEM, VMEM, VMEM],
        out_specs=(VMEM, VMEM),
        out_shape=(
            jax.ShapeDtypeStruct((cross, BLK, C), jnp.bfloat16),
            jax.ShapeDtypeStruct((blocks, BLK, C), jnp.float32),
        ),
        compiler_params=pltpu.CompilerParams(vmem_limit_bytes=VMEM_LIMIT),
        cost_estimate=pair_cost(cross, blocks),
        name="pairs_above",
    )(cross_meta, below, own)


def team_pairs(arrived, own, aggregate, passing):
    blocks = own.shape[0]
    some = CREW * CAP
    handed = len(passing)

    def kernel(arrived_ref, own_ref, given_ref, *rest):
        back_ref, total_ref, total, sem = rest[handed], rest[handed + 1], rest[-2], rest[-1]
        i = pl.program_id(0)

        @pl.when(i == 0)
        def _():
            copy = pltpu.make_async_copy(given_ref, total, sem)
            copy.start()
            copy.wait()

        mine, pairs = [], []
        for m in range(CREW):
            load = arrived_ref.at[m]
            for j, (block, cut) in enumerate(read_notes(load)):
                mine.append(block)
                pairs.append((load.at[pl.ds(j * ROWS, ROWS)], own_ref.at[block], cut))
        forward, backward = pair_terms(pairs)
        for b in range(some):
            back_ref[b] = forward[b].astype(jnp.bfloat16)
        for b in range(some):
            total[mine[b]] = total[mine[b]] + backward[b]

        @pl.when(i == pl.num_programs(0) - 1)
        def _():
            copy = pltpu.make_async_copy(total, total_ref, sem)
            copy.start()
            copy.wait()

    results = pl.pallas_call(
        kernel,
        grid=(MEMBERS // CREW,),
        in_specs=[
            pl.BlockSpec((CREW, LOAD, C), lambda i: (i, 0, 0)),
            pl.BlockSpec((blocks, ROWS, C), lambda i: (0, 0, 0)),
            ANYWHERE,
        ]
        + [ANYWHERE] * handed,
        out_specs=(pl.BlockSpec((some, BLK, C), lambda i: (i, 0, 0)), ANYWHERE) + (ANYWHERE,) * handed,
        scratch_shapes=[
            pltpu.VMEM((blocks, BLK, C), jnp.float32),
            pltpu.SemaphoreType.DMA,
        ],
        out_shape=(
            jax.ShapeDtypeStruct((MEMBERS * CAP, BLK, C), jnp.bfloat16),
            jax.ShapeDtypeStruct((blocks, BLK, C), jnp.float32),
        )
        + tuple(jax.ShapeDtypeStruct(array.shape, array.dtype) for array in passing),
        input_output_aliases={3 + n: 2 + n for n in range(handed)},
        compiler_params=pltpu.CompilerParams(vmem_limit_bytes=VMEM_LIMIT),
        cost_estimate=pair_cost(MEMBERS * CAP, blocks),
        name="team_pairs",
    )(arrived, own, aggregate, *passing)
    return results[0], results[1], results[2:]


def shifted_pairs(arrived, own, aggregate, passing):
    count = len(arrived)
    blocks = own.shape[0]
    handed = len(passing)

    def kernel(own_ref, given_ref, *rest):
        arrived_refs, rest = rest[handed : handed + count], rest[handed + count :]
        back_refs, total = rest[:count], rest[count]
        total[...] = given_ref[...]
        places = [
            (k, j, block, cut)
            for k in range(count)
            for j, (block, cut) in enumerate(read_notes(arrived_refs[k]))
        ]
        for first in range(0, len(places), STAGE):
            some = places[first : first + STAGE]
            forward, backward = pair_terms(
                [
                    (arrived_refs[k].at[pl.ds(j * ROWS, ROWS)], own_ref.at[block], cut)
                    for k, j, block, cut in some
                ]
            )
            for n, (k, j, _, _) in enumerate(some):
                back_refs[k][j] = forward[n].astype(jnp.bfloat16)
            for n, (_, _, block, _) in enumerate(some):
                total[block] = total[block] + backward[n]

    results = pl.pallas_call(
        kernel,
        in_specs=[VMEM] * 2 + [ANYWHERE] * handed + [VMEM] * count,
        out_specs=(VMEM,) * (count + 1) + (ANYWHERE,) * handed,
        out_shape=(jax.ShapeDtypeStruct((CAP, BLK, C), jnp.bfloat16),) * count
        + (jax.ShapeDtypeStruct((blocks, BLK, C), jnp.float32),)
        + tuple(jax.ShapeDtypeStruct(array.shape, array.dtype) for array in passing),
        input_output_aliases={1: count} | {2 + n: count + 1 + n for n in range(handed)},
        compiler_params=pltpu.CompilerParams(vmem_limit_bytes=VMEM_LIMIT),
        cost_estimate=pair_cost(count * CAP, blocks),
        name="shifted_pairs",
    )(own, aggregate, *passing, *arrived)
    return results[:count], results[count], results[count + 1 :]


def add_back(used_ref, places_ref, back_refs, total):
    for k, back_ref in enumerate(back_refs):
        for j in range(CAP):
            mine = used_ref[places_ref[k] * CAP + j]

            @pl.when(mine >= 0)
            def _():
                total[mine] = total[mine] + back_ref[j].astype(jnp.float32)


def gather_team(used, team, x_local, returned, returned_x, aggregate):
    cross = returned_x.shape[0]

    def kernel(used_ref, team_ref, cross_ref, given_ref, back_ref, back_x_ref, total):
        total[...] = given_ref[...]
        for t in range(cross):
            mine = cross_ref[t]
            total[mine] = total[mine] + back_x_ref[t].astype(jnp.float32)

        @pl.loop(0, MEMBERS)
        def _(m):
            for j in range(CAP):
                mine = used_ref[team_ref[m] * CAP + j]

                @pl.when(mine >= 0)
                def _():
                    total[mine] = total[mine] + back_ref[m * CAP + j].astype(jnp.float32)

    return pl.pallas_call(
        kernel,
        in_specs=[SMEM] * 3 + [VMEM] * 3,
        out_specs=VMEM,
        out_shape=jax.ShapeDtypeStruct(aggregate.shape, jnp.float32),
        input_output_aliases={3: 0},
        compiler_params=pltpu.CompilerParams(vmem_limit_bytes=VMEM_LIMIT),
        cost_estimate=pl.CostEstimate(
            flops=returned.size, bytes_accessed=returned.size * 2 + aggregate.size * 8, transcendentals=0
        ),
        name="gather_team",
    )(used, team, x_local, aggregate, returned, returned_x)


def gather_shifted(used, dests, returned, aggregate):
    count = len(returned)

    def kernel(used_ref, dests_ref, given_ref, *rest):
        back_refs, total = rest[:count], rest[count]
        total[...] = given_ref[...]
        add_back(used_ref, dests_ref, back_refs, total)

    return pl.pallas_call(
        kernel,
        in_specs=[SMEM] * 2 + [VMEM] * (1 + count),
        out_specs=VMEM,
        out_shape=jax.ShapeDtypeStruct(aggregate.shape, jnp.float32),
        input_output_aliases={2: 0},
        compiler_params=pltpu.CompilerParams(vmem_limit_bytes=VMEM_LIMIT),
        cost_estimate=pl.CostEstimate(
            flops=count * CAP * BLK * C,
            bytes_accessed=count * CAP * BLK * C * 2 + aggregate.size * 8,
            transcendentals=0,
        ),
        name="gather_shifted",
    )(used, dests, aggregate, *returned)


def gather_and_mix(used, dests, returned, aggregate, points, w_out, gain):
    count = len(returned)
    blocks = aggregate.shape[0]
    some = 8

    def kernel(used_ref, dests_ref, total_ref, points_ref, w_ref, gain_ref, *rest):
        back_refs, out_ref, total, sem = rest[:count], rest[count], rest[count + 1], rest[count + 2]
        i = pl.program_id(0)

        @pl.when(i == 0)
        def _():
            copy = pltpu.make_async_copy(total_ref, total, sem)
            copy.start()
            copy.wait()
            add_back(used_ref, dests_ref, back_refs, total)

        for b in range(some):
            flat = total[i * some + b]
            meansq = jnp.mean(flat * flat, -1, keepdims=True)
            normed = flat * lax.rsqrt(meansq + 1e-06) * gain_ref[...]
            hidden = jax.nn.gelu(normed).astype(jnp.bfloat16)
            mixed = points_ref[pl.ds(b * BLK, BLK), :].astype(jnp.float32) + jnp.dot(
                hidden, w_ref[...], preferred_element_type=jnp.float32
            )
            out_ref[pl.ds(b * BLK, BLK), :] = mixed.astype(jnp.bfloat16)

    return pl.pallas_call(
        kernel,
        grid_spec=pltpu.PrefetchScalarGridSpec(
            num_scalar_prefetch=2,
            grid=(blocks // some,),
            in_specs=[
                pl.BlockSpec(memory_space=pl.ANY),
                pl.BlockSpec((some * BLK, C), lambda i, *_: (i, 0)),
                pl.BlockSpec((C, C), lambda i, *_: (0, 0)),
                pl.BlockSpec((1, C), lambda i, *_: (0, 0)),
            ]
            + [pl.BlockSpec((CAP, BLK, C), lambda i, *_: (0, 0, 0))] * count,
            out_specs=pl.BlockSpec((some * BLK, C), lambda i, *_: (i, 0)),
            scratch_shapes=[
                pltpu.VMEM((blocks, BLK, C), jnp.float32),
                pltpu.SemaphoreType.DMA,
            ],
        ),
        out_shape=jax.ShapeDtypeStruct((blocks * BLK, C), jnp.bfloat16),
        compiler_params=pltpu.CompilerParams(vmem_limit_bytes=VMEM_LIMIT),
        name="gather_and_mix",
    )(used, dests, aggregate, points, w_out, gain[None], *returned)


def body(feats, geom, w_value, w_kern, w_out, gain, t_local, t_dest, t_block, t_cut, x_local, x_block, x_cut):
    points = feats[0]
    me = lax.axis_index("space")
    dests = jnp.stack([partner_of(me, shift) for shift in SHIFTS]).astype(jnp.int32)
    member = jnp.arange(MEMBERS, dtype=jnp.int32)
    team = (member // SPAN_Y * 2 + me // SPAN_Y % 2) * SPAN_Y + member % SPAN_Y
    lists = (t_local[0], t_dest[0, :, 0], t_block[0], t_cut[0])
    used, own, leaving, notes = project_and_pack(points, geom[0], w_value, w_kern, lists, team)
    arrived = team_exchange(leaving)
    rising, shifting = pack_shifting(used, dests, x_local[0], own, notes)
    cross_meta = group_shift(jnp.stack([x_block[0], x_cut[0]], 1), 1).reshape(-1)
    below = group_shift(rising, 1)
    shifting = list(shifting)
    shifted = [None] * len(SHIFTS)

    def send(first, end):
        for k in range(first, end):
            shifted[k] = space_shift(shifting[k], SHIFTS[k])

    back_x, aggregate = pairs_above(cross_meta, below, own)
    returned_x = group_shift(back_x, -1)
    send(*BATCHES[0])
    first, end = BATCHES[1]
    back, aggregate, shifting[first:end] = team_pairs(
        arrived, own, aggregate, shifting[first:end]
    )
    back_shifted = []
    for turn, (first, end) in enumerate(BATCHES):
        later = slice(*BATCHES[turn + 2]) if turn + 2 < len(BATCHES) else slice(0, 0)
        if turn + 1 < len(BATCHES):
            send(*BATCHES[turn + 1])
        passing = shifting[later] + ([back] if turn == PASSED else [])
        back_some, aggregate, passing = shifted_pairs(
            shifted[first:end], own, aggregate, passing
        )
        shifting[later] = passing[: later.stop - later.start]
        if turn == PASSED:
            returned = team_exchange(passing[-1])
        back_shifted += [
            space_shift(block, (-dz, -dy)) for block, (dz, dy) in zip(back_some, SHIFTS[first:end])
        ]
    aggregate = gather_team(used, team, x_local[0], returned, returned_x, aggregate)
    for first, end in BATCHES[:-1]:
        aggregate = gather_shifted(used, dests[first:end], back_shifted[first:end], aggregate)
    first, end = BATCHES[-1]
    mixed = gather_and_mix(used, dests[first:end], back_shifted[first:end], aggregate, points, w_out, gain)
    return mixed[None]


def solution(mesh):
    in_specs = (
        P("group", "space", None),
        P("group", "space", None),
        P(),
        P(),
        P(),
        P(),
        P("group", "space"),
        P("group", "space", None),
        P("group", "space"),
        P("group", "space"),
        P("group", "space"),
        P("group", "space"),
        P("group", "space"),
    )
    out_specs = P("group", "space", None)
    return jax.shard_map(body, mesh=mesh, in_specs=in_specs, out_specs=out_specs, check_vma=False)
```

```python
import math

import jax
import jax.numpy as jnp
from jax import lax
from jax.experimental import pallas as pl
from jax.experimental.pallas import tpu as pltpu
from jax.sharding import PartitionSpec as P

C = 128
K = 64
BLK = 256
HALF = BLK // 2
ROWS = BLK + HALF
CAP = 3
VMEM_LIMIT = 56 * 1024 * 1024
SPAN_Z, SPAN_Y = 8, 4
SPACES = SPAN_Z * SPAN_Y
SHIFTS = tuple(
    shift for dy in range(SPAN_Y) for shift in ((3, dy), (-3, -dy), (1, dy), (-1, -dy))
)
BATCHES = ((0, 8), (8, 14), (14, 16))
PASSED = 2
MEMBERS = SPACES // 2
TEAMS = [[z * SPAN_Y + y for z in range(p, SPAN_Z, 2) for y in range(SPAN_Y)] for p in range(2)]
LATE = 12
STAGE = 8
SMEM = pl.BlockSpec(memory_space=pltpu.SMEM)
VMEM = pl.BlockSpec(memory_space=pltpu.VMEM)
ANYWHERE = pl.BlockSpec(memory_space=pl.ANY)
CREW = 4
NOTES = CAP * ROWS
LOAD = NOTES + 16


def space_shift(value, shift):
    return lax.ppermute(
        value,
        "space",
        [
            (z * SPAN_Y + y, (z + shift[0]) % SPAN_Z * SPAN_Y + (y + shift[1]) % SPAN_Y)
            for z in range(SPAN_Z)
            for y in range(SPAN_Y)
        ],
    )


def partner_of(me, shift):
    return (me // SPAN_Y + shift[0]) % SPAN_Z * SPAN_Y + (me % SPAN_Y + shift[1]) % SPAN_Y


def team_exchange(value):
    return lax.all_to_all(
        value, "space", split_axis=0, concat_axis=0, tiled=True, axis_index_groups=TEAMS
    )


def group_shift(value, steps):
    count = lax.axis_size("group")
    leading, last = (max(0, -steps), min(count, count - steps))
    return lax.ppermute(value, "group", [(source, source + steps) for source in range(leading, last)])


def project_and_pack(points, geom, w_value, w_kern, lists, x_local, team, dests):
    blocks = points.shape[0] // BLK
    cross = x_local.shape[0]
    tiles = lists[0].shape[0]
    count = len(SHIFTS)
    slots = SPACES * CAP
    step = 8

    def kernel(
        local_ref, dest_ref, block_ref, cut_ref, cross_ref, team_ref, dests_ref,
        points_ref, geom_ref, wv_ref, wk_ref, used_ref, own_ref, up_ref, team_out_ref, *rest
    ):
        out_refs, (held, notes, filled, partner, cuts, sems) = rest[:count], rest[count:]
        i = pl.program_id(0)

        @pl.when(i == 0)
        def _():
            @pl.loop(0, slots, unroll=8)
            def _(s):
                used_ref[s] = -1
                partner[s] = 0
                cuts[s] = 0

            @pl.loop(0, SPACES, unroll=8)
            def _(s):
                filled[s] = 0

            @pl.loop(0, tiles, unroll=4)
            def _(t):
                dest = dest_ref[t]
                slot = dest * CAP + filled[dest]
                filled[dest] = filled[dest] + 1
                used_ref[slot] = local_ref[t]
                partner[slot] = block_ref[t]
                cuts[slot] = cut_ref[t]

            row = lax.broadcasted_iota(jnp.int32, (16, C), 0)

            @pl.loop(0, SPACES, unroll=4)
            def _(d):
                note = jnp.zeros((16, C), jnp.int32)
                for j in range(CAP):
                    cut = cuts[d * CAP + j]
                    note = jnp.where(row == j, partner[d * CAP + j], note)
                    note = jnp.where(row == CAP + j, cut // 16, note)
                    note = jnp.where(row == 2 * CAP + j, cut % 16, note)
                notes[d] = note.astype(jnp.float32).astype(jnp.bfloat16)

        values = jnp.dot(points_ref[...], wv_ref[...], preferred_element_type=jnp.float32).astype(jnp.bfloat16)
        for b in range(step):
            base = b * BLK
            wide = jnp.concatenate(
                [geom_ref[pl.ds(base, HALF), :], geom_ref[pl.ds(base + HALF, HALF), :]], axis=1
            )
            held[i * step + b, :BLK, :] = values[base : base + BLK]
            held[i * step + b, BLK:, :] = jnp.dot(
                wide, wk_ref[...], preferred_element_type=jnp.float32
            ).astype(jnp.bfloat16)

        @pl.when(i == pl.num_programs(0) - 1)
        def _():
            copies = []

            def leave(dest, out):
                for j in range(CAP):
                    block = jnp.maximum(used_ref[dest * CAP + j], 0)
                    copies.append((held.at[block], out.at[pl.ds(j * ROWS, ROWS)]))
                copies.append((notes.at[dest], out.at[pl.ds(NOTES, 16)]))

            for m in range(MEMBERS):
                leave(team_ref[m], team_out_ref.at[m])
            for k in range(count):
                leave(dests_ref[k], out_refs[k])
            for t in range(cross):
                copies.append((held.at[cross_ref[t]], up_ref.at[t]))
            copies.append((held, own_ref))
            started = [pltpu.make_async_copy(source, target, sems) for source, target in copies]
            for copy in started:
                copy.start()
            for copy in started:
                copy.wait()

    zero = jnp.zeros_like(w_kern)
    twice = jnp.concatenate(
        [jnp.concatenate([w_kern, zero], 1), jnp.concatenate([zero, w_kern], 1)], 0
    )
    results = pl.pallas_call(
        kernel,
        grid_spec=pltpu.PrefetchScalarGridSpec(
            num_scalar_prefetch=7,
            grid=(blocks // step,),
            in_specs=[
                pl.BlockSpec((step * BLK, C), lambda i, *_: (i, 0)),
                pl.BlockSpec((step * BLK, C), lambda i, *_: (i, 0)),
                pl.BlockSpec((C, C), lambda i, *_: (0, 0)),
                pl.BlockSpec((2 * C, 2 * K), lambda i, *_: (0, 0)),
            ],
            out_specs=(SMEM,) + (ANYWHERE,) * (3 + count),
            scratch_shapes=[
                pltpu.VMEM((blocks, ROWS, C), jnp.bfloat16),
                pltpu.VMEM((SPACES, 16, C), jnp.bfloat16),
                pltpu.SMEM((SPACES,), jnp.int32),
                pltpu.SMEM((slots,), jnp.int32),
                pltpu.SMEM((slots,), jnp.int32),
                pltpu.SemaphoreType.DMA,
            ],
        ),
        out_shape=(
            jax.ShapeDtypeStruct((slots,), jnp.int32),
            jax.ShapeDtypeStruct((blocks, ROWS, C), jnp.bfloat16),
            jax.ShapeDtypeStruct((cross, ROWS, C), jnp.bfloat16),
            jax.ShapeDtypeStruct((MEMBERS, LOAD, C), jnp.bfloat16),
        )
        + (jax.ShapeDtypeStruct((LOAD, C), jnp.bfloat16),) * count,
        compiler_params=pltpu.CompilerParams(vmem_limit_bytes=VMEM_LIMIT),
        name="project_and_pack",
    )(*lists, x_local, team, dests, points, geom, w_value, twice)
    return results[:4], results[4:]


def read_notes(load):
    note = load[pl.ds(NOTES, 16), :].astype(jnp.float32)
    entry = note[:CAP] * 512 + note[CAP : 2 * CAP] * 16 + note[2 * CAP : 3 * CAP]
    entries = [entry[j, 0].astype(jnp.int32) for j in range(CAP)]
    return [(value // 512, value % 512) for value in entries]


def unpack_kernels(packed):
    return jnp.concatenate([packed[:, :K], packed[:, K:]], axis=0)


def pair_terms(pairs):
    rows = lax.broadcasted_iota(jnp.int32, (BLK, BLK), 0)
    columns = lax.broadcasted_iota(jnp.int32, (BLK, BLK), 1)
    level = rows + columns
    scores = [
        lax.dot_general(
            unpack_kernels(a[BLK:, :]),
            unpack_kernels(b[BLK:, :]),
            (((1,), (1,)), ((), ())),
            preferred_element_type=jnp.float32,
        )
        for a, b, _ in pairs
    ]
    tiles = [
        jnp.where(level < cut, jnp.tanh(score * (1.0 / math.sqrt(K))), 0.0).astype(jnp.bfloat16)
        for score, (_, _, cut) in zip(scores, pairs)
    ]
    forward = [
        jnp.dot(tile, b[:BLK, :], preferred_element_type=jnp.float32) for tile, (_, b, _) in zip(tiles, pairs)
    ]
    backward = [
        lax.dot_general(tile, a[:BLK, :], (((0,), (0,)), ((), ())), preferred_element_type=jnp.float32)
        for tile, (a, _, _) in zip(tiles, pairs)
    ]
    return forward, backward


def pair_cost(number, blocks):
    return pl.CostEstimate(
        flops=2 * number * BLK * BLK * (K + 2 * C),
        bytes_accessed=number * (ROWS + BLK) * C * 2 + blocks * BLK * C * 8,
        transcendentals=number * BLK * BLK,
    )


def pairs_above(cross_meta, below, own):
    cross = below.shape[0]
    blocks = own.shape[0]

    def kernel(cross_ref, below_ref, own_ref, back_ref, total):
        total[...] = jnp.zeros_like(total)
        mine = [cross_ref[2 * t] for t in range(cross)]
        forward, backward = pair_terms(
            [(below_ref.at[t], own_ref.at[mine[t]], cross_ref[2 * t + 1]) for t in range(cross)]
        )
        for t in range(cross):
            back_ref[t] = forward[t].astype(jnp.bfloat16)
        for t in range(cross):
            total[mine[t]] = total[mine[t]] + backward[t]

    return pl.pallas_call(
        kernel,
        in_specs=[SMEM, VMEM, VMEM],
        out_specs=(VMEM, VMEM),
        out_shape=(
            jax.ShapeDtypeStruct((cross, BLK, C), jnp.bfloat16),
            jax.ShapeDtypeStruct((blocks, BLK, C), jnp.float32),
        ),
        compiler_params=pltpu.CompilerParams(vmem_limit_bytes=VMEM_LIMIT),
        cost_estimate=pair_cost(cross, blocks),
        name="pairs_above",
    )(cross_meta, below, own)


def team_pairs(arrived, own, aggregate, passing):
    blocks = own.shape[0]
    some = CREW * CAP
    handed = len(passing)

    def kernel(arrived_ref, own_ref, given_ref, *rest):
        back_ref, total_ref, total, sem = rest[handed], rest[handed + 1], rest[-2], rest[-1]
        i = pl.program_id(0)

        @pl.when(i == 0)
        def _():
            copy = pltpu.make_async_copy(given_ref, total, sem)
            copy.start()
            copy.wait()

        mine, pairs = [], []
        for m in range(CREW):
            load = arrived_ref.at[m]
            for j, (block, cut) in enumerate(read_notes(load)):
                mine.append(block)
                pairs.append((load.at[pl.ds(j * ROWS, ROWS)], own_ref.at[block], cut))
        forward, backward = pair_terms(pairs)
        for b in range(some):
            back_ref[b] = forward[b].astype(jnp.bfloat16)
        for b in range(some):
            total[mine[b]] = total[mine[b]] + backward[b]

        @pl.when(i == pl.num_programs(0) - 1)
        def _():
            copy = pltpu.make_async_copy(total, total_ref, sem)
            copy.start()
            copy.wait()

    results = pl.pallas_call(
        kernel,
        grid=(MEMBERS // CREW,),
        in_specs=[
            pl.BlockSpec((CREW, LOAD, C), lambda i: (i, 0, 0)),
            pl.BlockSpec((blocks, ROWS, C), lambda i: (0, 0, 0)),
            ANYWHERE,
        ]
        + [ANYWHERE] * handed,
        out_specs=(pl.BlockSpec((some, BLK, C), lambda i: (i, 0, 0)), ANYWHERE) + (ANYWHERE,) * handed,
        scratch_shapes=[
            pltpu.VMEM((blocks, BLK, C), jnp.float32),
            pltpu.SemaphoreType.DMA,
        ],
        out_shape=(
            jax.ShapeDtypeStruct((MEMBERS * CAP, BLK, C), jnp.bfloat16),
            jax.ShapeDtypeStruct((blocks, BLK, C), jnp.float32),
        )
        + tuple(jax.ShapeDtypeStruct(array.shape, array.dtype) for array in passing),
        input_output_aliases={3 + n: 2 + n for n in range(handed)},
        compiler_params=pltpu.CompilerParams(vmem_limit_bytes=VMEM_LIMIT),
        cost_estimate=pair_cost(MEMBERS * CAP, blocks),
        name="team_pairs",
    )(arrived, own, aggregate, *passing)
    return results[0], results[1], results[2:]


def shifted_pairs(arrived, own, aggregate, passing):
    count = len(arrived)
    blocks = own.shape[0]
    handed = len(passing)

    def kernel(own_ref, given_ref, *rest):
        arrived_refs, rest = rest[handed : handed + count], rest[handed + count :]
        back_refs, total = rest[:count], rest[count]
        total[...] = given_ref[...]
        places = [
            (k, j, block, cut)
            for k in range(count)
            for j, (block, cut) in enumerate(read_notes(arrived_refs[k]))
        ]
        for first in range(0, len(places), STAGE):
            some = places[first : first + STAGE]
            forward, backward = pair_terms(
                [
                    (arrived_refs[k].at[pl.ds(j * ROWS, ROWS)], own_ref.at[block], cut)
                    for k, j, block, cut in some
                ]
            )
            for n, (k, j, _, _) in enumerate(some):
                back_refs[k][j] = forward[n].astype(jnp.bfloat16)
            for n, (_, _, block, _) in enumerate(some):
                total[block] = total[block] + backward[n]

    results = pl.pallas_call(
        kernel,
        in_specs=[VMEM] * 2 + [ANYWHERE] * handed + [VMEM] * count,
        out_specs=(VMEM,) * (count + 1) + (ANYWHERE,) * handed,
        out_shape=(jax.ShapeDtypeStruct((CAP, BLK, C), jnp.bfloat16),) * count
        + (jax.ShapeDtypeStruct((blocks, BLK, C), jnp.float32),)
        + tuple(jax.ShapeDtypeStruct(array.shape, array.dtype) for array in passing),
        input_output_aliases={1: count} | {2 + n: count + 1 + n for n in range(handed)},
        compiler_params=pltpu.CompilerParams(vmem_limit_bytes=VMEM_LIMIT),
        cost_estimate=pair_cost(count * CAP, blocks),
        name="shifted_pairs",
    )(own, aggregate, *passing, *arrived)
    return results[:count], results[count], results[count + 1 :]


def add_back(used_ref, places_ref, back_refs, total):
    for k, back_ref in enumerate(back_refs):
        for j in range(CAP):
            mine = used_ref[places_ref[k] * CAP + j]

            @pl.when(mine >= 0)
            def _():
                total[mine] = total[mine] + back_ref[j].astype(jnp.float32)


def gather_team(used, team, x_local, returned, returned_x, aggregate, passing):
    cross = returned_x.shape[0]
    handed = len(passing)

    def kernel(used_ref, team_ref, cross_ref, given_ref, back_ref, back_x_ref, *rest):
        total = rest[handed]
        total[...] = given_ref[...]
        for t in range(cross):
            mine = cross_ref[t]
            total[mine] = total[mine] + back_x_ref[t].astype(jnp.float32)

        @pl.loop(0, MEMBERS)
        def _(m):
            for j in range(CAP):
                mine = used_ref[team_ref[m] * CAP + j]

                @pl.when(mine >= 0)
                def _():
                    total[mine] = total[mine] + back_ref[m * CAP + j].astype(jnp.float32)

    results = pl.pallas_call(
        kernel,
        in_specs=[SMEM] * 3 + [VMEM] * 3 + [ANYWHERE] * handed,
        out_specs=(VMEM,) + (ANYWHERE,) * handed,
        out_shape=(jax.ShapeDtypeStruct(aggregate.shape, jnp.float32),)
        + tuple(jax.ShapeDtypeStruct(array.shape, array.dtype) for array in passing),
        input_output_aliases={3: 0} | {6 + n: 1 + n for n in range(handed)},
        compiler_params=pltpu.CompilerParams(vmem_limit_bytes=VMEM_LIMIT),
        cost_estimate=pl.CostEstimate(
            flops=returned.size, bytes_accessed=returned.size * 2 + aggregate.size * 8, transcendentals=0
        ),
        name="gather_team",
    )(used, team, x_local, aggregate, returned, returned_x, *passing)
    return results[0], results[1:]


def gather_shifted(used, dests, returned, aggregate):
    count = len(returned)

    def kernel(used_ref, dests_ref, given_ref, *rest):
        back_refs, total = rest[:count], rest[count]
        total[...] = given_ref[...]
        add_back(used_ref, dests_ref, back_refs, total)

    return pl.pallas_call(
        kernel,
        in_specs=[SMEM] * 2 + [VMEM] * (1 + count),
        out_specs=VMEM,
        out_shape=jax.ShapeDtypeStruct(aggregate.shape, jnp.float32),
        input_output_aliases={2: 0},
        compiler_params=pltpu.CompilerParams(vmem_limit_bytes=VMEM_LIMIT),
        cost_estimate=pl.CostEstimate(
            flops=count * CAP * BLK * C,
            bytes_accessed=count * CAP * BLK * C * 2 + aggregate.size * 8,
            transcendentals=0,
        ),
        name="gather_shifted",
    )(used, dests, aggregate, *returned)


def gather_and_mix(used, dests, returned, aggregate, points, w_out, gain):
    count = len(returned)
    blocks = aggregate.shape[0]
    some = 8

    def kernel(used_ref, dests_ref, total_ref, points_ref, w_ref, gain_ref, *rest):
        back_refs, out_ref, total, sem = rest[:count], rest[count], rest[count + 1], rest[count + 2]
        i = pl.program_id(0)

        @pl.when(i == 0)
        def _():
            copy = pltpu.make_async_copy(total_ref, total, sem)
            copy.start()
            copy.wait()
            add_back(used_ref, dests_ref, back_refs, total)

        for b in range(some):
            flat = total[i * some + b]
            meansq = jnp.mean(flat * flat, -1, keepdims=True)
            normed = flat * lax.rsqrt(meansq + 1e-06) * gain_ref[...]
            hidden = jax.nn.gelu(normed).astype(jnp.bfloat16)
            mixed = points_ref[pl.ds(b * BLK, BLK), :].astype(jnp.float32) + jnp.dot(
                hidden, w_ref[...], preferred_element_type=jnp.float32
            )
            out_ref[pl.ds(b * BLK, BLK), :] = mixed.astype(jnp.bfloat16)

    return pl.pallas_call(
        kernel,
        grid_spec=pltpu.PrefetchScalarGridSpec(
            num_scalar_prefetch=2,
            grid=(blocks // some,),
            in_specs=[
                pl.BlockSpec(memory_space=pl.ANY),
                pl.BlockSpec((some * BLK, C), lambda i, *_: (i, 0)),
                pl.BlockSpec((C, C), lambda i, *_: (0, 0)),
                pl.BlockSpec((1, C), lambda i, *_: (0, 0)),
            ]
            + [pl.BlockSpec((CAP, BLK, C), lambda i, *_: (0, 0, 0))] * count,
            out_specs=pl.BlockSpec((some * BLK, C), lambda i, *_: (i, 0)),
            scratch_shapes=[
                pltpu.VMEM((blocks, BLK, C), jnp.float32),
                pltpu.SemaphoreType.DMA,
            ],
        ),
        out_shape=jax.ShapeDtypeStruct((blocks * BLK, C), jnp.bfloat16),
        compiler_params=pltpu.CompilerParams(vmem_limit_bytes=VMEM_LIMIT),
        name="gather_and_mix",
    )(used, dests, aggregate, points, w_out, gain[None], *returned)


def body(feats, geom, w_value, w_kern, w_out, gain, t_local, t_dest, t_block, t_cut, x_local, x_block, x_cut):
    points = feats[0]
    me = lax.axis_index("space")
    dests = jnp.stack([partner_of(me, shift) for shift in SHIFTS]).astype(jnp.int32)
    member = jnp.arange(MEMBERS, dtype=jnp.int32)
    team = (member // SPAN_Y * 2 + me // SPAN_Y % 2) * SPAN_Y + member % SPAN_Y
    lists = (t_local[0], t_dest[0, :, 0], t_block[0], t_cut[0])
    (used, own, rising, leaving), shifting = project_and_pack(
        points, geom[0], w_value, w_kern, lists, x_local[0], team, dests
    )
    arrived = team_exchange(leaving)
    cross_meta = group_shift(jnp.stack([x_block[0], x_cut[0]], 1), 1).reshape(-1)
    below = group_shift(rising, 1)
    shifting = list(shifting)
    shifted = [None] * len(SHIFTS)

    def send(first, end):
        for k in range(first, end):
            shifted[k] = space_shift(shifting[k], SHIFTS[k])

    back_x, aggregate = pairs_above(cross_meta, below, own)
    returned_x = group_shift(back_x, -1)
    send(*BATCHES[0])
    first, end = BATCHES[1]
    back, aggregate, shifting[first:end] = team_pairs(
        arrived, own, aggregate, shifting[first:end]
    )
    going_back = []
    for turn, (first, end) in enumerate(BATCHES):
        later = slice(*BATCHES[turn + 2]) if turn + 2 < len(BATCHES) else slice(0, 0)
        if turn + 1 < len(BATCHES):
            send(*BATCHES[turn + 1])
        passing = shifting[later] + ([back] if turn == PASSED else [])
        back_some, aggregate, passing = shifted_pairs(
            shifted[first:end], own, aggregate, passing
        )
        shifting[later] = passing[: later.stop - later.start]
        if turn == PASSED:
            returned = team_exchange(passing[-1])
        going_back += back_some
    back_shifted = [None] * len(SHIFTS)

    def send_back(first, end):
        for k in range(first, end):
            dz, dy = SHIFTS[k]
            back_shifted[k] = space_shift(going_back[k], (-dz, -dy))

    send_back(0, LATE)
    aggregate, going_back[LATE:] = gather_team(
        used, team, x_local[0], returned, returned_x, aggregate, going_back[LATE:]
    )
    send_back(LATE, len(SHIFTS))
    aggregate = gather_shifted(used, dests[:LATE], back_shifted[:LATE], aggregate)
    mixed = gather_and_mix(used, dests[LATE:], back_shifted[LATE:], aggregate, points, w_out, gain)
    return mixed[None]


def solution(mesh):
    in_specs = (
        P("group", "space", None),
        P("group", "space", None),
        P(),
        P(),
        P(),
        P(),
        P("group", "space"),
        P("group", "space", None),
        P("group", "space"),
        P("group", "space"),
        P("group", "space"),
        P("group", "space"),
        P("group", "space"),
    )
    out_specs = P("group", "space", None)
    return jax.shard_map(body, mesh=mesh, in_specs=in_specs, out_specs=out_specs, check_vma=False)
```

```python
import math

import jax
import jax.numpy as jnp
from jax import lax
from jax.experimental import pallas as pl
from jax.experimental.pallas import tpu as pltpu
from jax.sharding import PartitionSpec as P

C = 128
K = 64
BLK = 256
HALF = BLK // 2
ROWS = BLK + HALF
CAP = 3
VMEM_LIMIT = 56 * 1024 * 1024
SPAN_Z, SPAN_Y = 8, 4
SPACES = SPAN_Z * SPAN_Y
SHIFTS = tuple(
    shift for dy in range(SPAN_Y) for shift in ((3, dy), (-3, -dy), (1, dy), (-1, -dy))
)
BATCHES = ((0, 8), (8, 14), (14, 16))
PASSED = 1
MEMBERS = SPACES // 2
TEAMS = [[z * SPAN_Y + y for z in range(p, SPAN_Z, 2) for y in range(SPAN_Y)] for p in range(2)]
LATE = 8
STAGE = 6
LONG = 10**12
SMEM = pl.BlockSpec(memory_space=pltpu.SMEM)
VMEM = pl.BlockSpec(memory_space=pltpu.VMEM)
ANYWHERE = pl.BlockSpec(memory_space=pl.ANY)
CREW = 4
NOTES = CAP * ROWS
LOAD = NOTES + 16


def space_shift(value, shift):
    return lax.ppermute(
        value,
        "space",
        [
            (z * SPAN_Y + y, (z + shift[0]) % SPAN_Z * SPAN_Y + (y + shift[1]) % SPAN_Y)
            for z in range(SPAN_Z)
            for y in range(SPAN_Y)
        ],
    )


def partner_of(me, shift):
    return (me // SPAN_Y + shift[0]) % SPAN_Z * SPAN_Y + (me % SPAN_Y + shift[1]) % SPAN_Y


def team_exchange(value):
    return lax.all_to_all(
        value, "space", split_axis=0, concat_axis=0, tiled=True, axis_index_groups=TEAMS
    )


def group_shift(value, steps):
    count = lax.axis_size("group")
    leading, last = (max(0, -steps), min(count, count - steps))
    return lax.ppermute(value, "group", [(source, source + steps) for source in range(leading, last)])


def project_and_pack(points, geom, w_value, w_kern, lists, x_local, team, dests):
    blocks = points.shape[0] // BLK
    cross = x_local.shape[0]
    tiles = lists[0].shape[0]
    count = len(SHIFTS)
    slots = SPACES * CAP
    step = 8

    def kernel(
        local_ref, dest_ref, block_ref, cut_ref, cross_ref, team_ref, dests_ref,
        points_ref, geom_ref, wv_ref, wk_ref, used_ref, own_ref, up_ref, team_out_ref, *rest
    ):
        out_refs, (held, notes, filled, partner, cuts, sems) = rest[:count], rest[count:]
        i = pl.program_id(0)

        @pl.when(i == 0)
        def _():
            @pl.loop(0, slots, unroll=8)
            def _(s):
                used_ref[s] = -1
                partner[s] = 0
                cuts[s] = 0

            @pl.loop(0, SPACES, unroll=8)
            def _(s):
                filled[s] = 0

            @pl.loop(0, tiles, unroll=4)
            def _(t):
                dest = dest_ref[t]
                slot = dest * CAP + filled[dest]
                filled[dest] = filled[dest] + 1
                used_ref[slot] = local_ref[t]
                partner[slot] = block_ref[t]
                cuts[slot] = cut_ref[t]

            row = lax.broadcasted_iota(jnp.int32, (16, C), 0)

            @pl.loop(0, SPACES, unroll=4)
            def _(d):
                note = jnp.zeros((16, C), jnp.int32)
                for j in range(CAP):
                    cut = cuts[d * CAP + j]
                    note = jnp.where(row == j, partner[d * CAP + j], note)
                    note = jnp.where(row == CAP + j, cut // 16, note)
                    note = jnp.where(row == 2 * CAP + j, cut % 16, note)
                notes[d] = note.astype(jnp.float32).astype(jnp.bfloat16)

        @pl.loop(0, step, unroll=2)
        def _(b):
            upper = pl.ds(pl.multiple_of(b * BLK, BLK), HALF)
            lower = pl.ds(pl.multiple_of(b * BLK + HALF, HALF), HALF)
            whole = pl.ds(pl.multiple_of(b * BLK, BLK), BLK)
            held[i * step + b, :BLK, :] = jnp.dot(
                points_ref[whole, :], wv_ref[...], preferred_element_type=jnp.float32
            ).astype(jnp.bfloat16)
            wide = jnp.concatenate([geom_ref[upper, :], geom_ref[lower, :]], axis=1)
            held[i * step + b, BLK:, :] = jnp.dot(
                wide, wk_ref[...], preferred_element_type=jnp.float32
            ).astype(jnp.bfloat16)

        @pl.when(i == pl.num_programs(0) - 1)
        def _():
            copies = []

            def leave(dest, out):
                for j in range(CAP):
                    block = jnp.maximum(used_ref[dest * CAP + j], 0)
                    copies.append((held.at[block], out.at[pl.ds(j * ROWS, ROWS)]))
                copies.append((notes.at[dest], out.at[pl.ds(NOTES, 16)]))

            for m in range(MEMBERS):
                leave(team_ref[m], team_out_ref.at[m])
            for k in range(count):
                leave(dests_ref[k], out_refs[k])
            for t in range(cross):
                copies.append((held.at[cross_ref[t]], up_ref.at[t]))
            copies.append((held, own_ref))
            started = [pltpu.make_async_copy(source, target, sems) for source, target in copies]
            for copy in started:
                copy.start()
            for copy in started:
                copy.wait()

    zero = jnp.zeros_like(w_kern)
    twice = jnp.concatenate(
        [jnp.concatenate([w_kern, zero], 1), jnp.concatenate([zero, w_kern], 1)], 0
    )
    results = pl.pallas_call(
        kernel,
        grid_spec=pltpu.PrefetchScalarGridSpec(
            num_scalar_prefetch=7,
            grid=(blocks // step,),
            in_specs=[
                pl.BlockSpec((step * BLK, C), lambda i, *_: (i, 0)),
                pl.BlockSpec((step * BLK, C), lambda i, *_: (i, 0)),
                pl.BlockSpec((C, C), lambda i, *_: (0, 0)),
                pl.BlockSpec((2 * C, 2 * K), lambda i, *_: (0, 0)),
            ],
            out_specs=(SMEM,) + (ANYWHERE,) * (3 + count),
            scratch_shapes=[
                pltpu.VMEM((blocks, ROWS, C), jnp.bfloat16),
                pltpu.VMEM((SPACES, 16, C), jnp.bfloat16),
                pltpu.SMEM((SPACES,), jnp.int32),
                pltpu.SMEM((slots,), jnp.int32),
                pltpu.SMEM((slots,), jnp.int32),
                pltpu.SemaphoreType.DMA,
            ],
        ),
        out_shape=(
            jax.ShapeDtypeStruct((slots,), jnp.int32),
            jax.ShapeDtypeStruct((blocks, ROWS, C), jnp.bfloat16),
            jax.ShapeDtypeStruct((cross, ROWS, C), jnp.bfloat16),
            jax.ShapeDtypeStruct((MEMBERS, LOAD, C), jnp.bfloat16),
        )
        + (jax.ShapeDtypeStruct((LOAD, C), jnp.bfloat16),) * count,
        compiler_params=pltpu.CompilerParams(vmem_limit_bytes=VMEM_LIMIT),
        name="project_and_pack",
    )(*lists, x_local, team, dests, points, geom, w_value, twice)
    return results[:4], results[4:]


def read_notes(load):
    note = load[pl.ds(NOTES, 16), :].astype(jnp.float32)
    entry = note[:CAP] * 512 + note[CAP : 2 * CAP] * 16 + note[2 * CAP : 3 * CAP]
    entries = [entry[j, 0].astype(jnp.int32) for j in range(CAP)]
    return [(value // 512, value % 512) for value in entries]


def unpack_kernels(packed):
    return jnp.concatenate([packed[:, :K], packed[:, K:]], axis=0)


def pair_terms(pairs):
    rows = lax.broadcasted_iota(jnp.int32, (BLK, BLK), 0)
    columns = lax.broadcasted_iota(jnp.int32, (BLK, BLK), 1)
    level = rows + columns
    scores = [
        lax.dot_general(
            unpack_kernels(a[BLK:, :]),
            unpack_kernels(b[BLK:, :]),
            (((1,), (1,)), ((), ())),
            preferred_element_type=jnp.float32,
        )
        for a, b, _ in pairs
    ]
    tiles = [
        jnp.where(level < cut, jnp.tanh(score * (1.0 / math.sqrt(K))), 0.0).astype(jnp.bfloat16)
        for score, (_, _, cut) in zip(scores, pairs)
    ]
    forward = [
        jnp.dot(tile, b[:BLK, :], preferred_element_type=jnp.float32) for tile, (_, b, _) in zip(tiles, pairs)
    ]
    backward = [
        lax.dot_general(tile, a[:BLK, :], (((0,), (0,)), ((), ())), preferred_element_type=jnp.float32)
        for tile, (a, _, _) in zip(tiles, pairs)
    ]
    return forward, backward


def pair_cost(number, blocks):
    return pl.CostEstimate(
        flops=2 * number * BLK * BLK * (K + 2 * C),
        bytes_accessed=number * (ROWS + BLK) * C * 2 + blocks * BLK * C * 8,
        transcendentals=number * BLK * BLK,
    )


def pairs_above(cross_meta, below, own):
    cross = below.shape[0]
    blocks = own.shape[0]
    some = math.gcd(cross, 4)

    def kernel(cross_ref, below_ref, own_ref, back_ref, total):
        total[...] = jnp.zeros_like(total)

        @pl.loop(0, cross, step=some)
        def _(first):
            mine = [cross_ref[2 * (first + t)] for t in range(some)]
            forward, backward = pair_terms(
                [
                    (below_ref.at[first + t], own_ref.at[mine[t]], cross_ref[2 * (first + t) + 1])
                    for t in range(some)
                ]
            )
            for t in range(some):
                back_ref[first + t] = forward[t].astype(jnp.bfloat16)
            for t in range(some):
                total[mine[t]] = total[mine[t]] + backward[t]

    return pl.pallas_call(
        kernel,
        in_specs=[SMEM, VMEM, VMEM],
        out_specs=(VMEM, VMEM),
        out_shape=(
            jax.ShapeDtypeStruct((cross, BLK, C), jnp.bfloat16),
            jax.ShapeDtypeStruct((blocks, BLK, C), jnp.float32),
        ),
        compiler_params=pltpu.CompilerParams(vmem_limit_bytes=VMEM_LIMIT),
        cost_estimate=pl.CostEstimate(flops=LONG, bytes_accessed=0, transcendentals=0),
        name="pairs_above",
    )(cross_meta, below, own)


def team_pairs(arrived, own, aggregate, passing):
    blocks = own.shape[0]
    some = CREW * CAP
    handed = len(passing)

    def kernel(arrived_ref, own_ref, given_ref, *rest):
        back_ref, total_ref, total, sem = rest[handed], rest[handed + 1], rest[-2], rest[-1]
        i = pl.program_id(0)

        @pl.when(i == 0)
        def _():
            copy = pltpu.make_async_copy(given_ref, total, sem)
            copy.start()
            copy.wait()

        @pl.loop(0, CREW, step=STAGE // CAP)
        def _(first):
            places = []
            for m in range(STAGE // CAP):
                load = arrived_ref.at[first + m]
                for j, (block, cut) in enumerate(read_notes(load)):
                    places.append((load.at[pl.ds(j * ROWS, ROWS)], block, cut))
            forward, backward = pair_terms([(a, own_ref.at[block], cut) for a, block, cut in places])
            for n in range(STAGE):
                back_ref[first * CAP + n] = forward[n].astype(jnp.bfloat16)
            for n, (_, block, _) in enumerate(places):
                total[block] = total[block] + backward[n]

        @pl.when(i == pl.num_programs(0) - 1)
        def _():
            copy = pltpu.make_async_copy(total, total_ref, sem)
            copy.start()
            copy.wait()

    results = pl.pallas_call(
        kernel,
        grid=(MEMBERS // CREW,),
        in_specs=[
            pl.BlockSpec((CREW, LOAD, C), lambda i: (i, 0, 0)),
            pl.BlockSpec((blocks, ROWS, C), lambda i: (0, 0, 0)),
            ANYWHERE,
        ]
        + [ANYWHERE] * handed,
        out_specs=(pl.BlockSpec((some, BLK, C), lambda i: (i, 0, 0)), ANYWHERE) + (ANYWHERE,) * handed,
        scratch_shapes=[
            pltpu.VMEM((blocks, BLK, C), jnp.float32),
            pltpu.SemaphoreType.DMA,
        ],
        out_shape=(
            jax.ShapeDtypeStruct((MEMBERS * CAP, BLK, C), jnp.bfloat16),
            jax.ShapeDtypeStruct((blocks, BLK, C), jnp.float32),
        )
        + tuple(jax.ShapeDtypeStruct(array.shape, array.dtype) for array in passing),
        input_output_aliases={3 + n: 2 + n for n in range(handed)},
        compiler_params=pltpu.CompilerParams(vmem_limit_bytes=VMEM_LIMIT),
        cost_estimate=pair_cost(MEMBERS * CAP, blocks),
        name="team_pairs",
    )(arrived, own, aggregate, *passing)
    return results[0], results[1], results[2:]


def shifted_pairs(arrived, own, aggregate, passing, cost):
    count = len(arrived)
    blocks = own.shape[0]
    handed = len(passing)

    def kernel(own_ref, given_ref, *rest):
        arrived_refs, rest = rest[handed : handed + count], rest[handed + count :]
        back_refs, total, loads, backs = rest[:count], rest[count], rest[-2], rest[-1]
        total[...] = given_ref[...]
        for k in range(count):
            loads[k] = arrived_refs[k][...]

        @pl.loop(0, count, step=STAGE // CAP)
        def _(first):
            places = []
            for k in range(STAGE // CAP):
                load = loads.at[first + k]
                for j, (block, cut) in enumerate(read_notes(load)):
                    places.append((load.at[pl.ds(j * ROWS, ROWS)], block, cut))
            forward, backward = pair_terms([(a, own_ref.at[block], cut) for a, block, cut in places])
            for n in range(STAGE):
                backs[first + n // CAP, n % CAP] = forward[n].astype(jnp.bfloat16)
            for n, (_, block, _) in enumerate(places):
                total[block] = total[block] + backward[n]

        for k in range(count):
            back_refs[k][...] = backs[k]

    results = pl.pallas_call(
        kernel,
        in_specs=[VMEM] * 2 + [ANYWHERE] * handed + [VMEM] * count,
        out_specs=(VMEM,) * (count + 1) + (ANYWHERE,) * handed,
        out_shape=(jax.ShapeDtypeStruct((CAP, BLK, C), jnp.bfloat16),) * count
        + (jax.ShapeDtypeStruct((blocks, BLK, C), jnp.float32),)
        + tuple(jax.ShapeDtypeStruct(array.shape, array.dtype) for array in passing),
        input_output_aliases={1: count} | {2 + n: count + 1 + n for n in range(handed)},
        scratch_shapes=[
            pltpu.VMEM((count, LOAD, C), jnp.bfloat16),
            pltpu.VMEM((count, CAP, BLK, C), jnp.bfloat16),
        ],
        compiler_params=pltpu.CompilerParams(vmem_limit_bytes=VMEM_LIMIT),
        cost_estimate=cost,
        name="shifted_pairs",
    )(own, aggregate, *passing, *arrived)
    return results[:count], results[count], results[count + 1 :]


def add_back(used_ref, places_ref, back_refs, total):
    for k, back_ref in enumerate(back_refs):
        for j in range(CAP):
            mine = used_ref[places_ref[k] * CAP + j]

            @pl.when(mine >= 0)
            def _():
                total[mine] = total[mine] + back_ref[j].astype(jnp.float32)


def gather_team(used, team, x_local, returned, returned_x, aggregate, passing):
    cross = returned_x.shape[0]
    handed = len(passing)

    def kernel(used_ref, team_ref, cross_ref, given_ref, back_ref, back_x_ref, *rest):
        total = rest[handed]
        total[...] = given_ref[...]
        for t in range(cross):
            mine = cross_ref[t]
            total[mine] = total[mine] + back_x_ref[t].astype(jnp.float32)

        @pl.loop(0, MEMBERS)
        def _(m):
            for j in range(CAP):
                mine = used_ref[team_ref[m] * CAP + j]

                @pl.when(mine >= 0)
                def _():
                    total[mine] = total[mine] + back_ref[m * CAP + j].astype(jnp.float32)

    results = pl.pallas_call(
        kernel,
        in_specs=[SMEM] * 3 + [VMEM] * 3 + [ANYWHERE] * handed,
        out_specs=(VMEM,) + (ANYWHERE,) * handed,
        out_shape=(jax.ShapeDtypeStruct(aggregate.shape, jnp.float32),)
        + tuple(jax.ShapeDtypeStruct(array.shape, array.dtype) for array in passing),
        input_output_aliases={3: 0} | {6 + n: 1 + n for n in range(handed)},
        compiler_params=pltpu.CompilerParams(vmem_limit_bytes=VMEM_LIMIT),
        cost_estimate=pl.CostEstimate(
            flops=returned.size, bytes_accessed=returned.size * 2 + aggregate.size * 8, transcendentals=0
        ),
        name="gather_team",
    )(used, team, x_local, aggregate, returned, returned_x, *passing)
    return results[0], results[1:]


def gather_and_mix(used, dests, returned, aggregate, points, w_out, gain):
    count = len(returned)
    blocks = aggregate.shape[0]
    some = 8

    def kernel(used_ref, dests_ref, total_ref, points_ref, w_ref, gain_ref, *rest):
        back_refs, out_ref, total, sem = rest[:count], rest[count], rest[count + 1], rest[count + 2]
        i = pl.program_id(0)

        @pl.when(i == 0)
        def _():
            copy = pltpu.make_async_copy(total_ref, total, sem)
            copy.start()
            copy.wait()
            add_back(used_ref, dests_ref, back_refs, total)

        @pl.loop(0, some, unroll=2)
        def _(b):
            rows = pl.ds(pl.multiple_of(b * BLK, BLK), BLK)
            flat = total[i * some + b]
            meansq = jnp.mean(flat * flat, -1, keepdims=True)
            normed = flat * lax.rsqrt(meansq + 1e-06) * gain_ref[...]
            hidden = jax.nn.gelu(normed).astype(jnp.bfloat16)
            mixed = points_ref[rows, :].astype(jnp.float32) + jnp.dot(
                hidden, w_ref[...], preferred_element_type=jnp.float32
            )
            out_ref[rows, :] = mixed.astype(jnp.bfloat16)

    return pl.pallas_call(
        kernel,
        grid_spec=pltpu.PrefetchScalarGridSpec(
            num_scalar_prefetch=2,
            grid=(blocks // some,),
            in_specs=[
                pl.BlockSpec(memory_space=pl.ANY),
                pl.BlockSpec((some * BLK, C), lambda i, *_: (i, 0)),
                pl.BlockSpec((C, C), lambda i, *_: (0, 0)),
                pl.BlockSpec((1, C), lambda i, *_: (0, 0)),
            ]
            + [pl.BlockSpec((CAP, BLK, C), lambda i, *_: (0, 0, 0))] * count,
            out_specs=pl.BlockSpec((some * BLK, C), lambda i, *_: (i, 0)),
            scratch_shapes=[
                pltpu.VMEM((blocks, BLK, C), jnp.float32),
                pltpu.SemaphoreType.DMA,
            ],
        ),
        out_shape=jax.ShapeDtypeStruct((blocks * BLK, C), jnp.bfloat16),
        compiler_params=pltpu.CompilerParams(vmem_limit_bytes=VMEM_LIMIT),
        name="gather_and_mix",
    )(used, dests, aggregate, points, w_out, gain[None], *returned)


def body(feats, geom, w_value, w_kern, w_out, gain, t_local, t_dest, t_block, t_cut, x_local, x_block, x_cut):
    points = feats[0]
    me = lax.axis_index("space")
    dests = jnp.stack([partner_of(me, shift) for shift in SHIFTS]).astype(jnp.int32)
    member = jnp.arange(MEMBERS, dtype=jnp.int32)
    team = (member // SPAN_Y * 2 + me // SPAN_Y % 2) * SPAN_Y + member % SPAN_Y
    lists = (t_local[0], t_dest[0, :, 0], t_block[0], t_cut[0])
    (used, own, rising, leaving), shifting = project_and_pack(
        points, geom[0], w_value, w_kern, lists, x_local[0], team, dests
    )
    arrived = team_exchange(leaving)
    cross_meta = group_shift(jnp.stack([x_block[0], x_cut[0]], 1), 1).reshape(-1)
    below = group_shift(rising, 1)
    shifting = list(shifting)
    shifted = [None] * len(SHIFTS)

    def send(first, end):
        for k in range(first, end):
            shifted[k] = space_shift(shifting[k], SHIFTS[k])

    back_x, aggregate = pairs_above(cross_meta, below, own)
    returned_x = group_shift(back_x, -1)
    send(*BATCHES[0])
    first, end = BATCHES[1]
    back, aggregate, shifting[first:end] = team_pairs(
        arrived, own, aggregate, shifting[first:end]
    )
    going_back = []
    for turn, (first, end) in enumerate(BATCHES):
        later = slice(*BATCHES[turn + 2]) if turn + 2 < len(BATCHES) else slice(0, 0)
        if turn + 1 < len(BATCHES):
            send(*BATCHES[turn + 1])
        passing = shifting[later] + ([back] if turn == PASSED else [])
        back_some, aggregate, passing = shifted_pairs(
            shifted[first:end], own, aggregate, passing,
            pl.CostEstimate(flops=LONG, bytes_accessed=0, transcendentals=0)
            if turn > PASSED
            else pair_cost((end - first) * CAP, own.shape[0]),
        )
        shifting[later] = passing[: later.stop - later.start]
        if turn == PASSED:
            returned = team_exchange(passing[-1])
        going_back += back_some
    back_shifted = [None] * len(SHIFTS)

    def send_back(first, end):
        for k in range(first, end):
            dz, dy = SHIFTS[k]
            back_shifted[k] = space_shift(going_back[k], (-dz, -dy))

    send_back(0, LATE)
    aggregate, going_back[LATE:] = gather_team(
        used, team, x_local[0], returned, returned_x, aggregate, going_back[LATE:]
    )
    send_back(LATE, len(SHIFTS))
    mixed = gather_and_mix(used, dests, back_shifted, aggregate, points, w_out, gain)
    return mixed[None]


def solution(mesh):
    in_specs = (
        P("group", "space", None),
        P("group", "space", None),
        P(),
        P(),
        P(),
        P(),
        P("group", "space"),
        P("group", "space", None),
        P("group", "space"),
        P("group", "space"),
        P("group", "space"),
        P("group", "space"),
        P("group", "space"),
    )
    out_specs = P("group", "space", None)
    return jax.shard_map(body, mesh=mesh, in_specs=in_specs, out_specs=out_specs, check_vma=False)
```

```python
import math

import jax
import jax.numpy as jnp
from jax import lax
from jax.experimental import pallas as pl
from jax.experimental.pallas import tpu as pltpu
from jax.sharding import PartitionSpec as P

C = 128
K = 64
BLK = 256
HALF = BLK // 2
ROWS = BLK + HALF
CAP = 3
VMEM_LIMIT = 56 * 1024 * 1024
SPAN_Z, SPAN_Y = 8, 4
SPACES = SPAN_Z * SPAN_Y
SHIFTS = tuple(
    shift for dy in range(SPAN_Y) for shift in ((3, dy), (-3, -dy), (1, dy), (-1, -dy))
)
BATCHES = ((0, 8), (8, 14), (14, 16))
GATES = (4, 14)
GATE = 0
PASSED = 1
MEMBERS = SPACES // 2
TEAMS = [[z * SPAN_Y + y for z in range(p, SPAN_Z, 2) for y in range(SPAN_Y)] for p in range(2)]
LATE = 8
STAGE = 6
LONG = 10**12
SMEM = pl.BlockSpec(memory_space=pltpu.SMEM)
VMEM = pl.BlockSpec(memory_space=pltpu.VMEM)
ANYWHERE = pl.BlockSpec(memory_space=pl.ANY)
CREW = 4
NOTES = CAP * ROWS
LOAD = NOTES + 16


def space_shift(value, shift):
    return lax.ppermute(
        value,
        "space",
        [
            (z * SPAN_Y + y, (z + shift[0]) % SPAN_Z * SPAN_Y + (y + shift[1]) % SPAN_Y)
            for z in range(SPAN_Z)
            for y in range(SPAN_Y)
        ],
    )


def partner_of(me, shift):
    return (me // SPAN_Y + shift[0]) % SPAN_Z * SPAN_Y + (me % SPAN_Y + shift[1]) % SPAN_Y


def team_exchange(value):
    return lax.all_to_all(
        value, "space", split_axis=0, concat_axis=0, tiled=True, axis_index_groups=TEAMS
    )


def group_shift(value, steps):
    count = lax.axis_size("group")
    leading, last = (max(0, -steps), min(count, count - steps))
    return lax.ppermute(value, "group", [(source, source + steps) for source in range(leading, last)])


def project_and_pack(points, geom, w_value, w_kern, lists, x_local, team, dests):
    blocks = points.shape[0] // BLK
    cross = x_local.shape[0]
    tiles = lists[0].shape[0]
    count = len(SHIFTS)
    slots = SPACES * CAP
    step = 8

    def kernel(
        local_ref, dest_ref, block_ref, cut_ref, cross_ref, team_ref, dests_ref,
        points_ref, geom_ref, wv_ref, wk_ref, used_ref, own_ref, up_ref, team_out_ref, *rest
    ):
        out_refs, (held, notes, filled, partner, cuts, sems) = rest[:count], rest[count:]
        i = pl.program_id(0)

        @pl.when(i == 0)
        def _():
            @pl.loop(0, slots, unroll=8)
            def _(s):
                used_ref[s] = -1
                partner[s] = 0
                cuts[s] = 0

            @pl.loop(0, SPACES, unroll=8)
            def _(s):
                filled[s] = 0

            @pl.loop(0, tiles, unroll=4)
            def _(t):
                dest = dest_ref[t]
                slot = dest * CAP + filled[dest]
                filled[dest] = filled[dest] + 1
                used_ref[slot] = local_ref[t]
                partner[slot] = block_ref[t]
                cuts[slot] = cut_ref[t]

            row = lax.broadcasted_iota(jnp.int32, (16, C), 0)

            @pl.loop(0, SPACES, unroll=4)
            def _(d):
                note = jnp.zeros((16, C), jnp.int32)
                for j in range(CAP):
                    cut = cuts[d * CAP + j]
                    note = jnp.where(row == j, partner[d * CAP + j], note)
                    note = jnp.where(row == CAP + j, cut // 16, note)
                    note = jnp.where(row == 2 * CAP + j, cut % 16, note)
                notes[d] = note.astype(jnp.float32).astype(jnp.bfloat16)

        @pl.loop(0, step, unroll=4)
        def _(b):
            upper = pl.ds(pl.multiple_of(b * BLK, BLK), HALF)
            lower = pl.ds(pl.multiple_of(b * BLK + HALF, HALF), HALF)
            whole = pl.ds(pl.multiple_of(b * BLK, BLK), BLK)
            held[i * step + b, :BLK, :] = jnp.dot(
                points_ref[whole, :], wv_ref[...], preferred_element_type=jnp.float32
            ).astype(jnp.bfloat16)
            wide = jnp.concatenate([geom_ref[upper, :], geom_ref[lower, :]], axis=1)
            held[i * step + b, BLK:, :] = jnp.dot(
                wide, wk_ref[...], preferred_element_type=jnp.float32
            ).astype(jnp.bfloat16)

        @pl.when(i == pl.num_programs(0) - 1)
        def _():
            copies = []

            def leave(dest, out):
                for j in range(CAP):
                    block = jnp.maximum(used_ref[dest * CAP + j], 0)
                    copies.append((held.at[block], out.at[pl.ds(j * ROWS, ROWS)]))
                copies.append((notes.at[dest], out.at[pl.ds(NOTES, 16)]))

            for m in range(MEMBERS):
                leave(team_ref[m], team_out_ref.at[m])
            for k in range(count):
                leave(dests_ref[k], out_refs[k])
            for t in range(cross):
                copies.append((held.at[cross_ref[t]], up_ref.at[t]))
            copies.append((held, own_ref))
            started = [pltpu.make_async_copy(source, target, sems) for source, target in copies]
            for copy in started:
                copy.start()
            for copy in started:
                copy.wait()

    zero = jnp.zeros_like(w_kern)
    twice = jnp.concatenate(
        [jnp.concatenate([w_kern, zero], 1), jnp.concatenate([zero, w_kern], 1)], 0
    )
    results = pl.pallas_call(
        kernel,
        grid_spec=pltpu.PrefetchScalarGridSpec(
            num_scalar_prefetch=7,
            grid=(blocks // step,),
            in_specs=[
                pl.BlockSpec((step * BLK, C), lambda i, *_: (i, 0)),
                pl.BlockSpec((step * BLK, C), lambda i, *_: (i, 0)),
                pl.BlockSpec((C, C), lambda i, *_: (0, 0)),
                pl.BlockSpec((2 * C, 2 * K), lambda i, *_: (0, 0)),
            ],
            out_specs=(SMEM,) + (ANYWHERE,) * (3 + count),
            scratch_shapes=[
                pltpu.VMEM((blocks, ROWS, C), jnp.bfloat16),
                pltpu.VMEM((SPACES, 16, C), jnp.bfloat16),
                pltpu.SMEM((SPACES,), jnp.int32),
                pltpu.SMEM((slots,), jnp.int32),
                pltpu.SMEM((slots,), jnp.int32),
                pltpu.SemaphoreType.DMA,
            ],
        ),
        out_shape=(
            jax.ShapeDtypeStruct((slots,), jnp.int32),
            jax.ShapeDtypeStruct((blocks, ROWS, C), jnp.bfloat16),
            jax.ShapeDtypeStruct((cross, ROWS, C), jnp.bfloat16),
            jax.ShapeDtypeStruct((MEMBERS, LOAD, C), jnp.bfloat16),
        )
        + (jax.ShapeDtypeStruct((LOAD, C), jnp.bfloat16),) * count,
        compiler_params=pltpu.CompilerParams(vmem_limit_bytes=VMEM_LIMIT),
        name="project_and_pack",
    )(*lists, x_local, team, dests, points, geom, w_value, twice)
    return results[:4], results[4:]


def read_notes(load):
    note = load[pl.ds(NOTES, 16), :].astype(jnp.float32)
    entry = note[:CAP] * 512 + note[CAP : 2 * CAP] * 16 + note[2 * CAP : 3 * CAP]
    entries = [entry[j, 0].astype(jnp.int32) for j in range(CAP)]
    return [(value // 512, value % 512) for value in entries]


def unpack_kernels(packed):
    return jnp.concatenate([packed[:, :K], packed[:, K:]], axis=0)


def pair_terms(pairs):
    rows = lax.broadcasted_iota(jnp.int32, (BLK, BLK), 0)
    columns = lax.broadcasted_iota(jnp.int32, (BLK, BLK), 1)
    level = rows + columns
    scores = [
        lax.dot_general(
            unpack_kernels(a[BLK:, :]),
            unpack_kernels(b[BLK:, :]),
            (((1,), (1,)), ((), ())),
            preferred_element_type=jnp.float32,
        )
        for a, b, _ in pairs
    ]
    tiles = [
        jnp.where(level < cut, jnp.tanh(score * (1.0 / math.sqrt(K))), 0.0).astype(jnp.bfloat16)
        for score, (_, _, cut) in zip(scores, pairs)
    ]
    forward = [
        jnp.dot(tile, b[:BLK, :], preferred_element_type=jnp.float32) for tile, (_, b, _) in zip(tiles, pairs)
    ]
    backward = [
        lax.dot_general(tile, a[:BLK, :], (((0,), (0,)), ((), ())), preferred_element_type=jnp.float32)
        for tile, (a, _, _) in zip(tiles, pairs)
    ]
    return forward, backward


def pair_cost(number, blocks):
    return pl.CostEstimate(
        flops=2 * number * BLK * BLK * (K + 2 * C),
        bytes_accessed=number * (ROWS + BLK) * C * 2 + blocks * BLK * C * 8,
        transcendentals=number * BLK * BLK,
    )


def pairs_above(cross_meta, below, own):
    cross = below.shape[0]
    blocks = own.shape[0]
    some = math.gcd(cross, 4)

    def kernel(cross_ref, below_ref, own_ref, back_ref, total):
        total[...] = jnp.zeros_like(total)

        @pl.loop(0, cross, step=some)
        def _(first):
            mine = [cross_ref[2 * (first + t)] for t in range(some)]
            forward, backward = pair_terms(
                [
                    (below_ref.at[first + t], own_ref.at[mine[t]], cross_ref[2 * (first + t) + 1])
                    for t in range(some)
                ]
            )
            for t in range(some):
                back_ref[first + t] = forward[t].astype(jnp.bfloat16)
            for t in range(some):
                total[mine[t]] = total[mine[t]] + backward[t]

    return pl.pallas_call(
        kernel,
        in_specs=[SMEM, VMEM, VMEM],
        out_specs=(VMEM, VMEM),
        out_shape=(
            jax.ShapeDtypeStruct((cross, BLK, C), jnp.bfloat16),
            jax.ShapeDtypeStruct((blocks, BLK, C), jnp.float32),
        ),
        compiler_params=pltpu.CompilerParams(vmem_limit_bytes=VMEM_LIMIT),
        cost_estimate=pl.CostEstimate(flops=LONG, bytes_accessed=0, transcendentals=0),
        name="pairs_above",
    )(cross_meta, below, own)


def team_pairs(arrived, own, aggregate, passing):
    blocks = own.shape[0]
    some = CREW * CAP
    handed = len(passing)

    def kernel(arrived_ref, own_ref, given_ref, *rest):
        back_ref, total_ref, total, sem = rest[handed], rest[handed + 1], rest[-2], rest[-1]
        i = pl.program_id(0)

        @pl.when(i == 0)
        def _():
            copy = pltpu.make_async_copy(given_ref, total, sem)
            copy.start()
            copy.wait()

        @pl.loop(0, CREW, step=STAGE // CAP)
        def _(first):
            places = []
            for m in range(STAGE // CAP):
                load = arrived_ref.at[first + m]
                for j, (block, cut) in enumerate(read_notes(load)):
                    places.append((load.at[pl.ds(j * ROWS, ROWS)], block, cut))
            forward, backward = pair_terms([(a, own_ref.at[block], cut) for a, block, cut in places])
            for n in range(STAGE):
                back_ref[first * CAP + n] = forward[n].astype(jnp.bfloat16)
            for n, (_, block, _) in enumerate(places):
                total[block] = total[block] + backward[n]

        @pl.when(i == pl.num_programs(0) - 1)
        def _():
            copy = pltpu.make_async_copy(total, total_ref, sem)
            copy.start()
            copy.wait()

    results = pl.pallas_call(
        kernel,
        grid=(MEMBERS // CREW,),
        in_specs=[
            pl.BlockSpec((CREW, LOAD, C), lambda i: (i, 0, 0)),
            pl.BlockSpec((blocks, ROWS, C), lambda i: (0, 0, 0)),
            ANYWHERE,
        ]
        + [ANYWHERE] * handed,
        out_specs=(pl.BlockSpec((some, BLK, C), lambda i: (i, 0, 0)), ANYWHERE) + (ANYWHERE,) * handed,
        scratch_shapes=[
            pltpu.VMEM((blocks, BLK, C), jnp.float32),
            pltpu.SemaphoreType.DMA,
        ],
        out_shape=(
            jax.ShapeDtypeStruct((MEMBERS * CAP, BLK, C), jnp.bfloat16),
            jax.ShapeDtypeStruct((blocks, BLK, C), jnp.float32),
        )
        + tuple(jax.ShapeDtypeStruct(array.shape, array.dtype) for array in passing),
        input_output_aliases={3 + n: 2 + n for n in range(handed)},
        compiler_params=pltpu.CompilerParams(vmem_limit_bytes=VMEM_LIMIT),
        cost_estimate=pair_cost(MEMBERS * CAP, blocks),
        name="team_pairs",
    )(arrived, own, aggregate, *passing)
    return results[0], results[1], results[2:]


def shifted_pairs(arrived, own, aggregate, passing, cost):
    count = len(arrived)
    blocks = own.shape[0]
    handed = len(passing)

    def kernel(own_ref, given_ref, *rest):
        arrived_refs, rest = rest[handed : handed + count], rest[handed + count :]
        back_refs, total, loads, backs = rest[:count], rest[count], rest[-2], rest[-1]
        total[...] = given_ref[...]
        for k in range(count):
            loads[k] = arrived_refs[k][...]

        @pl.loop(0, count, step=STAGE // CAP)
        def _(first):
            places = []
            for k in range(STAGE // CAP):
                load = loads.at[first + k]
                for j, (block, cut) in enumerate(read_notes(load)):
                    places.append((load.at[pl.ds(j * ROWS, ROWS)], block, cut))
            forward, backward = pair_terms([(a, own_ref.at[block], cut) for a, block, cut in places])
            for n in range(STAGE):
                backs[first + n // CAP, n % CAP] = forward[n].astype(jnp.bfloat16)
            for n, (_, block, _) in enumerate(places):
                total[block] = total[block] + backward[n]

        for k in range(count):
            back_refs[k][...] = backs[k]

    results = pl.pallas_call(
        kernel,
        in_specs=[VMEM] * 2 + [ANYWHERE] * handed + [VMEM] * count,
        out_specs=(VMEM,) * (count + 1) + (ANYWHERE,) * handed,
        out_shape=(jax.ShapeDtypeStruct((CAP, BLK, C), jnp.bfloat16),) * count
        + (jax.ShapeDtypeStruct((blocks, BLK, C), jnp.float32),)
        + tuple(jax.ShapeDtypeStruct(array.shape, array.dtype) for array in passing),
        input_output_aliases={1: count} | {2 + n: count + 1 + n for n in range(handed)},
        scratch_shapes=[
            pltpu.VMEM((count, LOAD, C), jnp.bfloat16),
            pltpu.VMEM((count, CAP, BLK, C), jnp.bfloat16),
        ],
        compiler_params=pltpu.CompilerParams(vmem_limit_bytes=VMEM_LIMIT),
        cost_estimate=cost,
        name="shifted_pairs",
    )(own, aggregate, *passing, *arrived)
    return results[:count], results[count], results[count + 1 :]


def add_back(used_ref, places_ref, back_refs, total):
    for k, back_ref in enumerate(back_refs):
        for j in range(CAP):
            mine = used_ref[places_ref[k] * CAP + j]

            @pl.when(mine >= 0)
            def _():
                total[mine] = total[mine] + back_ref[j].astype(jnp.float32)


def gather_team(used, team, x_local, returned, returned_x, aggregate, passing):
    cross = returned_x.shape[0]
    handed = len(passing)

    def kernel(used_ref, team_ref, cross_ref, given_ref, back_ref, back_x_ref, *rest):
        total = rest[handed]
        total[...] = given_ref[...]
        for t in range(cross):
            mine = cross_ref[t]
            total[mine] = total[mine] + back_x_ref[t].astype(jnp.float32)

        @pl.loop(0, MEMBERS)
        def _(m):
            for j in range(CAP):
                mine = used_ref[team_ref[m] * CAP + j]

                @pl.when(mine >= 0)
                def _():
                    total[mine] = total[mine] + back_ref[m * CAP + j].astype(jnp.float32)

    results = pl.pallas_call(
        kernel,
        in_specs=[SMEM] * 3 + [VMEM] * 3 + [ANYWHERE] * handed,
        out_specs=(VMEM,) + (ANYWHERE,) * handed,
        out_shape=(jax.ShapeDtypeStruct(aggregate.shape, jnp.float32),)
        + tuple(jax.ShapeDtypeStruct(array.shape, array.dtype) for array in passing),
        input_output_aliases={3: 0} | {6 + n: 1 + n for n in range(handed)},
        compiler_params=pltpu.CompilerParams(vmem_limit_bytes=VMEM_LIMIT),
        cost_estimate=pl.CostEstimate(
            flops=returned.size, bytes_accessed=returned.size * 2 + aggregate.size * 8, transcendentals=0
        ),
        name="gather_team",
    )(used, team, x_local, aggregate, returned, returned_x, *passing)
    return results[0], results[1:]


def gather_and_mix(used, dests, returned, aggregate, points, w_out, gain):
    count = len(returned)
    blocks = aggregate.shape[0]
    some = 8

    def kernel(used_ref, dests_ref, total_ref, points_ref, w_ref, gain_ref, *rest):
        back_refs, out_ref, total, sem = rest[:count], rest[count], rest[count + 1], rest[count + 2]
        i = pl.program_id(0)

        @pl.when(i == 0)
        def _():
            copy = pltpu.make_async_copy(total_ref, total, sem)
            copy.start()
            copy.wait()
            add_back(used_ref, dests_ref, back_refs, total)

        @pl.loop(0, some, unroll=2)
        def _(b):
            rows = pl.ds(pl.multiple_of(b * BLK, BLK), BLK)
            flat = total[i * some + b]
            meansq = jnp.mean(flat * flat, -1, keepdims=True)
            normed = flat * lax.rsqrt(meansq + 1e-06) * gain_ref[...]
            hidden = jax.nn.gelu(normed).astype(jnp.bfloat16)
            mixed = points_ref[rows, :].astype(jnp.float32) + jnp.dot(
                hidden, w_ref[...], preferred_element_type=jnp.float32
            )
            out_ref[rows, :] = mixed.astype(jnp.bfloat16)

    return pl.pallas_call(
        kernel,
        grid_spec=pltpu.PrefetchScalarGridSpec(
            num_scalar_prefetch=2,
            grid=(blocks // some,),
            in_specs=[
                pl.BlockSpec(memory_space=pl.ANY),
                pl.BlockSpec((some * BLK, C), lambda i, *_: (i, 0)),
                pl.BlockSpec((C, C), lambda i, *_: (0, 0)),
                pl.BlockSpec((1, C), lambda i, *_: (0, 0)),
            ]
            + [pl.BlockSpec((CAP, BLK, C), lambda i, *_: (0, 0, 0))] * count,
            out_specs=pl.BlockSpec((some * BLK, C), lambda i, *_: (i, 0)),
            scratch_shapes=[
                pltpu.VMEM((blocks, BLK, C), jnp.float32),
                pltpu.SemaphoreType.DMA,
            ],
        ),
        out_shape=jax.ShapeDtypeStruct((blocks * BLK, C), jnp.bfloat16),
        compiler_params=pltpu.CompilerParams(vmem_limit_bytes=VMEM_LIMIT),
        name="gather_and_mix",
    )(used, dests, aggregate, points, w_out, gain[None], *returned)


def body(feats, geom, w_value, w_kern, w_out, gain, t_local, t_dest, t_block, t_cut, x_local, x_block, x_cut):
    points = feats[0]
    me = lax.axis_index("space")
    dests = jnp.stack([partner_of(me, shift) for shift in SHIFTS]).astype(jnp.int32)
    member = jnp.arange(MEMBERS, dtype=jnp.int32)
    team = (member // SPAN_Y * 2 + me // SPAN_Y % 2) * SPAN_Y + member % SPAN_Y
    lists = (t_local[0], t_dest[0, :, 0], t_block[0], t_cut[0])
    (used, own, rising, leaving), shifting = project_and_pack(
        points, geom[0], w_value, w_kern, lists, x_local[0], team, dests
    )
    arrived = team_exchange(leaving)
    cross_meta = group_shift(jnp.stack([x_block[0], x_cut[0]], 1), 1).reshape(-1)
    below = group_shift(rising, 1)
    shifting = list(shifting)
    shifted = [None] * len(SHIFTS)

    def send(first, end):
        for k in range(first, end):
            shifted[k] = space_shift(shifting[k], SHIFTS[k])

    back_x, aggregate = pairs_above(cross_meta, below, own)
    returned_x = group_shift(back_x, -1)
    send(0, GATES[0])
    first, end = GATES
    back, aggregate, shifting[first:end] = team_pairs(arrived, own, aggregate, shifting[first:end])
    send(first, end)
    going_back = []
    for turn, (first, end) in enumerate(BATCHES):
        later = slice(GATES[1], len(SHIFTS)) if turn == GATE else slice(0, 0)
        passing = shifting[later] + ([back] if turn == PASSED else [])
        back_some, aggregate, passing = shifted_pairs(
            shifted[first:end], own, aggregate, passing,
            pl.CostEstimate(flops=LONG, bytes_accessed=0, transcendentals=0)
            if turn > PASSED
            else pair_cost((end - first) * CAP, own.shape[0]),
        )
        shifting[later] = passing[: later.stop - later.start]
        if turn == GATE:
            send(GATES[1], len(SHIFTS))
        if turn == PASSED:
            returned = team_exchange(passing[-1])
        going_back += back_some
    back_shifted = [None] * len(SHIFTS)

    def send_back(first, end):
        for k in range(first, end):
            dz, dy = SHIFTS[k]
            back_shifted[k] = space_shift(going_back[k], (-dz, -dy))

    send_back(0, LATE)
    aggregate, going_back[LATE:] = gather_team(
        used, team, x_local[0], returned, returned_x, aggregate, going_back[LATE:]
    )
    send_back(LATE, len(SHIFTS))
    mixed = gather_and_mix(used, dests, back_shifted, aggregate, points, w_out, gain)
    return mixed[None]


def solution(mesh):
    in_specs = (
        P("group", "space", None),
        P("group", "space", None),
        P(),
        P(),
        P(),
        P(),
        P("group", "space"),
        P("group", "space", None),
        P("group", "space"),
        P("group", "space"),
        P("group", "space"),
        P("group", "space"),
        P("group", "space"),
    )
    out_specs = P("group", "space", None)
    return jax.shard_map(body, mesh=mesh, in_specs=in_specs, out_specs=out_specs, check_vma=False)
```

```python
import math

import jax
import jax.numpy as jnp
from jax import lax
from jax.experimental import pallas as pl
from jax.experimental.pallas import tpu as pltpu
from jax.sharding import PartitionSpec as P

C = 128
K = 64
BLK = 256
HALF = BLK // 2
ROWS = BLK + HALF
CAP = 3
VMEM_LIMIT = 56 * 1024 * 1024
SPAN_Z, SPAN_Y = 8, 4
SPACES = SPAN_Z * SPAN_Y
SHIFTS = tuple(
    shift for dy in range(SPAN_Y) for shift in ((3, dy), (-3, -dy), (1, dy), (-1, -dy))
)
BATCHES = ((0, 8), (8, 14), (14, 16))
GATES = (6, 14)
GATE = 0
FIRST = 2
PASSED = 1
MEMBERS = SPACES // 2
TEAMS = [[z * SPAN_Y + y for z in range(p, SPAN_Z, 2) for y in range(SPAN_Y)] for p in range(2)]
LATE = 8
STAGE = 6
LONG = 10**12
SMEM = pl.BlockSpec(memory_space=pltpu.SMEM)
VMEM = pl.BlockSpec(memory_space=pltpu.VMEM)
ANYWHERE = pl.BlockSpec(memory_space=pl.ANY)
CREW = 4
NOTES = CAP * ROWS
LOAD = NOTES + 16


def space_shift(value, shift):
    return lax.ppermute(
        value,
        "space",
        [
            (z * SPAN_Y + y, (z + shift[0]) % SPAN_Z * SPAN_Y + (y + shift[1]) % SPAN_Y)
            for z in range(SPAN_Z)
            for y in range(SPAN_Y)
        ],
    )


def partner_of(me, shift):
    return (me // SPAN_Y + shift[0]) % SPAN_Z * SPAN_Y + (me % SPAN_Y + shift[1]) % SPAN_Y


def team_exchange(value):
    return lax.all_to_all(
        value, "space", split_axis=0, concat_axis=0, tiled=True, axis_index_groups=TEAMS
    )


def group_shift(value, steps):
    count = lax.axis_size("group")
    leading, last = (max(0, -steps), min(count, count - steps))
    return lax.ppermute(value, "group", [(source, source + steps) for source in range(leading, last)])


def project_and_pack(points, geom, w_value, w_kern, lists, x_local, team, dests):
    blocks = points.shape[0] // BLK
    cross = x_local.shape[0]
    tiles = lists[0].shape[0]
    count = len(SHIFTS)
    slots = SPACES * CAP
    step = 8

    def kernel(
        local_ref, dest_ref, block_ref, cut_ref, cross_ref, team_ref, dests_ref,
        points_ref, geom_ref, wv_ref, wk_ref, used_ref, own_ref, up_ref, team_out_ref, *rest
    ):
        out_refs, (held, notes, filled, partner, cuts, sems) = rest[:count], rest[count:]
        i = pl.program_id(0)

        @pl.when(i == 0)
        def _():
            @pl.loop(0, slots, unroll=8)
            def _(s):
                used_ref[s] = -1
                partner[s] = 0
                cuts[s] = 0

            @pl.loop(0, SPACES, unroll=8)
            def _(s):
                filled[s] = 0

            @pl.loop(0, tiles, unroll=4)
            def _(t):
                dest = dest_ref[t]
                slot = dest * CAP + filled[dest]
                filled[dest] = filled[dest] + 1
                used_ref[slot] = local_ref[t]
                partner[slot] = block_ref[t]
                cuts[slot] = cut_ref[t]

            row = lax.broadcasted_iota(jnp.int32, (16, C), 0)

            @pl.loop(0, SPACES, unroll=4)
            def _(d):
                note = jnp.zeros((16, C), jnp.int32)
                for j in range(CAP):
                    cut = cuts[d * CAP + j]
                    note = jnp.where(row == j, partner[d * CAP + j], note)
                    note = jnp.where(row == CAP + j, cut // 16, note)
                    note = jnp.where(row == 2 * CAP + j, cut % 16, note)
                notes[d] = note.astype(jnp.float32).astype(jnp.bfloat16)

        @pl.loop(0, step, unroll=4)
        def _(b):
            upper = pl.ds(pl.multiple_of(b * BLK, BLK), HALF)
            lower = pl.ds(pl.multiple_of(b * BLK + HALF, HALF), HALF)
            whole = pl.ds(pl.multiple_of(b * BLK, BLK), BLK)
            held[i * step + b, :BLK, :] = jnp.dot(
                points_ref[whole, :], wv_ref[...], preferred_element_type=jnp.float32
            ).astype(jnp.bfloat16)
            wide = jnp.concatenate([geom_ref[upper, :], geom_ref[lower, :]], axis=1)
            held[i * step + b, BLK:, :] = jnp.dot(
                wide, wk_ref[...], preferred_element_type=jnp.float32
            ).astype(jnp.bfloat16)

        @pl.when(i == pl.num_programs(0) - 1)
        def _():
            copies = []

            def leave(dest, out):
                for j in range(CAP):
                    block = jnp.maximum(used_ref[dest * CAP + j], 0)
                    copies.append((held.at[block], out.at[pl.ds(j * ROWS, ROWS)]))
                copies.append((notes.at[dest], out.at[pl.ds(NOTES, 16)]))

            for m in range(MEMBERS):
                leave(team_ref[m], team_out_ref.at[m])
            for k in range(count):
                leave(dests_ref[k], out_refs[k])
            for t in range(cross):
                copies.append((held.at[cross_ref[t]], up_ref.at[t]))
            copies.append((held, own_ref))
            started = [pltpu.make_async_copy(source, target, sems) for source, target in copies]
            for copy in started:
                copy.start()
            for copy in started:
                copy.wait()

    zero = jnp.zeros_like(w_kern)
    twice = jnp.concatenate(
        [jnp.concatenate([w_kern, zero], 1), jnp.concatenate([zero, w_kern], 1)], 0
    )
    results = pl.pallas_call(
        kernel,
        grid_spec=pltpu.PrefetchScalarGridSpec(
            num_scalar_prefetch=7,
            grid=(blocks // step,),
            in_specs=[
                pl.BlockSpec((step * BLK, C), lambda i, *_: (i, 0)),
                pl.BlockSpec((step * BLK, C), lambda i, *_: (i, 0)),
                pl.BlockSpec((C, C), lambda i, *_: (0, 0)),
                pl.BlockSpec((2 * C, 2 * K), lambda i, *_: (0, 0)),
            ],
            out_specs=(SMEM,) + (ANYWHERE,) * (3 + count),
            scratch_shapes=[
                pltpu.VMEM((blocks, ROWS, C), jnp.bfloat16),
                pltpu.VMEM((SPACES, 16, C), jnp.bfloat16),
                pltpu.SMEM((SPACES,), jnp.int32),
                pltpu.SMEM((slots,), jnp.int32),
                pltpu.SMEM((slots,), jnp.int32),
                pltpu.SemaphoreType.DMA,
            ],
        ),
        out_shape=(
            jax.ShapeDtypeStruct((slots,), jnp.int32),
            jax.ShapeDtypeStruct((blocks, ROWS, C), jnp.bfloat16),
            jax.ShapeDtypeStruct((cross, ROWS, C), jnp.bfloat16),
            jax.ShapeDtypeStruct((MEMBERS, LOAD, C), jnp.bfloat16),
        )
        + (jax.ShapeDtypeStruct((LOAD, C), jnp.bfloat16),) * count,
        compiler_params=pltpu.CompilerParams(vmem_limit_bytes=VMEM_LIMIT),
        name="project_and_pack",
    )(*lists, x_local, team, dests, points, geom, w_value, twice)
    return results[:4], results[4:]


def read_notes(load):
    note = load[pl.ds(NOTES, 16), :].astype(jnp.float32)
    entry = note[:CAP] * 512 + note[CAP : 2 * CAP] * 16 + note[2 * CAP : 3 * CAP]
    entries = [entry[j, 0].astype(jnp.int32) for j in range(CAP)]
    return [(value // 512, value % 512) for value in entries]


def unpack_kernels(packed):
    return jnp.concatenate([packed[:, :K], packed[:, K:]], axis=0)


def pair_terms(pairs):
    rows = lax.broadcasted_iota(jnp.int32, (BLK, BLK), 0)
    columns = lax.broadcasted_iota(jnp.int32, (BLK, BLK), 1)
    level = rows + columns
    scores = [
        lax.dot_general(
            unpack_kernels(a[BLK:, :]),
            unpack_kernels(b[BLK:, :]),
            (((1,), (1,)), ((), ())),
            preferred_element_type=jnp.float32,
        )
        for a, b, _ in pairs
    ]
    tiles = [
        jnp.where(level < cut, jnp.tanh(score * (1.0 / math.sqrt(K))), 0.0).astype(jnp.bfloat16)
        for score, (_, _, cut) in zip(scores, pairs)
    ]
    forward = [
        jnp.dot(tile, b[:BLK, :], preferred_element_type=jnp.float32) for tile, (_, b, _) in zip(tiles, pairs)
    ]
    backward = [
        lax.dot_general(tile, a[:BLK, :], (((0,), (0,)), ((), ())), preferred_element_type=jnp.float32)
        for tile, (a, _, _) in zip(tiles, pairs)
    ]
    return forward, backward


def pair_cost(number, blocks):
    return pl.CostEstimate(
        flops=2 * number * BLK * BLK * (K + 2 * C),
        bytes_accessed=number * (ROWS + BLK) * C * 2 + blocks * BLK * C * 8,
        transcendentals=number * BLK * BLK,
    )


def pairs_above(cross_meta, below, own, before):
    cross = below.shape[0]
    blocks = own.shape[0]
    some = math.gcd(cross, 4)

    def kernel(cross_ref, below_ref, own_ref, *rest):
        back_ref, total = rest[len(before) :]
        total[...] = jnp.zeros_like(total)

        @pl.loop(0, cross, step=some)
        def _(first):
            mine = [cross_ref[2 * (first + t)] for t in range(some)]
            forward, backward = pair_terms(
                [
                    (below_ref.at[first + t], own_ref.at[mine[t]], cross_ref[2 * (first + t) + 1])
                    for t in range(some)
                ]
            )
            for t in range(some):
                back_ref[first + t] = forward[t].astype(jnp.bfloat16)
            for t in range(some):
                total[mine[t]] = total[mine[t]] + backward[t]

    return pl.pallas_call(
        kernel,
        in_specs=[SMEM, VMEM, VMEM] + [ANYWHERE] * len(before),
        out_specs=(VMEM, VMEM),
        out_shape=(
            jax.ShapeDtypeStruct((cross, BLK, C), jnp.bfloat16),
            jax.ShapeDtypeStruct((blocks, BLK, C), jnp.float32),
        ),
        compiler_params=pltpu.CompilerParams(vmem_limit_bytes=VMEM_LIMIT),
        cost_estimate=pl.CostEstimate(flops=LONG, bytes_accessed=0, transcendentals=0),
        name="pairs_above",
    )(cross_meta, below, own, *before)


def team_pairs(arrived, own, aggregate, passing):
    blocks = own.shape[0]
    some = CREW * CAP
    handed = len(passing)

    def kernel(arrived_ref, own_ref, given_ref, *rest):
        back_ref, total_ref, total, sem = rest[handed], rest[handed + 1], rest[-2], rest[-1]
        i = pl.program_id(0)

        @pl.when(i == 0)
        def _():
            copy = pltpu.make_async_copy(given_ref, total, sem)
            copy.start()
            copy.wait()

        @pl.loop(0, CREW, step=STAGE // CAP)
        def _(first):
            places = []
            for m in range(STAGE // CAP):
                load = arrived_ref.at[first + m]
                for j, (block, cut) in enumerate(read_notes(load)):
                    places.append((load.at[pl.ds(j * ROWS, ROWS)], block, cut))
            forward, backward = pair_terms([(a, own_ref.at[block], cut) for a, block, cut in places])
            for n in range(STAGE):
                back_ref[first * CAP + n] = forward[n].astype(jnp.bfloat16)
            for n, (_, block, _) in enumerate(places):
                total[block] = total[block] + backward[n]

        @pl.when(i == pl.num_programs(0) - 1)
        def _():
            copy = pltpu.make_async_copy(total, total_ref, sem)
            copy.start()
            copy.wait()

    results = pl.pallas_call(
        kernel,
        grid=(MEMBERS // CREW,),
        in_specs=[
            pl.BlockSpec((CREW, LOAD, C), lambda i: (i, 0, 0)),
            pl.BlockSpec((blocks, ROWS, C), lambda i: (0, 0, 0)),
            ANYWHERE,
        ]
        + [ANYWHERE] * handed,
        out_specs=(pl.BlockSpec((some, BLK, C), lambda i: (i, 0, 0)), ANYWHERE) + (ANYWHERE,) * handed,
        scratch_shapes=[
            pltpu.VMEM((blocks, BLK, C), jnp.float32),
            pltpu.SemaphoreType.DMA,
        ],
        out_shape=(
            jax.ShapeDtypeStruct((MEMBERS * CAP, BLK, C), jnp.bfloat16),
            jax.ShapeDtypeStruct((blocks, BLK, C), jnp.float32),
        )
        + tuple(jax.ShapeDtypeStruct(array.shape, array.dtype) for array in passing),
        input_output_aliases={3 + n: 2 + n for n in range(handed)},
        compiler_params=pltpu.CompilerParams(vmem_limit_bytes=VMEM_LIMIT),
        cost_estimate=pair_cost(MEMBERS * CAP, blocks),
        name="team_pairs",
    )(arrived, own, aggregate, *passing)
    return results[0], results[1], results[2:]


def shifted_pairs(arrived, own, aggregate, passing, cost):
    count = len(arrived)
    blocks = own.shape[0]
    handed = len(passing)

    def kernel(own_ref, given_ref, *rest):
        arrived_refs, rest = rest[handed : handed + count], rest[handed + count :]
        back_refs, total, loads, backs = rest[:count], rest[count], rest[-2], rest[-1]
        total[...] = given_ref[...]
        for k in range(count):
            loads[k] = arrived_refs[k][...]

        @pl.loop(0, count, step=STAGE // CAP)
        def _(first):
            places = []
            for k in range(STAGE // CAP):
                load = loads.at[first + k]
                for j, (block, cut) in enumerate(read_notes(load)):
                    places.append((load.at[pl.ds(j * ROWS, ROWS)], block, cut))
            forward, backward = pair_terms([(a, own_ref.at[block], cut) for a, block, cut in places])
            for n in range(STAGE):
                backs[first + n // CAP, n % CAP] = forward[n].astype(jnp.bfloat16)
            for n, (_, block, _) in enumerate(places):
                total[block] = total[block] + backward[n]

        for k in range(count):
            back_refs[k][...] = backs[k]

    results = pl.pallas_call(
        kernel,
        in_specs=[VMEM] * 2 + [ANYWHERE] * handed + [VMEM] * count,
        out_specs=(VMEM,) * (count + 1) + (ANYWHERE,) * handed,
        out_shape=(jax.ShapeDtypeStruct((CAP, BLK, C), jnp.bfloat16),) * count
        + (jax.ShapeDtypeStruct((blocks, BLK, C), jnp.float32),)
        + tuple(jax.ShapeDtypeStruct(array.shape, array.dtype) for array in passing),
        input_output_aliases={1: count} | {2 + n: count + 1 + n for n in range(handed)},
        scratch_shapes=[
            pltpu.VMEM((count, LOAD, C), jnp.bfloat16),
            pltpu.VMEM((count, CAP, BLK, C), jnp.bfloat16),
        ],
        compiler_params=pltpu.CompilerParams(vmem_limit_bytes=VMEM_LIMIT),
        cost_estimate=cost,
        name="shifted_pairs",
    )(own, aggregate, *passing, *arrived)
    return results[:count], results[count], results[count + 1 :]


def add_back(used_ref, places_ref, back_refs, total):
    for k, back_ref in enumerate(back_refs):
        for j in range(CAP):
            mine = used_ref[places_ref[k] * CAP + j]

            @pl.when(mine >= 0)
            def _():
                total[mine] = total[mine] + back_ref[j].astype(jnp.float32)


def gather_team(used, team, x_local, returned, returned_x, aggregate, passing):
    cross = returned_x.shape[0]
    handed = len(passing)

    def kernel(used_ref, team_ref, cross_ref, given_ref, back_ref, back_x_ref, *rest):
        total = rest[handed]
        total[...] = given_ref[...]
        for t in range(cross):
            mine = cross_ref[t]
            total[mine] = total[mine] + back_x_ref[t].astype(jnp.float32)

        @pl.loop(0, MEMBERS)
        def _(m):
            for j in range(CAP):
                mine = used_ref[team_ref[m] * CAP + j]

                @pl.when(mine >= 0)
                def _():
                    total[mine] = total[mine] + back_ref[m * CAP + j].astype(jnp.float32)

    results = pl.pallas_call(
        kernel,
        in_specs=[SMEM] * 3 + [VMEM] * 3 + [ANYWHERE] * handed,
        out_specs=(VMEM,) + (ANYWHERE,) * handed,
        out_shape=(jax.ShapeDtypeStruct(aggregate.shape, jnp.float32),)
        + tuple(jax.ShapeDtypeStruct(array.shape, array.dtype) for array in passing),
        input_output_aliases={3: 0} | {6 + n: 1 + n for n in range(handed)},
        compiler_params=pltpu.CompilerParams(vmem_limit_bytes=VMEM_LIMIT),
        cost_estimate=pl.CostEstimate(
            flops=returned.size, bytes_accessed=returned.size * 2 + aggregate.size * 8, transcendentals=0
        ),
        name="gather_team",
    )(used, team, x_local, aggregate, returned, returned_x, *passing)
    return results[0], results[1:]


def gather_and_mix(used, dests, returned, aggregate, points, w_out, gain):
    count = len(returned)
    blocks = aggregate.shape[0]
    some = 8

    def kernel(used_ref, dests_ref, total_ref, points_ref, w_ref, gain_ref, *rest):
        back_refs, out_ref, total, sem = rest[:count], rest[count], rest[count + 1], rest[count + 2]
        i = pl.program_id(0)

        @pl.when(i == 0)
        def _():
            copy = pltpu.make_async_copy(total_ref, total, sem)
            copy.start()
            copy.wait()
            add_back(used_ref, dests_ref, back_refs, total)

        @pl.loop(0, some, unroll=2)
        def _(b):
            rows = pl.ds(pl.multiple_of(b * BLK, BLK), BLK)
            flat = total[i * some + b]
            meansq = jnp.mean(flat * flat, -1, keepdims=True)
            normed = flat * lax.rsqrt(meansq + 1e-06) * gain_ref[...]
            hidden = jax.nn.gelu(normed).astype(jnp.bfloat16)
            mixed = points_ref[rows, :].astype(jnp.float32) + jnp.dot(
                hidden, w_ref[...], preferred_element_type=jnp.float32
            )
            out_ref[rows, :] = mixed.astype(jnp.bfloat16)

    return pl.pallas_call(
        kernel,
        grid_spec=pltpu.PrefetchScalarGridSpec(
            num_scalar_prefetch=2,
            grid=(blocks // some,),
            in_specs=[
                pl.BlockSpec(memory_space=pl.ANY),
                pl.BlockSpec((some * BLK, C), lambda i, *_: (i, 0)),
                pl.BlockSpec((C, C), lambda i, *_: (0, 0)),
                pl.BlockSpec((1, C), lambda i, *_: (0, 0)),
            ]
            + [pl.BlockSpec((CAP, BLK, C), lambda i, *_: (0, 0, 0))] * count,
            out_specs=pl.BlockSpec((some * BLK, C), lambda i, *_: (i, 0)),
            scratch_shapes=[
                pltpu.VMEM((blocks, BLK, C), jnp.float32),
                pltpu.SemaphoreType.DMA,
            ],
        ),
        out_shape=jax.ShapeDtypeStruct((blocks * BLK, C), jnp.bfloat16),
        compiler_params=pltpu.CompilerParams(vmem_limit_bytes=VMEM_LIMIT),
        name="gather_and_mix",
    )(used, dests, aggregate, points, w_out, gain[None], *returned)


def body(feats, geom, w_value, w_kern, w_out, gain, t_local, t_dest, t_block, t_cut, x_local, x_block, x_cut):
    points = feats[0]
    me = lax.axis_index("space")
    dests = jnp.stack([partner_of(me, shift) for shift in SHIFTS]).astype(jnp.int32)
    member = jnp.arange(MEMBERS, dtype=jnp.int32)
    team = (member // SPAN_Y * 2 + me // SPAN_Y % 2) * SPAN_Y + member % SPAN_Y
    lists = (t_local[0], t_dest[0, :, 0], t_block[0], t_cut[0])
    (used, own, rising, leaving), shifting = project_and_pack(
        points, geom[0], w_value, w_kern, lists, x_local[0], team, dests
    )
    arrived = team_exchange(leaving)
    cross_meta = group_shift(jnp.stack([x_block[0], x_cut[0]], 1), 1).reshape(-1)
    below = group_shift(rising, 1)
    shifting = list(shifting)
    shifted = [None] * len(SHIFTS)

    def send(first, end):
        for k in range(first, end):
            shifted[k] = space_shift(shifting[k], SHIFTS[k])

    send(0, GATES[0])
    back_x, aggregate = pairs_above(cross_meta, below, own, shifted[:FIRST])
    returned_x = group_shift(back_x, -1)
    first, end = GATES
    back, aggregate, shifting[first:end] = team_pairs(arrived, own, aggregate, shifting[first:end])
    send(first, end)
    going_back = []
    for turn, (first, end) in enumerate(BATCHES):
        later = slice(GATES[1], len(SHIFTS)) if turn == GATE else slice(0, 0)
        passing = shifting[later] + ([back] if turn == PASSED else [])
        back_some, aggregate, passing = shifted_pairs(
            shifted[first:end], own, aggregate, passing,
            pl.CostEstimate(flops=LONG, bytes_accessed=0, transcendentals=0)
            if turn > PASSED
            else pair_cost((end - first) * CAP, own.shape[0]),
        )
        shifting[later] = passing[: later.stop - later.start]
        if turn == GATE:
            send(GATES[1], len(SHIFTS))
        if turn == PASSED:
            returned = team_exchange(passing[-1])
        going_back += back_some
    back_shifted = [None] * len(SHIFTS)

    def send_back(first, end):
        for k in range(first, end):
            dz, dy = SHIFTS[k]
            back_shifted[k] = space_shift(going_back[k], (-dz, -dy))

    send_back(0, LATE)
    aggregate, going_back[LATE:] = gather_team(
        used, team, x_local[0], returned, returned_x, aggregate, going_back[LATE:]
    )
    send_back(LATE, len(SHIFTS))
    mixed = gather_and_mix(used, dests, back_shifted, aggregate, points, w_out, gain)
    return mixed[None]


def solution(mesh):
    in_specs = (
        P("group", "space", None),
        P("group", "space", None),
        P(),
        P(),
        P(),
        P(),
        P("group", "space"),
        P("group", "space", None),
        P("group", "space"),
        P("group", "space"),
        P("group", "space"),
        P("group", "space"),
        P("group", "space"),
    )
    out_specs = P("group", "space", None)
    return jax.shard_map(body, mesh=mesh, in_specs=in_specs, out_specs=out_specs, check_vma=False)
```

```python
import math

import jax
import jax.numpy as jnp
from jax import lax
from jax.experimental import pallas as pl
from jax.experimental.pallas import tpu as pltpu
from jax.sharding import PartitionSpec as P

C = 128
K = 64
BLK = 256
HALF = BLK // 2
ROWS = BLK + HALF
CAP = 3
VMEM_LIMIT = 56 * 1024 * 1024
SPAN_Z, SPAN_Y = 8, 4
SPACES = SPAN_Z * SPAN_Y
SHIFTS = tuple(
    shift for dy in range(SPAN_Y) for shift in ((3, dy), (-3, -dy), (1, dy), (-1, -dy))
)
BATCHES = ((0, 8), (8, 14), (14, 16))
GATES = (6, 14)
GATE = 0
FIRST = 2
PASSED = 1
MEMBERS = SPACES // 2
TEAMS = [[z * SPAN_Y + y for z in range(p, SPAN_Z, 2) for y in range(SPAN_Y)] for p in range(2)]
LATE = 16
STAGE = 6
LONG = 10**12
SMEM = pl.BlockSpec(memory_space=pltpu.SMEM)
VMEM = pl.BlockSpec(memory_space=pltpu.VMEM)
ANYWHERE = pl.BlockSpec(memory_space=pl.ANY)
CREW = 4
NOTES = CAP * ROWS
LOAD = NOTES + 16


def space_shift(value, shift):
    return lax.ppermute(
        value,
        "space",
        [
            (z * SPAN_Y + y, (z + shift[0]) % SPAN_Z * SPAN_Y + (y + shift[1]) % SPAN_Y)
            for z in range(SPAN_Z)
            for y in range(SPAN_Y)
        ],
    )


def partner_of(me, shift):
    return (me // SPAN_Y + shift[0]) % SPAN_Z * SPAN_Y + (me % SPAN_Y + shift[1]) % SPAN_Y


def team_exchange(value):
    return lax.all_to_all(
        value, "space", split_axis=0, concat_axis=0, tiled=True, axis_index_groups=TEAMS
    )


def group_shift(value, steps):
    count = lax.axis_size("group")
    leading, last = (max(0, -steps), min(count, count - steps))
    return lax.ppermute(value, "group", [(source, source + steps) for source in range(leading, last)])


def project_and_pack(points, geom, w_value, w_kern, lists, x_local, team, dests):
    blocks = points.shape[0] // BLK
    cross = x_local.shape[0]
    tiles = lists[0].shape[0]
    count = len(SHIFTS)
    slots = SPACES * CAP
    step = 8

    def kernel(
        local_ref, dest_ref, block_ref, cut_ref, cross_ref, team_ref, dests_ref,
        points_ref, geom_ref, wv_ref, wk_ref, used_ref, own_ref, up_ref, team_out_ref, *rest
    ):
        out_refs, (held, notes, filled, partner, cuts, sems) = rest[:count], rest[count:]
        i = pl.program_id(0)

        @pl.when(i == 0)
        def _():
            @pl.loop(0, slots, unroll=8)
            def _(s):
                used_ref[s] = -1
                partner[s] = 0
                cuts[s] = 0

            @pl.loop(0, SPACES, unroll=8)
            def _(s):
                filled[s] = 0

            @pl.loop(0, tiles, unroll=4)
            def _(t):
                dest = dest_ref[t]
                slot = dest * CAP + filled[dest]
                filled[dest] = filled[dest] + 1
                used_ref[slot] = local_ref[t]
                partner[slot] = block_ref[t]
                cuts[slot] = cut_ref[t]

            row = lax.broadcasted_iota(jnp.int32, (16, C), 0)

            @pl.loop(0, SPACES, unroll=4)
            def _(d):
                note = jnp.zeros((16, C), jnp.int32)
                for j in range(CAP):
                    cut = cuts[d * CAP + j]
                    note = jnp.where(row == j, partner[d * CAP + j], note)
                    note = jnp.where(row == CAP + j, cut // 16, note)
                    note = jnp.where(row == 2 * CAP + j, cut % 16, note)
                notes[d] = note.astype(jnp.float32).astype(jnp.bfloat16)

        @pl.loop(0, step, unroll=8)
        def _(b):
            upper = pl.ds(pl.multiple_of(b * BLK, BLK), HALF)
            lower = pl.ds(pl.multiple_of(b * BLK + HALF, HALF), HALF)
            whole = pl.ds(pl.multiple_of(b * BLK, BLK), BLK)
            held[i * step + b, :BLK, :] = jnp.dot(
                points_ref[whole, :], wv_ref[...], preferred_element_type=jnp.float32
            ).astype(jnp.bfloat16)
            wide = jnp.concatenate([geom_ref[upper, :], geom_ref[lower, :]], axis=1)
            held[i * step + b, BLK:, :] = jnp.dot(
                wide, wk_ref[...], preferred_element_type=jnp.float32
            ).astype(jnp.bfloat16)

        @pl.when(i == pl.num_programs(0) - 1)
        def _():
            copies = []

            def leave(dest, out):
                for j in range(CAP):
                    block = jnp.maximum(used_ref[dest * CAP + j], 0)
                    copies.append((held.at[block], out.at[pl.ds(j * ROWS, ROWS)]))
                copies.append((notes.at[dest], out.at[pl.ds(NOTES, 16)]))

            for m in range(MEMBERS):
                leave(team_ref[m], team_out_ref.at[m])
            for k in range(count):
                leave(dests_ref[k], out_refs[k])
            for t in range(cross):
                copies.append((held.at[cross_ref[t]], up_ref.at[t]))
            copies.append((held, own_ref))
            started = [pltpu.make_async_copy(source, target, sems) for source, target in copies]
            for copy in started:
                copy.start()
            for copy in started:
                copy.wait()

    zero = jnp.zeros_like(w_kern)
    twice = jnp.concatenate(
        [jnp.concatenate([w_kern, zero], 1), jnp.concatenate([zero, w_kern], 1)], 0
    )
    results = pl.pallas_call(
        kernel,
        grid_spec=pltpu.PrefetchScalarGridSpec(
            num_scalar_prefetch=7,
            grid=(blocks // step,),
            in_specs=[
                pl.BlockSpec((step * BLK, C), lambda i, *_: (i, 0)),
                pl.BlockSpec((step * BLK, C), lambda i, *_: (i, 0)),
                pl.BlockSpec((C, C), lambda i, *_: (0, 0)),
                pl.BlockSpec((2 * C, 2 * K), lambda i, *_: (0, 0)),
            ],
            out_specs=(SMEM,) + (ANYWHERE,) * (3 + count),
            scratch_shapes=[
                pltpu.VMEM((blocks, ROWS, C), jnp.bfloat16),
                pltpu.VMEM((SPACES, 16, C), jnp.bfloat16),
                pltpu.SMEM((SPACES,), jnp.int32),
                pltpu.SMEM((slots,), jnp.int32),
                pltpu.SMEM((slots,), jnp.int32),
                pltpu.SemaphoreType.DMA,
            ],
        ),
        out_shape=(
            jax.ShapeDtypeStruct((slots,), jnp.int32),
            jax.ShapeDtypeStruct((blocks, ROWS, C), jnp.bfloat16),
            jax.ShapeDtypeStruct((cross, ROWS, C), jnp.bfloat16),
            jax.ShapeDtypeStruct((MEMBERS, LOAD, C), jnp.bfloat16),
        )
        + (jax.ShapeDtypeStruct((LOAD, C), jnp.bfloat16),) * count,
        compiler_params=pltpu.CompilerParams(vmem_limit_bytes=VMEM_LIMIT),
        name="project_and_pack",
    )(*lists, x_local, team, dests, points, geom, w_value, twice)
    return results[:4], results[4:]


def read_notes(load):
    note = load[pl.ds(NOTES, 16), :].astype(jnp.float32)
    entry = note[:CAP] * 512 + note[CAP : 2 * CAP] * 16 + note[2 * CAP : 3 * CAP]
    entries = [entry[j, 0].astype(jnp.int32) for j in range(CAP)]
    return [(value // 512, value % 512) for value in entries]


def unpack_kernels(packed):
    return jnp.concatenate([packed[:, :K], packed[:, K:]], axis=0)


def pair_terms(pairs):
    rows = lax.broadcasted_iota(jnp.int32, (BLK, BLK), 0)
    columns = lax.broadcasted_iota(jnp.int32, (BLK, BLK), 1)
    level = rows + columns
    scores = [
        lax.dot_general(
            unpack_kernels(a[BLK:, :]),
            unpack_kernels(b[BLK:, :]),
            (((1,), (1,)), ((), ())),
            preferred_element_type=jnp.float32,
        )
        for a, b, _ in pairs
    ]
    tiles = [
        jnp.where(level < cut, jnp.tanh(score * (1.0 / math.sqrt(K))), 0.0).astype(jnp.bfloat16)
        for score, (_, _, cut) in zip(scores, pairs)
    ]
    forward = [
        jnp.dot(tile, b[:BLK, :], preferred_element_type=jnp.float32) for tile, (_, b, _) in zip(tiles, pairs)
    ]
    backward = [
        lax.dot_general(tile, a[:BLK, :], (((0,), (0,)), ((), ())), preferred_element_type=jnp.float32)
        for tile, (a, _, _) in zip(tiles, pairs)
    ]
    return forward, backward


def pair_cost(number, blocks):
    return pl.CostEstimate(
        flops=2 * number * BLK * BLK * (K + 2 * C),
        bytes_accessed=number * (ROWS + BLK) * C * 2 + blocks * BLK * C * 8,
        transcendentals=number * BLK * BLK,
    )


def pairs_above(cross_meta, below, own, before):
    cross = below.shape[0]
    blocks = own.shape[0]
    some = math.gcd(cross, 4)

    def kernel(cross_ref, below_ref, own_ref, *rest):
        back_ref, total = rest[len(before) :]
        total[...] = jnp.zeros_like(total)

        @pl.loop(0, cross, step=some)
        def _(first):
            mine = [cross_ref[2 * (first + t)] for t in range(some)]
            forward, backward = pair_terms(
                [
                    (below_ref.at[first + t], own_ref.at[mine[t]], cross_ref[2 * (first + t) + 1])
                    for t in range(some)
                ]
            )
            for t in range(some):
                back_ref[first + t] = forward[t].astype(jnp.bfloat16)
            for t in range(some):
                total[mine[t]] = total[mine[t]] + backward[t]

    return pl.pallas_call(
        kernel,
        in_specs=[SMEM, VMEM, VMEM] + [ANYWHERE] * len(before),
        out_specs=(VMEM, VMEM),
        out_shape=(
            jax.ShapeDtypeStruct((cross, BLK, C), jnp.bfloat16),
            jax.ShapeDtypeStruct((blocks, BLK, C), jnp.float32),
        ),
        compiler_params=pltpu.CompilerParams(vmem_limit_bytes=VMEM_LIMIT),
        cost_estimate=pl.CostEstimate(flops=LONG, bytes_accessed=0, transcendentals=0),
        name="pairs_above",
    )(cross_meta, below, own, *before)


def team_pairs(arrived, own, aggregate, passing):
    blocks = own.shape[0]
    some = CREW * CAP
    handed = len(passing)

    def kernel(arrived_ref, own_ref, given_ref, *rest):
        back_ref, total_ref, total, sem = rest[handed], rest[handed + 1], rest[-2], rest[-1]
        i = pl.program_id(0)

        @pl.when(i == 0)
        def _():
            copy = pltpu.make_async_copy(given_ref, total, sem)
            copy.start()
            copy.wait()

        @pl.loop(0, CREW, step=STAGE // CAP)
        def _(first):
            places = []
            for m in range(STAGE // CAP):
                load = arrived_ref.at[first + m]
                for j, (block, cut) in enumerate(read_notes(load)):
                    places.append((load.at[pl.ds(j * ROWS, ROWS)], block, cut))
            forward, backward = pair_terms([(a, own_ref.at[block], cut) for a, block, cut in places])
            for n in range(STAGE):
                back_ref[first * CAP + n] = forward[n].astype(jnp.bfloat16)
            for n, (_, block, _) in enumerate(places):
                total[block] = total[block] + backward[n]

        @pl.when(i == pl.num_programs(0) - 1)
        def _():
            copy = pltpu.make_async_copy(total, total_ref, sem)
            copy.start()
            copy.wait()

    results = pl.pallas_call(
        kernel,
        grid=(MEMBERS // CREW,),
        in_specs=[
            pl.BlockSpec((CREW, LOAD, C), lambda i: (i, 0, 0)),
            pl.BlockSpec((blocks, ROWS, C), lambda i: (0, 0, 0)),
            ANYWHERE,
        ]
        + [ANYWHERE] * handed,
        out_specs=(pl.BlockSpec((some, BLK, C), lambda i: (i, 0, 0)), ANYWHERE) + (ANYWHERE,) * handed,
        scratch_shapes=[
            pltpu.VMEM((blocks, BLK, C), jnp.float32),
            pltpu.SemaphoreType.DMA,
        ],
        out_shape=(
            jax.ShapeDtypeStruct((MEMBERS * CAP, BLK, C), jnp.bfloat16),
            jax.ShapeDtypeStruct((blocks, BLK, C), jnp.float32),
        )
        + tuple(jax.ShapeDtypeStruct(array.shape, array.dtype) for array in passing),
        input_output_aliases={3 + n: 2 + n for n in range(handed)},
        compiler_params=pltpu.CompilerParams(vmem_limit_bytes=VMEM_LIMIT),
        cost_estimate=pair_cost(MEMBERS * CAP, blocks),
        name="team_pairs",
    )(arrived, own, aggregate, *passing)
    return results[0], results[1], results[2:]


def shifted_pairs(arrived, own, aggregate, passing, cost):
    count = len(arrived)
    blocks = own.shape[0]
    handed = len(passing)

    def kernel(own_ref, given_ref, *rest):
        arrived_refs, rest = rest[handed : handed + count], rest[handed + count :]
        back_refs, total, loads, backs = rest[:count], rest[count], rest[-2], rest[-1]
        total[...] = given_ref[...]
        for k in range(count):
            loads[k] = arrived_refs[k][...]

        @pl.loop(0, count, step=STAGE // CAP)
        def _(first):
            places = []
            for k in range(STAGE // CAP):
                load = loads.at[first + k]
                for j, (block, cut) in enumerate(read_notes(load)):
                    places.append((load.at[pl.ds(j * ROWS, ROWS)], block, cut))
            forward, backward = pair_terms([(a, own_ref.at[block], cut) for a, block, cut in places])
            for n in range(STAGE):
                backs[first + n // CAP, n % CAP] = forward[n].astype(jnp.bfloat16)
            for n, (_, block, _) in enumerate(places):
                total[block] = total[block] + backward[n]

        for k in range(count):
            back_refs[k][...] = backs[k]

    results = pl.pallas_call(
        kernel,
        in_specs=[VMEM] * 2 + [ANYWHERE] * handed + [VMEM] * count,
        out_specs=(VMEM,) * (count + 1) + (ANYWHERE,) * handed,
        out_shape=(jax.ShapeDtypeStruct((CAP, BLK, C), jnp.bfloat16),) * count
        + (jax.ShapeDtypeStruct((blocks, BLK, C), jnp.float32),)
        + tuple(jax.ShapeDtypeStruct(array.shape, array.dtype) for array in passing),
        input_output_aliases={1: count} | {2 + n: count + 1 + n for n in range(handed)},
        scratch_shapes=[
            pltpu.VMEM((count, LOAD, C), jnp.bfloat16),
            pltpu.VMEM((count, CAP, BLK, C), jnp.bfloat16),
        ],
        compiler_params=pltpu.CompilerParams(vmem_limit_bytes=VMEM_LIMIT),
        cost_estimate=cost,
        name="shifted_pairs",
    )(own, aggregate, *passing, *arrived)
    return results[:count], results[count], results[count + 1 :]


def add_back(used_ref, places_ref, back_refs, total):
    for k, back_ref in enumerate(back_refs):
        for j in range(CAP):
            mine = used_ref[places_ref[k] * CAP + j]

            @pl.when(mine >= 0)
            def _():
                total[mine] = total[mine] + back_ref[j].astype(jnp.float32)


def gather_team(used, team, x_local, returned, returned_x, aggregate, passing):
    cross = returned_x.shape[0]
    handed = len(passing)

    def kernel(used_ref, team_ref, cross_ref, given_ref, back_ref, back_x_ref, *rest):
        total = rest[handed]
        total[...] = given_ref[...]
        for t in range(cross):
            mine = cross_ref[t]
            total[mine] = total[mine] + back_x_ref[t].astype(jnp.float32)

        @pl.loop(0, MEMBERS)
        def _(m):
            for j in range(CAP):
                mine = used_ref[team_ref[m] * CAP + j]

                @pl.when(mine >= 0)
                def _():
                    total[mine] = total[mine] + back_ref[m * CAP + j].astype(jnp.float32)

    results = pl.pallas_call(
        kernel,
        in_specs=[SMEM] * 3 + [VMEM] * 3 + [ANYWHERE] * handed,
        out_specs=(VMEM,) + (ANYWHERE,) * handed,
        out_shape=(jax.ShapeDtypeStruct(aggregate.shape, jnp.float32),)
        + tuple(jax.ShapeDtypeStruct(array.shape, array.dtype) for array in passing),
        input_output_aliases={3: 0} | {6 + n: 1 + n for n in range(handed)},
        compiler_params=pltpu.CompilerParams(vmem_limit_bytes=VMEM_LIMIT),
        cost_estimate=pl.CostEstimate(
            flops=returned.size, bytes_accessed=returned.size * 2 + aggregate.size * 8, transcendentals=0
        ),
        name="gather_team",
    )(used, team, x_local, aggregate, returned, returned_x, *passing)
    return results[0], results[1:]


def gather_and_mix(used, dests, returned, aggregate, points, w_out, gain):
    count = len(returned)
    blocks = aggregate.shape[0]
    some = 8

    def kernel(used_ref, dests_ref, total_ref, points_ref, w_ref, gain_ref, *rest):
        back_refs, out_ref, total, sem = rest[:count], rest[count], rest[count + 1], rest[count + 2]
        i = pl.program_id(0)

        @pl.when(i == 0)
        def _():
            copy = pltpu.make_async_copy(total_ref, total, sem)
            copy.start()
            copy.wait()
            add_back(used_ref, dests_ref, back_refs, total)

        @pl.loop(0, some, unroll=8)
        def _(b):
            rows = pl.ds(pl.multiple_of(b * BLK, BLK), BLK)
            flat = total[i * some + b]
            meansq = jnp.mean(flat * flat, -1, keepdims=True)
            normed = flat * lax.rsqrt(meansq + 1e-06) * gain_ref[...]
            hidden = jax.nn.gelu(normed).astype(jnp.bfloat16)
            mixed = points_ref[rows, :].astype(jnp.float32) + jnp.dot(
                hidden, w_ref[...], preferred_element_type=jnp.float32
            )
            out_ref[rows, :] = mixed.astype(jnp.bfloat16)

    return pl.pallas_call(
        kernel,
        grid_spec=pltpu.PrefetchScalarGridSpec(
            num_scalar_prefetch=2,
            grid=(blocks // some,),
            in_specs=[
                pl.BlockSpec(memory_space=pl.ANY),
                pl.BlockSpec((some * BLK, C), lambda i, *_: (i, 0)),
                pl.BlockSpec((C, C), lambda i, *_: (0, 0)),
                pl.BlockSpec((1, C), lambda i, *_: (0, 0)),
            ]
            + [pl.BlockSpec((CAP, BLK, C), lambda i, *_: (0, 0, 0))] * count,
            out_specs=pl.BlockSpec((some * BLK, C), lambda i, *_: (i, 0)),
            scratch_shapes=[
                pltpu.VMEM((blocks, BLK, C), jnp.float32),
                pltpu.SemaphoreType.DMA,
            ],
        ),
        out_shape=jax.ShapeDtypeStruct((blocks * BLK, C), jnp.bfloat16),
        compiler_params=pltpu.CompilerParams(vmem_limit_bytes=VMEM_LIMIT),
        name="gather_and_mix",
    )(used, dests, aggregate, points, w_out, gain[None], *returned)


def body(feats, geom, w_value, w_kern, w_out, gain, t_local, t_dest, t_block, t_cut, x_local, x_block, x_cut):
    points = feats[0]
    me = lax.axis_index("space")
    dests = jnp.stack([partner_of(me, shift) for shift in SHIFTS]).astype(jnp.int32)
    member = jnp.arange(MEMBERS, dtype=jnp.int32)
    team = (member // SPAN_Y * 2 + me // SPAN_Y % 2) * SPAN_Y + member % SPAN_Y
    lists = (t_local[0], t_dest[0, :, 0], t_block[0], t_cut[0])
    (used, own, rising, leaving), shifting = project_and_pack(
        points, geom[0], w_value, w_kern, lists, x_local[0], team, dests
    )
    arrived = team_exchange(leaving)
    cross_meta = group_shift(jnp.stack([x_block[0], x_cut[0]], 1), 1).reshape(-1)
    below = group_shift(rising, 1)
    shifting = list(shifting)
    shifted = [None] * len(SHIFTS)

    def send(first, end):
        for k in range(first, end):
            shifted[k] = space_shift(shifting[k], SHIFTS[k])

    send(0, GATES[0])
    back_x, aggregate = pairs_above(cross_meta, below, own, shifted[:FIRST])
    returned_x = group_shift(back_x, -1)
    first, end = GATES
    back, aggregate, shifting[first:end] = team_pairs(arrived, own, aggregate, shifting[first:end])
    send(first, end)
    going_back = []
    for turn, (first, end) in enumerate(BATCHES):
        later = slice(GATES[1], len(SHIFTS)) if turn == GATE else slice(0, 0)
        passing = shifting[later] + ([back] if turn == PASSED else [])
        back_some, aggregate, passing = shifted_pairs(
            shifted[first:end], own, aggregate, passing,
            pl.CostEstimate(flops=LONG, bytes_accessed=0, transcendentals=0)
            if turn > PASSED
            else pair_cost((end - first) * CAP, own.shape[0]),
        )
        shifting[later] = passing[: later.stop - later.start]
        if turn == GATE:
            send(GATES[1], len(SHIFTS))
        if turn == PASSED:
            returned = team_exchange(passing[-1])
        going_back += back_some
    back_shifted = [None] * len(SHIFTS)

    def send_back(first, end):
        for k in range(first, end):
            dz, dy = SHIFTS[k]
            back_shifted[k] = space_shift(going_back[k], (-dz, -dy))

    send_back(0, LATE)
    aggregate, going_back[LATE:] = gather_team(
        used, team, x_local[0], returned, returned_x, aggregate, going_back[LATE:]
    )
    send_back(LATE, len(SHIFTS))
    mixed = gather_and_mix(used, dests, back_shifted, aggregate, points, w_out, gain)
    return mixed[None]


def solution(mesh):
    in_specs = (
        P("group", "space", None),
        P("group", "space", None),
        P(),
        P(),
        P(),
        P(),
        P("group", "space"),
        P("group", "space", None),
        P("group", "space"),
        P("group", "space"),
        P("group", "space"),
        P("group", "space"),
        P("group", "space"),
    )
    out_specs = P("group", "space", None)
    return jax.shard_map(body, mesh=mesh, in_specs=in_specs, out_specs=out_specs, check_vma=False)
```

```python
import math

import jax
import jax.numpy as jnp
from jax import lax
from jax.experimental import pallas as pl
from jax.experimental.pallas import tpu as pltpu
from jax.sharding import PartitionSpec as P

C = 128
K = 64
BLK = 256
HALF = BLK // 2
ROWS = BLK + HALF
CAP = 3
VMEM_LIMIT = 56 * 1024 * 1024
SPAN_Z, SPAN_Y = 8, 4
SPACES = SPAN_Z * SPAN_Y
SHIFTS = tuple(
    shift for dy in range(SPAN_Y) for shift in ((3, dy), (-3, -dy), (1, dy), (-1, -dy))
)
BATCHES = ((0, 8), (8, 14), (14, 16))
GATES = (4, 14)
GATE = 0
PASSED = 1
MEMBERS = SPACES // 2
TEAMS = [[z * SPAN_Y + y for z in range(p, SPAN_Z, 2) for y in range(SPAN_Y)] for p in range(2)]
LATE = 8
STAGE = 6
LONG = 10**12
SMEM = pl.BlockSpec(memory_space=pltpu.SMEM)
VMEM = pl.BlockSpec(memory_space=pltpu.VMEM)
ANYWHERE = pl.BlockSpec(memory_space=pl.ANY)
CREW = 4
NOTES = CAP * ROWS
LOAD = NOTES + 16


def space_shift(value, shift):
    return lax.ppermute(
        value,
        "space",
        [
            (z * SPAN_Y + y, (z + shift[0]) % SPAN_Z * SPAN_Y + (y + shift[1]) % SPAN_Y)
            for z in range(SPAN_Z)
            for y in range(SPAN_Y)
        ],
    )


def partner_of(me, shift):
    return (me // SPAN_Y + shift[0]) % SPAN_Z * SPAN_Y + (me % SPAN_Y + shift[1]) % SPAN_Y


def team_exchange(value):
    return lax.all_to_all(
        value, "space", split_axis=0, concat_axis=0, tiled=True, axis_index_groups=TEAMS
    )


def group_shift(value, steps):
    count = lax.axis_size("group")
    leading, last = (max(0, -steps), min(count, count - steps))
    return lax.ppermute(value, "group", [(source, source + steps) for source in range(leading, last)])


def project_and_pack(points, geom, w_value, w_kern, lists, x_local, team, dests):
    blocks = points.shape[0] // BLK
    cross = x_local.shape[0]
    tiles = lists[0].shape[0]
    count = len(SHIFTS)
    slots = SPACES * CAP
    step = 8

    def kernel(
        local_ref, dest_ref, block_ref, cut_ref, cross_ref, team_ref, dests_ref,
        points_ref, geom_ref, wv_ref, wk_ref, used_ref, own_ref, up_ref, team_out_ref, *rest
    ):
        out_refs, (held, notes, filled, partner, cuts, sems) = rest[:count], rest[count:]
        i = pl.program_id(0)

        @pl.when(i == 0)
        def _():
            @pl.loop(0, slots, unroll=8)
            def _(s):
                used_ref[s] = -1
                partner[s] = 0
                cuts[s] = 0

            @pl.loop(0, SPACES, unroll=8)
            def _(s):
                filled[s] = 0

            @pl.loop(0, tiles, unroll=4)
            def _(t):
                dest = dest_ref[t]
                slot = dest * CAP + filled[dest]
                filled[dest] = filled[dest] + 1
                used_ref[slot] = local_ref[t]
                partner[slot] = block_ref[t]
                cuts[slot] = cut_ref[t]

            row = lax.broadcasted_iota(jnp.int32, (16, C), 0)

            @pl.loop(0, SPACES, unroll=4)
            def _(d):
                note = jnp.zeros((16, C), jnp.int32)
                for j in range(CAP):
                    cut = cuts[d * CAP + j]
                    note = jnp.where(row == j, partner[d * CAP + j], note)
                    note = jnp.where(row == CAP + j, cut // 16, note)
                    note = jnp.where(row == 2 * CAP + j, cut % 16, note)
                notes[d] = note.astype(jnp.float32).astype(jnp.bfloat16)

        @pl.loop(0, step, unroll=8)
        def _(b):
            upper = pl.ds(pl.multiple_of(b * BLK, BLK), HALF)
            lower = pl.ds(pl.multiple_of(b * BLK + HALF, HALF), HALF)
            whole = pl.ds(pl.multiple_of(b * BLK, BLK), BLK)
            held[i * step + b, :BLK, :] = jnp.dot(
                points_ref[whole, :], wv_ref[...], preferred_element_type=jnp.float32
            ).astype(jnp.bfloat16)
            wide = jnp.concatenate([geom_ref[upper, :], geom_ref[lower, :]], axis=1)
            held[i * step + b, BLK:, :] = jnp.dot(
                wide, wk_ref[...], preferred_element_type=jnp.float32
            ).astype(jnp.bfloat16)

        @pl.when(i == pl.num_programs(0) - 1)
        def _():
            copies = []

            def leave(dest, out):
                for j in range(CAP):
                    block = jnp.maximum(used_ref[dest * CAP + j], 0)
                    copies.append((held.at[block], out.at[pl.ds(j * ROWS, ROWS)]))
                copies.append((notes.at[dest], out.at[pl.ds(NOTES, 16)]))

            for m in range(MEMBERS):
                leave(team_ref[m], team_out_ref.at[m])
            for k in range(count):
                leave(dests_ref[k], out_refs[k])
            for t in range(cross):
                copies.append((held.at[cross_ref[t]], up_ref.at[t]))
            copies.append((held, own_ref))
            started = [pltpu.make_async_copy(source, target, sems) for source, target in copies]
            for copy in started:
                copy.start()
            for copy in started:
                copy.wait()

    zero = jnp.zeros_like(w_kern)
    twice = jnp.concatenate(
        [jnp.concatenate([w_kern, zero], 1), jnp.concatenate([zero, w_kern], 1)], 0
    )
    results = pl.pallas_call(
        kernel,
        grid_spec=pltpu.PrefetchScalarGridSpec(
            num_scalar_prefetch=7,
            grid=(blocks // step,),
            in_specs=[
                pl.BlockSpec((step * BLK, C), lambda i, *_: (i, 0)),
                pl.BlockSpec((step * BLK, C), lambda i, *_: (i, 0)),
                pl.BlockSpec((C, C), lambda i, *_: (0, 0)),
                pl.BlockSpec((2 * C, 2 * K), lambda i, *_: (0, 0)),
            ],
            out_specs=(SMEM,) + (ANYWHERE,) * (3 + count),
            scratch_shapes=[
                pltpu.VMEM((blocks, ROWS, C), jnp.bfloat16),
                pltpu.VMEM((SPACES, 16, C), jnp.bfloat16),
                pltpu.SMEM((SPACES,), jnp.int32),
                pltpu.SMEM((slots,), jnp.int32),
                pltpu.SMEM((slots,), jnp.int32),
                pltpu.SemaphoreType.DMA,
            ],
        ),
        out_shape=(
            jax.ShapeDtypeStruct((slots,), jnp.int32),
            jax.ShapeDtypeStruct((blocks, ROWS, C), jnp.bfloat16),
            jax.ShapeDtypeStruct((cross, ROWS, C), jnp.bfloat16),
            jax.ShapeDtypeStruct((MEMBERS, LOAD, C), jnp.bfloat16),
        )
        + (jax.ShapeDtypeStruct((LOAD, C), jnp.bfloat16),) * count,
        compiler_params=pltpu.CompilerParams(vmem_limit_bytes=VMEM_LIMIT),
        name="project_and_pack",
    )(*lists, x_local, team, dests, points, geom, w_value, twice)
    return results[:4], results[4:]


def read_notes(load):
    note = load[pl.ds(NOTES, 16), :].astype(jnp.float32)
    entry = note[:CAP] * 512 + note[CAP : 2 * CAP] * 16 + note[2 * CAP : 3 * CAP]
    entries = [entry[j, 0].astype(jnp.int32) for j in range(CAP)]
    return [(value // 512, value % 512) for value in entries]


def unpack_kernels(packed):
    return jnp.concatenate([packed[:, :K], packed[:, K:]], axis=0)


def pair_terms(pairs):
    rows = lax.broadcasted_iota(jnp.int32, (BLK, BLK), 0)
    columns = lax.broadcasted_iota(jnp.int32, (BLK, BLK), 1)
    level = rows + columns
    scores = [
        lax.dot_general(
            unpack_kernels(a[BLK:, :]),
            unpack_kernels(b[BLK:, :]),
            (((1,), (1,)), ((), ())),
            preferred_element_type=jnp.float32,
        )
        for a, b, _ in pairs
    ]
    tiles = [
        jnp.where(level < cut, jnp.tanh(score * (1.0 / math.sqrt(K))), 0.0).astype(jnp.bfloat16)
        for score, (_, _, cut) in zip(scores, pairs)
    ]
    forward = [
        jnp.dot(tile, b[:BLK, :], preferred_element_type=jnp.float32) for tile, (_, b, _) in zip(tiles, pairs)
    ]
    backward = [
        lax.dot_general(tile, a[:BLK, :], (((0,), (0,)), ((), ())), preferred_element_type=jnp.float32)
        for tile, (a, _, _) in zip(tiles, pairs)
    ]
    return forward, backward


def pair_cost(number, blocks):
    return pl.CostEstimate(
        flops=2 * number * BLK * BLK * (K + 2 * C),
        bytes_accessed=number * (ROWS + BLK) * C * 2 + blocks * BLK * C * 8,
        transcendentals=number * BLK * BLK,
    )


def pairs_above(cross_meta, below, own):
    cross = below.shape[0]
    blocks = own.shape[0]
    some = math.gcd(cross, 4)

    def kernel(cross_ref, below_ref, own_ref, back_ref, total):
        total[...] = jnp.zeros_like(total)

        @pl.loop(0, cross, step=some)
        def _(first):
            mine = [cross_ref[2 * (first + t)] for t in range(some)]
            forward, backward = pair_terms(
                [
                    (below_ref.at[first + t], own_ref.at[mine[t]], cross_ref[2 * (first + t) + 1])
                    for t in range(some)
                ]
            )
            for t in range(some):
                back_ref[first + t] = forward[t].astype(jnp.bfloat16)
            for t in range(some):
                total[mine[t]] = total[mine[t]] + backward[t]

    return pl.pallas_call(
        kernel,
        in_specs=[SMEM, VMEM, VMEM],
        out_specs=(VMEM, VMEM),
        out_shape=(
            jax.ShapeDtypeStruct((cross, BLK, C), jnp.bfloat16),
            jax.ShapeDtypeStruct((blocks, BLK, C), jnp.float32),
        ),
        compiler_params=pltpu.CompilerParams(vmem_limit_bytes=VMEM_LIMIT),
        cost_estimate=pl.CostEstimate(flops=LONG, bytes_accessed=0, transcendentals=0),
        name="pairs_above",
    )(cross_meta, below, own)


def team_pairs(arrived, own, aggregate, passing):
    blocks = own.shape[0]
    some = CREW * CAP
    handed = len(passing)

    def kernel(arrived_ref, own_ref, given_ref, *rest):
        back_ref, total_ref, total, sem = rest[handed], rest[handed + 1], rest[-2], rest[-1]
        i = pl.program_id(0)

        @pl.when(i == 0)
        def _():
            copy = pltpu.make_async_copy(given_ref, total, sem)
            copy.start()
            copy.wait()

        @pl.loop(0, CREW, step=STAGE // CAP)
        def _(first):
            places = []
            for m in range(STAGE // CAP):
                load = arrived_ref.at[first + m]
                for j, (block, cut) in enumerate(read_notes(load)):
                    places.append((load.at[pl.ds(j * ROWS, ROWS)], block, cut))
            forward, backward = pair_terms([(a, own_ref.at[block], cut) for a, block, cut in places])
            for n in range(STAGE):
                back_ref[first * CAP + n] = forward[n].astype(jnp.bfloat16)
            for n, (_, block, _) in enumerate(places):
                total[block] = total[block] + backward[n]

        @pl.when(i == pl.num_programs(0) - 1)
        def _():
            copy = pltpu.make_async_copy(total, total_ref, sem)
            copy.start()
            copy.wait()

    results = pl.pallas_call(
        kernel,
        grid=(MEMBERS // CREW,),
        in_specs=[
            pl.BlockSpec((CREW, LOAD, C), lambda i: (i, 0, 0)),
            pl.BlockSpec((blocks, ROWS, C), lambda i: (0, 0, 0)),
            ANYWHERE,
        ]
        + [ANYWHERE] * handed,
        out_specs=(pl.BlockSpec((some, BLK, C), lambda i: (i, 0, 0)), ANYWHERE) + (ANYWHERE,) * handed,
        scratch_shapes=[
            pltpu.VMEM((blocks, BLK, C), jnp.float32),
            pltpu.SemaphoreType.DMA,
        ],
        out_shape=(
            jax.ShapeDtypeStruct((MEMBERS * CAP, BLK, C), jnp.bfloat16),
            jax.ShapeDtypeStruct((blocks, BLK, C), jnp.float32),
        )
        + tuple(jax.ShapeDtypeStruct(array.shape, array.dtype) for array in passing),
        input_output_aliases={3 + n: 2 + n for n in range(handed)},
        compiler_params=pltpu.CompilerParams(vmem_limit_bytes=VMEM_LIMIT),
        cost_estimate=pair_cost(MEMBERS * CAP, blocks),
        name="team_pairs",
    )(arrived, own, aggregate, *passing)
    return results[0], results[1], results[2:]


def shifted_pairs(arrived, own, aggregate, passing, cost):
    count = len(arrived)
    blocks = own.shape[0]
    handed = len(passing)

    def kernel(own_ref, given_ref, *rest):
        arrived_refs, rest = rest[handed : handed + count], rest[handed + count :]
        back_refs, total, loads, backs = rest[:count], rest[count], rest[-2], rest[-1]
        total[...] = given_ref[...]
        for k in range(count):
            loads[k] = arrived_refs[k][...]

        @pl.loop(0, count, step=STAGE // CAP)
        def _(first):
            places = []
            for k in range(STAGE // CAP):
                load = loads.at[first + k]
                for j, (block, cut) in enumerate(read_notes(load)):
                    places.append((load.at[pl.ds(j * ROWS, ROWS)], block, cut))
            forward, backward = pair_terms([(a, own_ref.at[block], cut) for a, block, cut in places])
            for n in range(STAGE):
                backs[first + n // CAP, n % CAP] = forward[n].astype(jnp.bfloat16)
            for n, (_, block, _) in enumerate(places):
                total[block] = total[block] + backward[n]

        for k in range(count):
            back_refs[k][...] = backs[k]

    results = pl.pallas_call(
        kernel,
        in_specs=[VMEM] * 2 + [ANYWHERE] * handed + [VMEM] * count,
        out_specs=(VMEM,) * (count + 1) + (ANYWHERE,) * handed,
        out_shape=(jax.ShapeDtypeStruct((CAP, BLK, C), jnp.bfloat16),) * count
        + (jax.ShapeDtypeStruct((blocks, BLK, C), jnp.float32),)
        + tuple(jax.ShapeDtypeStruct(array.shape, array.dtype) for array in passing),
        input_output_aliases={1: count} | {2 + n: count + 1 + n for n in range(handed)},
        scratch_shapes=[
            pltpu.VMEM((count, LOAD, C), jnp.bfloat16),
            pltpu.VMEM((count, CAP, BLK, C), jnp.bfloat16),
        ],
        compiler_params=pltpu.CompilerParams(vmem_limit_bytes=VMEM_LIMIT),
        cost_estimate=cost,
        name="shifted_pairs",
    )(own, aggregate, *passing, *arrived)
    return results[:count], results[count], results[count + 1 :]


def add_back(used_ref, places_ref, back_refs, total):
    for k, back_ref in enumerate(back_refs):
        for j in range(CAP):
            mine = used_ref[places_ref[k] * CAP + j]

            @pl.when(mine >= 0)
            def _():
                total[mine] = total[mine] + back_ref[j].astype(jnp.float32)


def gather_team(used, team, x_local, returned, returned_x, aggregate, passing):
    cross = returned_x.shape[0]
    handed = len(passing)

    def kernel(used_ref, team_ref, cross_ref, given_ref, back_ref, back_x_ref, *rest):
        total = rest[handed]
        total[...] = given_ref[...]
        for t in range(cross):
            mine = cross_ref[t]
            total[mine] = total[mine] + back_x_ref[t].astype(jnp.float32)

        @pl.loop(0, MEMBERS)
        def _(m):
            for j in range(CAP):
                mine = used_ref[team_ref[m] * CAP + j]

                @pl.when(mine >= 0)
                def _():
                    total[mine] = total[mine] + back_ref[m * CAP + j].astype(jnp.float32)

    results = pl.pallas_call(
        kernel,
        in_specs=[SMEM] * 3 + [VMEM] * 3 + [ANYWHERE] * handed,
        out_specs=(VMEM,) + (ANYWHERE,) * handed,
        out_shape=(jax.ShapeDtypeStruct(aggregate.shape, jnp.float32),)
        + tuple(jax.ShapeDtypeStruct(array.shape, array.dtype) for array in passing),
        input_output_aliases={3: 0} | {6 + n: 1 + n for n in range(handed)},
        compiler_params=pltpu.CompilerParams(vmem_limit_bytes=VMEM_LIMIT),
        cost_estimate=pl.CostEstimate(
            flops=returned.size, bytes_accessed=returned.size * 2 + aggregate.size * 8, transcendentals=0
        ),
        name="gather_team",
    )(used, team, x_local, aggregate, returned, returned_x, *passing)
    return results[0], results[1:]


def gather_and_mix(used, dests, returned, aggregate, points, w_out, gain):
    count = len(returned)
    blocks = aggregate.shape[0]
    some = 8

    def kernel(used_ref, dests_ref, total_ref, points_ref, w_ref, gain_ref, *rest):
        back_refs, out_ref, total, sem = rest[:count], rest[count], rest[count + 1], rest[count + 2]
        i = pl.program_id(0)

        @pl.when(i == 0)
        def _():
            copy = pltpu.make_async_copy(total_ref, total, sem)
            copy.start()
            copy.wait()
            add_back(used_ref, dests_ref, back_refs, total)

        @pl.loop(0, some, unroll=8)
        def _(b):
            rows = pl.ds(pl.multiple_of(b * BLK, BLK), BLK)
            flat = total[i * some + b]
            meansq = jnp.mean(flat * flat, -1, keepdims=True)
            normed = flat * lax.rsqrt(meansq + 1e-06) * gain_ref[...]
            hidden = jax.nn.gelu(normed).astype(jnp.bfloat16)
            mixed = points_ref[rows, :].astype(jnp.float32) + jnp.dot(
                hidden, w_ref[...], preferred_element_type=jnp.float32
            )
            out_ref[rows, :] = mixed.astype(jnp.bfloat16)

    return pl.pallas_call(
        kernel,
        grid_spec=pltpu.PrefetchScalarGridSpec(
            num_scalar_prefetch=2,
            grid=(blocks // some,),
            in_specs=[
                pl.BlockSpec(memory_space=pl.ANY),
                pl.BlockSpec((some * BLK, C), lambda i, *_: (i, 0)),
                pl.BlockSpec((C, C), lambda i, *_: (0, 0)),
                pl.BlockSpec((1, C), lambda i, *_: (0, 0)),
            ]
            + [pl.BlockSpec((CAP, BLK, C), lambda i, *_: (0, 0, 0))] * count,
            out_specs=pl.BlockSpec((some * BLK, C), lambda i, *_: (i, 0)),
            scratch_shapes=[
                pltpu.VMEM((blocks, BLK, C), jnp.float32),
                pltpu.SemaphoreType.DMA,
            ],
        ),
        out_shape=jax.ShapeDtypeStruct((blocks * BLK, C), jnp.bfloat16),
        compiler_params=pltpu.CompilerParams(vmem_limit_bytes=VMEM_LIMIT),
        name="gather_and_mix",
    )(used, dests, aggregate, points, w_out, gain[None], *returned)


def body(feats, geom, w_value, w_kern, w_out, gain, t_local, t_dest, t_block, t_cut, x_local, x_block, x_cut):
    points = feats[0]
    me = lax.axis_index("space")
    dests = jnp.stack([partner_of(me, shift) for shift in SHIFTS]).astype(jnp.int32)
    member = jnp.arange(MEMBERS, dtype=jnp.int32)
    team = (member // SPAN_Y * 2 + me // SPAN_Y % 2) * SPAN_Y + member % SPAN_Y
    lists = (t_local[0], t_dest[0, :, 0], t_block[0], t_cut[0])
    (used, own, rising, leaving), shifting = project_and_pack(
        points, geom[0], w_value, w_kern, lists, x_local[0], team, dests
    )
    arrived = team_exchange(leaving)
    cross_meta = group_shift(jnp.stack([x_block[0], x_cut[0]], 1), 1).reshape(-1)
    below = group_shift(rising, 1)
    shifting = list(shifting)
    shifted = [None] * len(SHIFTS)

    def send(first, end):
        for k in range(first, end):
            shifted[k] = space_shift(shifting[k], SHIFTS[k])

    back_x, aggregate = pairs_above(cross_meta, below, own)
    returned_x = group_shift(back_x, -1)
    send(0, GATES[0])
    first, end = GATES
    back, aggregate, shifting[first:end] = team_pairs(arrived, own, aggregate, shifting[first:end])
    send(first, end)
    going_back = []
    for turn, (first, end) in enumerate(BATCHES):
        later = slice(GATES[1], len(SHIFTS)) if turn == GATE else slice(0, 0)
        passing = shifting[later] + ([back] if turn == PASSED else [])
        back_some, aggregate, passing = shifted_pairs(
            shifted[first:end], own, aggregate, passing,
            pl.CostEstimate(flops=LONG, bytes_accessed=0, transcendentals=0)
            if turn > PASSED
            else pair_cost((end - first) * CAP, own.shape[0]),
        )
        shifting[later] = passing[: later.stop - later.start]
        if turn == GATE:
            send(GATES[1], len(SHIFTS))
        if turn == PASSED:
            returned = team_exchange(passing[-1])
        going_back += back_some
    back_shifted = [None] * len(SHIFTS)

    def send_back(first, end):
        for k in range(first, end):
            dz, dy = SHIFTS[k]
            back_shifted[k] = space_shift(going_back[k], (-dz, -dy))

    send_back(0, LATE)
    aggregate, going_back[LATE:] = gather_team(
        used, team, x_local[0], returned, returned_x, aggregate, going_back[LATE:]
    )
    send_back(LATE, len(SHIFTS))
    mixed = gather_and_mix(used, dests, back_shifted, aggregate, points, w_out, gain)
    return mixed[None]


def solution(mesh):
    in_specs = (
        P("group", "space", None),
        P("group", "space", None),
        P(),
        P(),
        P(),
        P(),
        P("group", "space"),
        P("group", "space", None),
        P("group", "space"),
        P("group", "space"),
        P("group", "space"),
        P("group", "space"),
        P("group", "space"),
    )
    out_specs = P("group", "space", None)
    return jax.shard_map(body, mesh=mesh, in_specs=in_specs, out_specs=out_specs, check_vma=False)
```

```python
import math

import jax
import jax.numpy as jnp
from jax import lax
from jax.experimental import pallas as pl
from jax.experimental.pallas import tpu as pltpu
from jax.sharding import PartitionSpec as P

C = 128
K = 64
BLK = 256
HALF = BLK // 2
ROWS = BLK + HALF
CAP = 3
VMEM_LIMIT = 56 * 1024 * 1024
SPAN_Z, SPAN_Y = 8, 4
SPACES = SPAN_Z * SPAN_Y
SHIFTS = tuple(
    shift for dy in range(SPAN_Y) for shift in ((3, dy), (-3, -dy), (1, dy), (-1, -dy))
)
BATCHES = ((0, 8), (8, 14), (14, 16))
GATES = (4, 14)
GATE = 0
PASSED = 1
MEMBERS = SPACES // 2
TEAMS = [[z * SPAN_Y + y for z in range(p, SPAN_Z, 2) for y in range(SPAN_Y)] for p in range(2)]
LATE = 12
STAGE = 6
LONG = 10**12
SMEM = pl.BlockSpec(memory_space=pltpu.SMEM)
VMEM = pl.BlockSpec(memory_space=pltpu.VMEM)
ANYWHERE = pl.BlockSpec(memory_space=pl.ANY)
CREW = 4
NOTES = CAP * ROWS
LOAD = NOTES + 16


def space_shift(value, shift):
    return lax.ppermute(
        value,
        "space",
        [
            (z * SPAN_Y + y, (z + shift[0]) % SPAN_Z * SPAN_Y + (y + shift[1]) % SPAN_Y)
            for z in range(SPAN_Z)
            for y in range(SPAN_Y)
        ],
    )


def partner_of(me, shift):
    return (me // SPAN_Y + shift[0]) % SPAN_Z * SPAN_Y + (me % SPAN_Y + shift[1]) % SPAN_Y


def team_exchange(value):
    return lax.all_to_all(
        value, "space", split_axis=0, concat_axis=0, tiled=True, axis_index_groups=TEAMS
    )


def group_shift(value, steps):
    count = lax.axis_size("group")
    leading, last = (max(0, -steps), min(count, count - steps))
    return lax.ppermute(value, "group", [(source, source + steps) for source in range(leading, last)])


def project_and_pack(points, geom, w_value, w_kern, lists, x_local, team, dests):
    blocks = points.shape[0] // BLK
    cross = x_local.shape[0]
    tiles = lists[0].shape[0]
    count = len(SHIFTS)
    slots = SPACES * CAP
    step = 8

    def kernel(
        local_ref, dest_ref, block_ref, cut_ref, cross_ref, team_ref, dests_ref,
        points_ref, geom_ref, wv_ref, wk_ref, used_ref, own_ref, up_ref, team_out_ref, *rest
    ):
        out_refs, (held, notes, filled, partner, cuts, sems) = rest[:count], rest[count:]
        i = pl.program_id(0)

        @pl.when(i == 0)
        def _():
            @pl.loop(0, slots, unroll=8)
            def _(s):
                used_ref[s] = -1
                partner[s] = 0
                cuts[s] = 0

            @pl.loop(0, SPACES, unroll=8)
            def _(s):
                filled[s] = 0

            @pl.loop(0, tiles, unroll=4)
            def _(t):
                dest = dest_ref[t]
                slot = dest * CAP + filled[dest]
                filled[dest] = filled[dest] + 1
                used_ref[slot] = local_ref[t]
                partner[slot] = block_ref[t]
                cuts[slot] = cut_ref[t]

            row = lax.broadcasted_iota(jnp.int32, (16, C), 0)

            @pl.loop(0, SPACES, unroll=4)
            def _(d):
                note = jnp.zeros((16, C), jnp.int32)
                for j in range(CAP):
                    cut = cuts[d * CAP + j]
                    note = jnp.where(row == j, partner[d * CAP + j], note)
                    note = jnp.where(row == CAP + j, cut // 16, note)
                    note = jnp.where(row == 2 * CAP + j, cut % 16, note)
                notes[d] = note.astype(jnp.float32).astype(jnp.bfloat16)

        @pl.loop(0, step, unroll=8)
        def _(b):
            upper = pl.ds(pl.multiple_of(b * BLK, BLK), HALF)
            lower = pl.ds(pl.multiple_of(b * BLK + HALF, HALF), HALF)
            whole = pl.ds(pl.multiple_of(b * BLK, BLK), BLK)
            held[i * step + b, :BLK, :] = jnp.dot(
                points_ref[whole, :], wv_ref[...], preferred_element_type=jnp.float32
            ).astype(jnp.bfloat16)
            wide = jnp.concatenate([geom_ref[upper, :], geom_ref[lower, :]], axis=1)
            held[i * step + b, BLK:, :] = jnp.dot(
                wide, wk_ref[...], preferred_element_type=jnp.float32
            ).astype(jnp.bfloat16)

        @pl.when(i == pl.num_programs(0) - 1)
        def _():
            copies = []

            def leave(dest, out):
                for j in range(CAP):
                    block = jnp.maximum(used_ref[dest * CAP + j], 0)
                    copies.append((held.at[block], out.at[pl.ds(j * ROWS, ROWS)]))
                copies.append((notes.at[dest], out.at[pl.ds(NOTES, 16)]))

            for m in range(MEMBERS):
                leave(team_ref[m], team_out_ref.at[m])
            for k in range(count):
                leave(dests_ref[k], out_refs[k])
            for t in range(cross):
                copies.append((held.at[cross_ref[t]], up_ref.at[t]))
            copies.append((held, own_ref))
            started = [pltpu.make_async_copy(source, target, sems) for source, target in copies]
            for copy in started:
                copy.start()
            for copy in started:
                copy.wait()

    zero = jnp.zeros_like(w_kern)
    twice = jnp.concatenate(
        [jnp.concatenate([w_kern, zero], 1), jnp.concatenate([zero, w_kern], 1)], 0
    )
    results = pl.pallas_call(
        kernel,
        grid_spec=pltpu.PrefetchScalarGridSpec(
            num_scalar_prefetch=7,
            grid=(blocks // step,),
            in_specs=[
                pl.BlockSpec((step * BLK, C), lambda i, *_: (i, 0)),
                pl.BlockSpec((step * BLK, C), lambda i, *_: (i, 0)),
                pl.BlockSpec((C, C), lambda i, *_: (0, 0)),
                pl.BlockSpec((2 * C, 2 * K), lambda i, *_: (0, 0)),
            ],
            out_specs=(SMEM,) + (ANYWHERE,) * (3 + count),
            scratch_shapes=[
                pltpu.VMEM((blocks, ROWS, C), jnp.bfloat16),
                pltpu.VMEM((SPACES, 16, C), jnp.bfloat16),
                pltpu.SMEM((SPACES,), jnp.int32),
                pltpu.SMEM((slots,), jnp.int32),
                pltpu.SMEM((slots,), jnp.int32),
                pltpu.SemaphoreType.DMA,
            ],
        ),
        out_shape=(
            jax.ShapeDtypeStruct((slots,), jnp.int32),
            jax.ShapeDtypeStruct((blocks, ROWS, C), jnp.bfloat16),
            jax.ShapeDtypeStruct((cross, ROWS, C), jnp.bfloat16),
            jax.ShapeDtypeStruct((MEMBERS, LOAD, C), jnp.bfloat16),
        )
        + (jax.ShapeDtypeStruct((LOAD, C), jnp.bfloat16),) * count,
        compiler_params=pltpu.CompilerParams(vmem_limit_bytes=VMEM_LIMIT),
        name="project_and_pack",
    )(*lists, x_local, team, dests, points, geom, w_value, twice)
    return results[:4], results[4:]


def read_notes(load):
    note = load[pl.ds(NOTES, 16), :].astype(jnp.float32)
    entry = note[:CAP] * 512 + note[CAP : 2 * CAP] * 16 + note[2 * CAP : 3 * CAP]
    entries = [entry[j, 0].astype(jnp.int32) for j in range(CAP)]
    return [(value // 512, value % 512) for value in entries]


def unpack_kernels(packed):
    return jnp.concatenate([packed[:, :K], packed[:, K:]], axis=0)


def pair_terms(pairs):
    rows = lax.broadcasted_iota(jnp.int32, (BLK, BLK), 0)
    columns = lax.broadcasted_iota(jnp.int32, (BLK, BLK), 1)
    level = rows + columns
    scores = [
        lax.dot_general(
            unpack_kernels(a[BLK:, :]),
            unpack_kernels(b[BLK:, :]),
            (((1,), (1,)), ((), ())),
            preferred_element_type=jnp.float32,
        )
        for a, b, _ in pairs
    ]
    tiles = [
        jnp.where(level < cut, jnp.tanh(score * (1.0 / math.sqrt(K))), 0.0).astype(jnp.bfloat16)
        for score, (_, _, cut) in zip(scores, pairs)
    ]
    forward = [
        jnp.dot(tile, b[:BLK, :], preferred_element_type=jnp.float32) for tile, (_, b, _) in zip(tiles, pairs)
    ]
    backward = [
        lax.dot_general(tile, a[:BLK, :], (((0,), (0,)), ((), ())), preferred_element_type=jnp.float32)
        for tile, (a, _, _) in zip(tiles, pairs)
    ]
    return forward, backward


def pair_cost(number, blocks):
    return pl.CostEstimate(
        flops=2 * number * BLK * BLK * (K + 2 * C),
        bytes_accessed=number * (ROWS + BLK) * C * 2 + blocks * BLK * C * 8,
        transcendentals=number * BLK * BLK,
    )


def pairs_above(cross_meta, below, own):
    cross = below.shape[0]
    blocks = own.shape[0]
    some = math.gcd(cross, 4)

    def kernel(cross_ref, below_ref, own_ref, back_ref, total):
        total[...] = jnp.zeros_like(total)

        @pl.loop(0, cross, step=some)
        def _(first):
            mine = [cross_ref[2 * (first + t)] for t in range(some)]
            forward, backward = pair_terms(
                [
                    (below_ref.at[first + t], own_ref.at[mine[t]], cross_ref[2 * (first + t) + 1])
                    for t in range(some)
                ]
            )
            for t in range(some):
                back_ref[first + t] = forward[t].astype(jnp.bfloat16)
            for t in range(some):
                total[mine[t]] = total[mine[t]] + backward[t]

    return pl.pallas_call(
        kernel,
        in_specs=[SMEM, VMEM, VMEM],
        out_specs=(VMEM, VMEM),
        out_shape=(
            jax.ShapeDtypeStruct((cross, BLK, C), jnp.bfloat16),
            jax.ShapeDtypeStruct((blocks, BLK, C), jnp.float32),
        ),
        compiler_params=pltpu.CompilerParams(vmem_limit_bytes=VMEM_LIMIT),
        cost_estimate=pl.CostEstimate(flops=LONG, bytes_accessed=0, transcendentals=0),
        name="pairs_above",
    )(cross_meta, below, own)


def team_pairs(arrived, own, aggregate, passing):
    blocks = own.shape[0]
    some = CREW * CAP
    handed = len(passing)

    def kernel(arrived_ref, own_ref, given_ref, *rest):
        back_ref, total_ref, total, sem = rest[handed], rest[handed + 1], rest[-2], rest[-1]
        i = pl.program_id(0)

        @pl.when(i == 0)
        def _():
            copy = pltpu.make_async_copy(given_ref, total, sem)
            copy.start()
            copy.wait()

        @pl.loop(0, CREW, step=STAGE // CAP)
        def _(first):
            places = []
            for m in range(STAGE // CAP):
                load = arrived_ref.at[first + m]
                for j, (block, cut) in enumerate(read_notes(load)):
                    places.append((load.at[pl.ds(j * ROWS, ROWS)], block, cut))
            forward, backward = pair_terms([(a, own_ref.at[block], cut) for a, block, cut in places])
            for n in range(STAGE):
                back_ref[first * CAP + n] = forward[n].astype(jnp.bfloat16)
            for n, (_, block, _) in enumerate(places):
                total[block] = total[block] + backward[n]

        @pl.when(i == pl.num_programs(0) - 1)
        def _():
            copy = pltpu.make_async_copy(total, total_ref, sem)
            copy.start()
            copy.wait()

    results = pl.pallas_call(
        kernel,
        grid=(MEMBERS // CREW,),
        in_specs=[
            pl.BlockSpec((CREW, LOAD, C), lambda i: (i, 0, 0)),
            pl.BlockSpec((blocks, ROWS, C), lambda i: (0, 0, 0)),
            ANYWHERE,
        ]
        + [ANYWHERE] * handed,
        out_specs=(pl.BlockSpec((some, BLK, C), lambda i: (i, 0, 0)), ANYWHERE) + (ANYWHERE,) * handed,
        scratch_shapes=[
            pltpu.VMEM((blocks, BLK, C), jnp.float32),
            pltpu.SemaphoreType.DMA,
        ],
        out_shape=(
            jax.ShapeDtypeStruct((MEMBERS * CAP, BLK, C), jnp.bfloat16),
            jax.ShapeDtypeStruct((blocks, BLK, C), jnp.float32),
        )
        + tuple(jax.ShapeDtypeStruct(array.shape, array.dtype) for array in passing),
        input_output_aliases={3 + n: 2 + n for n in range(handed)},
        compiler_params=pltpu.CompilerParams(vmem_limit_bytes=VMEM_LIMIT),
        cost_estimate=pair_cost(MEMBERS * CAP, blocks),
        name="team_pairs",
    )(arrived, own, aggregate, *passing)
    return results[0], results[1], results[2:]


def shifted_pairs(arrived, own, aggregate, passing, cost):
    count = len(arrived)
    blocks = own.shape[0]
    handed = len(passing)

    def kernel(own_ref, given_ref, *rest):
        arrived_refs, rest = rest[handed : handed + count], rest[handed + count :]
        back_refs, total, loads, backs = rest[:count], rest[count], rest[-2], rest[-1]
        total[...] = given_ref[...]
        for k in range(count):
            loads[k] = arrived_refs[k][...]

        @pl.loop(0, count, step=STAGE // CAP)
        def _(first):
            places = []
            for k in range(STAGE // CAP):
                load = loads.at[first + k]
                for j, (block, cut) in enumerate(read_notes(load)):
                    places.append((load.at[pl.ds(j * ROWS, ROWS)], block, cut))
            forward, backward = pair_terms([(a, own_ref.at[block], cut) for a, block, cut in places])
            for n in range(STAGE):
                backs[first + n // CAP, n % CAP] = forward[n].astype(jnp.bfloat16)
            for n, (_, block, _) in enumerate(places):
                total[block] = total[block] + backward[n]

        for k in range(count):
            back_refs[k][...] = backs[k]

    results = pl.pallas_call(
        kernel,
        in_specs=[VMEM] * 2 + [ANYWHERE] * handed + [VMEM] * count,
        out_specs=(VMEM,) * (count + 1) + (ANYWHERE,) * handed,
        out_shape=(jax.ShapeDtypeStruct((CAP, BLK, C), jnp.bfloat16),) * count
        + (jax.ShapeDtypeStruct((blocks, BLK, C), jnp.float32),)
        + tuple(jax.ShapeDtypeStruct(array.shape, array.dtype) for array in passing),
        input_output_aliases={1: count} | {2 + n: count + 1 + n for n in range(handed)},
        scratch_shapes=[
            pltpu.VMEM((count, LOAD, C), jnp.bfloat16),
            pltpu.VMEM((count, CAP, BLK, C), jnp.bfloat16),
        ],
        compiler_params=pltpu.CompilerParams(vmem_limit_bytes=VMEM_LIMIT),
        cost_estimate=cost,
        name="shifted_pairs",
    )(own, aggregate, *passing, *arrived)
    return results[:count], results[count], results[count + 1 :]


def add_back(used_ref, places_ref, back_refs, total):
    for k, back_ref in enumerate(back_refs):
        for j in range(CAP):
            mine = used_ref[places_ref[k] * CAP + j]

            @pl.when(mine >= 0)
            def _():
                total[mine] = total[mine] + back_ref[j].astype(jnp.float32)


def gather_team(used, team, x_local, returned, returned_x, aggregate, passing):
    cross = returned_x.shape[0]
    handed = len(passing)

    def kernel(used_ref, team_ref, cross_ref, given_ref, back_ref, back_x_ref, *rest):
        total = rest[handed]
        total[...] = given_ref[...]
        for t in range(cross):
            mine = cross_ref[t]
            total[mine] = total[mine] + back_x_ref[t].astype(jnp.float32)

        @pl.loop(0, MEMBERS)
        def _(m):
            for j in range(CAP):
                mine = used_ref[team_ref[m] * CAP + j]

                @pl.when(mine >= 0)
                def _():
                    total[mine] = total[mine] + back_ref[m * CAP + j].astype(jnp.float32)

    results = pl.pallas_call(
        kernel,
        in_specs=[SMEM] * 3 + [VMEM] * 3 + [ANYWHERE] * handed,
        out_specs=(VMEM,) + (ANYWHERE,) * handed,
        out_shape=(jax.ShapeDtypeStruct(aggregate.shape, jnp.float32),)
        + tuple(jax.ShapeDtypeStruct(array.shape, array.dtype) for array in passing),
        input_output_aliases={3: 0} | {6 + n: 1 + n for n in range(handed)},
        compiler_params=pltpu.CompilerParams(vmem_limit_bytes=VMEM_LIMIT),
        cost_estimate=pl.CostEstimate(
            flops=returned.size, bytes_accessed=returned.size * 2 + aggregate.size * 8, transcendentals=0
        ),
        name="gather_team",
    )(used, team, x_local, aggregate, returned, returned_x, *passing)
    return results[0], results[1:]


def gather_and_mix(used, dests, returned, aggregate, points, w_out, gain):
    count = len(returned)
    blocks = aggregate.shape[0]
    some = 8

    def kernel(used_ref, dests_ref, total_ref, points_ref, w_ref, gain_ref, *rest):
        back_refs, out_ref, total, sem = rest[:count], rest[count], rest[count + 1], rest[count + 2]
        i = pl.program_id(0)

        @pl.when(i == 0)
        def _():
            copy = pltpu.make_async_copy(total_ref, total, sem)
            copy.start()
            copy.wait()
            add_back(used_ref, dests_ref, back_refs, total)

        @pl.loop(0, some, unroll=8)
        def _(b):
            rows = pl.ds(pl.multiple_of(b * BLK, BLK), BLK)
            flat = total[i * some + b]
            meansq = jnp.mean(flat * flat, -1, keepdims=True)
            normed = flat * lax.rsqrt(meansq + 1e-06) * gain_ref[...]
            hidden = jax.nn.gelu(normed).astype(jnp.bfloat16)
            mixed = points_ref[rows, :].astype(jnp.float32) + jnp.dot(
                hidden, w_ref[...], preferred_element_type=jnp.float32
            )
            out_ref[rows, :] = mixed.astype(jnp.bfloat16)

    return pl.pallas_call(
        kernel,
        grid_spec=pltpu.PrefetchScalarGridSpec(
            num_scalar_prefetch=2,
            grid=(blocks // some,),
            in_specs=[
                pl.BlockSpec(memory_space=pl.ANY),
                pl.BlockSpec((some * BLK, C), lambda i, *_: (i, 0)),
                pl.BlockSpec((C, C), lambda i, *_: (0, 0)),
                pl.BlockSpec((1, C), lambda i, *_: (0, 0)),
            ]
            + [pl.BlockSpec((CAP, BLK, C), lambda i, *_: (0, 0, 0))] * count,
            out_specs=pl.BlockSpec((some * BLK, C), lambda i, *_: (i, 0)),
            scratch_shapes=[
                pltpu.VMEM((blocks, BLK, C), jnp.float32),
                pltpu.SemaphoreType.DMA,
            ],
        ),
        out_shape=jax.ShapeDtypeStruct((blocks * BLK, C), jnp.bfloat16),
        compiler_params=pltpu.CompilerParams(vmem_limit_bytes=VMEM_LIMIT),
        name="gather_and_mix",
    )(used, dests, aggregate, points, w_out, gain[None], *returned)


def body(feats, geom, w_value, w_kern, w_out, gain, t_local, t_dest, t_block, t_cut, x_local, x_block, x_cut):
    points = feats[0]
    me = lax.axis_index("space")
    dests = jnp.stack([partner_of(me, shift) for shift in SHIFTS]).astype(jnp.int32)
    member = jnp.arange(MEMBERS, dtype=jnp.int32)
    team = (member // SPAN_Y * 2 + me // SPAN_Y % 2) * SPAN_Y + member % SPAN_Y
    lists = (t_local[0], t_dest[0, :, 0], t_block[0], t_cut[0])
    (used, own, rising, leaving), shifting = project_and_pack(
        points, geom[0], w_value, w_kern, lists, x_local[0], team, dests
    )
    arrived = team_exchange(leaving)
    cross_meta = group_shift(jnp.stack([x_block[0], x_cut[0]], 1), 1).reshape(-1)
    below = group_shift(rising, 1)
    shifting = list(shifting)
    shifted = [None] * len(SHIFTS)

    def send(first, end):
        for k in range(first, end):
            shifted[k] = space_shift(shifting[k], SHIFTS[k])

    back_x, aggregate = pairs_above(cross_meta, below, own)
    returned_x = group_shift(back_x, -1)
    send(0, GATES[0])
    first, end = GATES
    back, aggregate, shifting[first:end] = team_pairs(arrived, own, aggregate, shifting[first:end])
    send(first, end)
    going_back = []
    for turn, (first, end) in enumerate(BATCHES):
        later = slice(GATES[1], len(SHIFTS)) if turn == GATE else slice(0, 0)
        passing = shifting[later] + ([back] if turn == PASSED else [])
        back_some, aggregate, passing = shifted_pairs(
            shifted[first:end], own, aggregate, passing,
            pl.CostEstimate(flops=LONG, bytes_accessed=0, transcendentals=0)
            if turn > PASSED
            else pair_cost((end - first) * CAP, own.shape[0]),
        )
        shifting[later] = passing[: later.stop - later.start]
        if turn == GATE:
            send(GATES[1], len(SHIFTS))
        if turn == PASSED:
            returned = team_exchange(passing[-1])
        going_back += back_some
    back_shifted = [None] * len(SHIFTS)

    def send_back(first, end):
        for k in range(first, end):
            dz, dy = SHIFTS[k]
            back_shifted[k] = space_shift(going_back[k], (-dz, -dy))

    send_back(0, LATE)
    aggregate, going_back[LATE:] = gather_team(
        used, team, x_local[0], returned, returned_x, aggregate, going_back[LATE:]
    )
    send_back(LATE, len(SHIFTS))
    mixed = gather_and_mix(used, dests, back_shifted, aggregate, points, w_out, gain)
    return mixed[None]


def solution(mesh):
    in_specs = (
        P("group", "space", None),
        P("group", "space", None),
        P(),
        P(),
        P(),
        P(),
        P("group", "space"),
        P("group", "space", None),
        P("group", "space"),
        P("group", "space"),
        P("group", "space"),
        P("group", "space"),
        P("group", "space"),
    )
    out_specs = P("group", "space", None)
    return jax.shard_map(body, mesh=mesh, in_specs=in_specs, out_specs=out_specs, check_vma=False)
```
